256 devices in a mesh: depth: 32 (over z, x_lo, core), height: 4 (over y), batch: 2 (over x_hi).
Axes of the slice: x: 4 (x_hi: 2, x_lo: 2; x = x_hi * 2 + x_lo), y: 4, z: 8, core: 2. Of those that a mesh axis runs over, the one named last changes fastest.
Arguments:
- volumes: bfloat16 [8, 4, 128, 32, 128], P('batch', None, 'depth', 'height'), may hold values from -6 to 6
- first_kernel: bfloat16 [3, 3, 3, 4, 32], replicated, may hold values from -0.625 to 0.625
- first_bias: float32 [32], replicated, may hold values from -3 to 3
- second_kernel: bfloat16 [3, 3, 3, 32, 64], replicated, may hold values from -0.21875 to 0.21875
- second_bias: float32 [64], replicated, may hold values from -3 to 3
- deep_grad: bfloat16 [8, 64, 32, 8, 32], P(('batch', 'height'), None, 'depth'), may hold values from -0.15917969 to 0.15917969
Outputs:
- deep_maps: bfloat16 [8, 64, 32, 8, 32], P(('batch', 'height'), None, 'depth')
- first_kernel_grad: float32 [3, 3, 3, 4, 32], replicated
- first_bias_grad: float32 [32], replicated
- second_kernel_grad: float32 [3, 3, 3, 32, 64], replicated
- second_bias_grad: float32 [64], replicated
The draws below stay inside these ranges and needn't reach their ends.
All inputs are finite; a program needn't handle non-finite values.
Results may differ from the reference program's by a relative error of at most 0.0051.
Values may be sent and summed in bfloat16 or wider, within the bound.
No kernel may reach another device: no remote copies, remote signals or barrier semaphores. Data moves between devices by JAX's collectives and lax.ppermute only.
A program may use at most 128 MiB of HBM per device.

```python
import jax
import jax.numpy as jnp
from jax import lax

CH_IN = 4
CH_ONE = 32
CH_TWO = 64
WIDTH = 128
SAMPLES = 8
DEPTH = 128
HEIGHT = 32


def block_levels(stream_key, shape, split, low, top_value):
    loudness, own = 1.0, jax.random.fold_in(stream_key, 6)
    for dim, blocks in split:
        draws = jnp.exp(jax.random.uniform(jax.random.fold_in(own, dim), (blocks,), jnp.float32, low / len(split), top_value / len(split)))
        loudness = loudness * jnp.repeat(draws, shape[dim] // blocks).reshape([-1 if axis == dim else 1 for axis in range(len(shape))])
    return loudness


def centred(rng, dims, scale, most, split=(), held_as=jnp.bfloat16):
    entries = scale * jax.random.normal(rng, dims, jnp.float32)
    if split:
        entries = entries * block_levels(rng, dims, split, -0.22, 0.18)
    return jnp.clip(entries, -most, most).astype(held_as)


def setup_inputs(seed: int = 0) -> dict:
    key_list = jax.random.split(jax.random.key(seed), 7)
    volumes = centred(key_list[0], (SAMPLES, CH_IN, DEPTH, HEIGHT, WIDTH), 1.0, 6.0, ((0, 2), (2, 32), (3, 4)))
    first_kernel = centred(key_list[1], (3, 3, 3, CH_IN, CH_ONE), (27 * CH_IN) ** -0.5, 0.625)
    first_bias = centred(key_list[2], (CH_ONE,), 0.5, 3.0, (), jnp.float32)
    second_kernel = centred(key_list[3], (3, 3, 3, CH_ONE, CH_TWO), (27 * CH_ONE) ** -0.5, 0.21875)
    second_bias = centred(key_list[4], (CH_TWO,), 0.5, 3.0, (), jnp.float32)
    deep_grad = centred(key_list[5], (SAMPLES, CH_TWO, DEPTH // 4, HEIGHT // 4, WIDTH // 4), 0.02, 0.15917969, ((0, 8), (2, 32)))
    return dict(volumes=volumes, first_kernel=first_kernel, first_bias=first_bias, second_kernel=second_kernel, second_bias=second_bias, deep_grad=deep_grad)


def framed(field):
    return jnp.pad(field, ((0, 0), (1, 1), (1, 1), (1, 1)))

def shifted_conv(padded, kernel):
    depth_len = padded.shape[1] - 2
    height_len = padded.shape[2] - 2
    width_len = padded.shape[3] - 2
    total = jnp.zeros((kernel.shape[4], depth_len, height_len, width_len), jnp.float32)
    for depth_at in range(3):
        for height_at in range(3):
            for width_at in range(3):
                window = padded[:, depth_at:depth_at + depth_len, height_at:height_at + height_len, width_at:width_at + width_len]
                total = total + jnp.einsum('cdhw,co->odhw', window, kernel[depth_at, height_at, width_at], precision=lax.Precision.HIGHEST)
    return total

def kernel_grad(padded, cotangent):
    depth_len, height_len, width_len = (cotangent.shape[1], cotangent.shape[2], cotangent.shape[3])
    rows = []
    for depth_at in range(3):
        for height_at in range(3):
            for width_at in range(3):
                window = padded[:, depth_at:depth_at + depth_len, height_at:height_at + height_len, width_at:width_at + width_len]
                rows.append(jnp.einsum('cdhw,odhw->co', window, cotangent, precision=lax.Precision.HIGHEST))
    stacked = jnp.stack(rows, axis=0)
    return stacked.reshape((3, 3, 3) + stacked.shape[1:])

def pooled(field):
    chans, depth_len, height_len, width_len = field.shape
    blocks = field.reshape(chans, depth_len // 2, 2, height_len // 2, 2, width_len // 2, 2)
    return lax.optimization_barrier(jnp.mean(blocks, axis=(2, 4, 6)))

def widened(field):
    chans, depth_len, height_len, width_len = field.shape
    spread = jnp.broadcast_to(field[:, :, None, :, None, :, None], (chans, depth_len, 2, height_len, 2, width_len, 2))
    return spread.reshape(chans, depth_len * 2, height_len * 2, width_len * 2)

def slope(values):
    sigma = jax.nn.sigmoid(values)
    return sigma * (1.0 + values * (1.0 - sigma))

def reference(volumes, first_kernel, first_bias, second_kernel, second_bias, deep_grad):
    kernel_one = first_kernel.astype(jnp.float32)
    kernel_two = second_kernel.astype(jnp.float32)
    back_kernel = jnp.swapaxes(kernel_two[::-1, ::-1, ::-1], 3, 4)

    def one_sample(pair):
        sample, cotangent = pair
        framed_in = framed(sample.astype(jnp.float32))
        pre_first = shifted_conv(framed_in, kernel_one) + first_bias[:, None, None, None]
        pooled_first = pooled(jax.nn.silu(pre_first)).astype(jnp.bfloat16)
        framed_pool = framed(pooled_first.astype(jnp.float32))
        pre_second = shifted_conv(framed_pool, kernel_two) + second_bias[:, None, None, None]
        deep = pooled(jax.nn.silu(pre_second)).astype(jnp.bfloat16)
        grad_second = (widened(cotangent.astype(jnp.float32)) * 0.125 * slope(pre_second)).astype(jnp.bfloat16)
        grad_wide = grad_second.astype(jnp.float32)
        second_kgrad = kernel_grad(framed_pool, grad_wide)
        second_bgrad = lax.optimization_barrier(jnp.sum(grad_wide, axis=(1, 2, 3)))
        back_pool = shifted_conv(framed(grad_wide), back_kernel)
        grad_first = (widened(back_pool) * 0.125 * slope(pre_first)).astype(jnp.bfloat16)
        first_wide = grad_first.astype(jnp.float32)
        first_kgrad = kernel_grad(framed_in, first_wide)
        first_bgrad = lax.optimization_barrier(jnp.sum(first_wide, axis=(1, 2, 3)))
        return (deep, first_kgrad, first_bgrad, second_kgrad, second_bgrad)
    results = lax.map(one_sample, (volumes, deep_grad))
    return (results[0], lax.optimization_barrier(jnp.sum(results[1], axis=0)), lax.optimization_barrier(jnp.sum(results[2], axis=0)), lax.optimization_barrier(jnp.sum(results[3], axis=0)), lax.optimization_barrier(jnp.sum(results[4], axis=0)))
```

```python
import jax
import jax.numpy as jnp
import numpy as np
from jax import lax
from jax.experimental import pallas as pl
from jax.experimental.pallas import tpu as pltpu
from jax.sharding import PartitionSpec as P

F32 = jnp.float32
BF16 = jnp.bfloat16
AXES = ("depth", "height", "batch")
ROWS = 512
NT = (((1,), (1,)), ((), ()))


def window_index(a4, b4, k4, ch):
    half, low = divmod(a4, 2)
    hb, hs = ((1, 1), (0, 0), (1, 0), (0, 1))[b4]
    wb, ws = ((1, 1), (0, 0), (1, 0), (0, 1))[k4]
    return half * 128 + (hs * 2 + ws) * 32 + hb * 16 + wb * 8 + low * 4 + ch


def select_taps():
    sel = np.zeros((128, 2048), np.float32)
    for pos in range(8):
        dz, dy, dx = pos // 4, pos // 2 % 2, pos % 2
        for a in range(3):
            for b in range(3):
                for c in range(3):
                    for ch in range(4):
                        tap = ((a * 3 + b) * 3 + c) * 4 + ch
                        sel[tap, pos * 256 + window_index(a + dz, b + dy, c + dx, ch)] = 1.0
    return sel


def split_width():
    out = np.zeros((256, 256), np.float32)
    for row in range(2):
        for cell in range(128):
            out[row * 128 + cell, (cell % 2) * 128 + row * 64 + cell // 2] = 1.0
    return out


def pool_lanes():
    out = np.zeros((512, 128), np.float32)
    for lane in range(512):
        out[lane, lane // 128 * 32 + lane % 64 // 2] = 0.125
    return out


def dot(a, b):
    return jnp.dot(a, b, preferred_element_type=F32)


def dot_nt(a, b):
    return lax.dot_general(a, b, NT, preferred_element_type=F32)


def prep_kernel(k1_ref, k2_ref, sel_ref, w1_ref, w2_ref, wb_ref):
    flat = lax.dot_general(k1_ref[...], sel_ref[...], (((0,), (0,)), ((), ())), preferred_element_type=F32)
    for pos in range(8):
        w1_ref[pos * 32 : pos * 32 + 32, :] = (0.5 * flat[:, pos * 256 : pos * 256 + 256]).astype(BF16)
    rows = lax.broadcasted_iota(jnp.int32, (64, 64), 0)
    cols = lax.broadcasted_iota(jnp.int32, (64, 64), 1)
    half_eye = jnp.where(rows == cols, 0.5, 0.0).astype(BF16)
    for a in range(3):
        w2_ref[a] = dot_nt(half_eye, k2_ref[a * 288 : a * 288 + 288, :]).astype(BF16)
        blocks = []
        for b in range(3):
            for c in range(3):
                at = ((a * 3 + 2 - b) * 3 + 2 - c) * 32
                blocks.append(k2_ref[at : at + 32, :].astype(F32))
        wb_ref[a * 32 : a * 32 + 32, :] = jnp.concatenate(blocks, axis=1).astype(BF16)


def lane_masks(rows):
    lane = lax.broadcasted_iota(jnp.int32, (rows, 128), 1)
    cell = lane % 64
    return lane < 64, cell != 0, cell != 63


def width_shift(tiles, step, masks):
    _, not_first, not_last = masks
    if step < 0:
        return [jnp.where(not_first, pltpu.roll(t, 1, 1), 0.0) for t in tiles]
    return [jnp.where(not_last, pltpu.roll(t, 127, 1), 0.0) for t in tiles]


def height_shift(tiles, steps, masks):
    low = masks[0]
    swapped = [pltpu.roll(t, 64, 1) for t in tiles]
    zero = jnp.zeros_like(tiles[0])
    out = []
    for step in steps:
        if step < 0:
            before = [zero] + swapped[:-1]
            out.append([jnp.where(low, before[i], swapped[i]) for i in range(len(tiles))])
        else:
            after = swapped[1:] + [zero]
            out.append([jnp.where(low, swapped[i], after[i]) for i in range(len(tiles))])
    return out


def store_shifts(tiles, put, masks):
    for c in range(3):
        moved = tiles if c == 1 else width_shift(tiles, c - 1, masks)
        before, after = height_shift(moved, (-1, 1), masks)
        for b, group in enumerate((before, moved, after)):
            for t in range(8):
                put(b * 3 + c, t, group[t])


def main_kernel(
    own_ref, chip_ref, link_ref, dg_ref, w1_ref, w2_ref, wb_ref, b1_ref, b2_ref, sel_ref, split_ref, pool_ref,
    deep_ref, packed_ref,
    f_ref, l_ref, g_ref, x_ref, slope_ref, y_ref, z_ref, g2_ref, gz_ref, back_ref, ds_ref, g1_ref, kg_ref,
):
    place = lax.axis_index("depth")
    parity = place % 2
    keep_low = jnp.where(place > 0, 1.0, 0.0).astype(F32)
    keep_high = jnp.where(place < lax.axis_size("depth") - 1, 1.0, 0.0).astype(F32)

    def fill(ref, plane, at):
        for y in range(4):
            for ch in range(4):
                f_ref[pl.ds((at * 4 + ch) * 32 + y * 8, 8), :] = ref[y, ch, plane].astype(F32)

    for plane in range(4):
        fill(own_ref, plane, 3 + plane)

    @pl.when(parity == 0)
    def _():
        for plane in range(3):
            fill(link_ref, plane + 1, plane)
            fill(chip_ref, plane, 7 + plane)

    @pl.when(parity == 1)
    def _():
        for plane in range(3):
            fill(chip_ref, plane + 1, plane)
            fill(link_ref, plane, 7 + plane)

    for hb in range(2):
        for qq in range(8):
            for low in range(2):
                l_ref[pl.ds((hb * 8 + qq) * 40, 40), low * 128 : low * 128 + 128] = f_ref[
                    pl.ds(4 * qq + 2 * low + hb, 40, stride=32), :
                ]
    g_ref[...] = dot(l_ref[...].astype(BF16), split_ref[...])

    masks8 = lane_masks(8)
    for pair in range(5):
        for hb in range(2):
            still, moved = [], []
            for wb in range(2):
                tiles = [
                    g_ref[(hb * 8 + qq) * 40 + pair * 8 : (hb * 8 + qq) * 40 + pair * 8 + 8, wb * 128 : wb * 128 + 128]
                    for qq in range(8)
                ]
                still.append(tiles)
                moved.append(width_shift(tiles, 1 if wb == 0 else -1, masks8))
            for ws, group in enumerate((still, moved)):
                step = 1 if hb == 0 else -1
                raised = [height_shift(group[wb], (step,), masks8)[0] for wb in range(2)]
                for hs, part in enumerate((group, raised)):
                    at = pair * 128 + (hs * 2 + ws) * 32 + hb * 16
                    for qq in range(8):
                        both = jnp.concatenate([part[0][qq], part[1][qq]], axis=0)
                        x_ref[at : at + 16, qq * 128 : qq * 128 + 128] = both.astype(BF16)

    bias1 = jnp.broadcast_to(0.5 * b1_ref[...], (32, 256))
    for plane in range(4):
        for t in range(4):
            lanes = slice(t * 256, t * 256 + 256)
            pre = dot(w1_ref[...], x_ref[plane * 128 : plane * 128 + 256, lanes])
            total = jnp.zeros((32, 256), F32)
            for pos in range(8):
                u = pre[pos * 32 : pos * 32 + 32] + bias1
                tanh = jnp.tanh(u)
                w = 1.0 + tanh
                silu = u * w
                slope_ref[plane, pos * 32 : pos * 32 + 32, lanes] = w + silu * (1.0 - tanh)
                total = total + silu
            scale = 0.125
            if plane == 0:
                scale = 0.125 * keep_low
            if plane == 3:
                scale = 0.125 * keep_high
            y_ref[plane, :, lanes] = total * scale

    masks32 = lane_masks(32)
    for plane in range(4):

        def put(at, t, value, plane=plane):
            z_ref[plane, at * 32 : at * 32 + 32, t * 128 : t * 128 + 128] = value.astype(BF16)

        store_shifts([y_ref[plane, :, t * 128 : t * 128 + 128] for t in range(8)], put, masks32)

    bias2 = jnp.broadcast_to(0.5 * b2_ref[...], (64, 256))
    sum2 = jnp.zeros((64, 128), F32)
    for plane in range(2):
        for t in range(4):
            lanes = slice(t * 256, t * 256 + 256)
            if plane == 0 and t % 2 == 0:
                wide = dot_nt(dg_ref[:, t * 64 : t * 64 + 128], pool_ref[...])
                g2_ref[0, :, t * 256 : t * 256 + 512] = wide
                g2_ref[1, :, t * 256 : t * 256 + 512] = wide
            u = bias2
            for a in range(3):
                u = u + dot(w2_ref[a], z_ref[plane + a, :, lanes])
            tanh = jnp.tanh(u)
            w = 1.0 + tanh
            silu = u * w
            if plane == 0:
                ds_ref[:, lanes] = silu
            else:
                ds_ref[:, lanes] = ds_ref[:, lanes] + silu
            grad = (0.5 * g2_ref[plane, :, lanes]) * (w + silu * (1.0 - tanh))
            g2_ref[plane, :, lanes] = grad
            sum2 = sum2 + grad[:, :128] + grad[:, 128:]

    for half in range(2):
        part = ds_ref[:, half * 512 : half * 512 + 512]
        high = part.astype(BF16)
        low = (part - high.astype(F32)).astype(BF16)
        deep = dot(high, pool_ref[...]) + dot(low, pool_ref[...])
        deep_ref[:, half * 128 : half * 128 + 128] = deep.astype(BF16)

    masks64 = lane_masks(64)
    for plane in range(2):

        def put(at, t, value, plane=plane):
            gz_ref[plane, at * 64 : at * 64 + 64, t * 128 : t * 128 + 128] = value.astype(BF16)

        store_shifts([g2_ref[plane, :, t * 128 : t * 128 + 128] for t in range(8)], put, masks64)

    for a in range(3):
        total = dot_nt(z_ref[a], gz_ref[0, 256:320, :]) + dot_nt(z_ref[a + 1], gz_ref[1, 256:320, :])
        kg_ref[a * 288 : a * 288 + 288, :] = total

    for t in range(4):
        lanes = slice(t * 256, t * 256 + 256)
        one = dot(wb_ref[...], gz_ref[0, :, lanes])
        two = dot(wb_ref[...], gz_ref[1, :, lanes])
        back_ref[0, :, lanes] = one[0:32] * (0.0625 * keep_low)
        back_ref[1, :, lanes] = (one[32:64] + two[0:32]) * 0.0625
        back_ref[2, :, lanes] = (one[64:96] + two[32:64]) * 0.0625
        back_ref[3, :, lanes] = two[64:96] * (0.0625 * keep_high)

    sum1 = jnp.zeros((32, 128), F32)
    grads = jnp.zeros((256, 256), F32)
    for plane in range(4):
        for t in range(4):
            lanes = slice(t * 256, t * 256 + 256)
            back = back_ref[plane, :, lanes]
            for pos in range(8):
                grad = back * slope_ref[plane, pos * 32 : pos * 32 + 32, lanes]
                g1_ref[pos * 32 : pos * 32 + 32, lanes] = grad.astype(BF16)
                sum1 = sum1 + grad[:, :128] + grad[:, 128:]
        grads = grads + dot_nt(g1_ref[...], x_ref[plane * 128 : plane * 128 + 256, :])

    first = jnp.zeros((128, 32), F32)
    for pos in range(8):
        part = grads[pos * 32 : pos * 32 + 32]
        high = part.astype(BF16)
        low = (part - high.astype(F32)).astype(BF16)
        sel = sel_ref[:, pos * 256 : pos * 256 + 256]
        first = first + dot_nt(sel, high) + dot_nt(sel, low)

    ones = jnp.ones((8, 128), F32)
    bias_rows = [
        lax.dot_general(ones, s, NT, precision=lax.Precision.HIGHEST, preferred_element_type=F32) for s in (sum1, sum2)
    ]
    packed_ref[0:432, :] = jnp.concatenate([kg_ref[0:432, :], kg_ref[432:864, :]], axis=1)
    packed_ref[432:464, :] = jnp.concatenate([first[32 * i : 32 * i + 32] for i in range(4)], axis=1)
    packed_ref[464:472, :] = jnp.concatenate(bias_rows + [jnp.zeros((8, 32), F32)], axis=1)
    packed_ref[472:512, :] = jnp.zeros((40, 128), F32)


def sum_kernel(in_ref, out_ref):
    total = in_ref[0:8, :]
    for i in range(1, ROWS // 8):
        total = total + in_ref[8 * i : 8 * i + 8, :]
    total = total + pltpu.roll(total, 4, 0)
    total = total + pltpu.roll(total, 2, 0)
    for i in range(ROWS // 8):
        out_ref[8 * i : 8 * i + 8, :] = total


def unpack_kernel(in_ref, second_ref, first_ref, bias1_ref, bias2_ref):
    second_ref[0:432, :] = in_ref[0:432, 0:64]
    second_ref[432:864, :] = in_ref[0:432, 64:128]
    for g in range(4):
        for m in range(8):
            if 8 * g + m < 27:
                first_ref[8 * g + m] = in_ref[432 + 4 * m : 436 + 4 * m, 32 * g : 32 * g + 32]
    bias1_ref[...] = in_ref[464:465, 0:32]
    bias2_ref[...] = in_ref[464:465, 32:96]


def vmem(count):
    return [pl.BlockSpec(memory_space=pltpu.VMEM) for _ in range(count)]


def call(kernel, outs, inputs, scratch=(), limit=None):
    params = pltpu.CompilerParams(vmem_limit_bytes=limit) if limit else None
    return pl.pallas_call(
        kernel,
        out_shape=outs,
        in_specs=vmem(len(inputs)),
        out_specs=vmem(len(outs)),
        scratch_shapes=[pltpu.VMEM(shape, dtype) for shape, dtype in scratch],
        compiler_params=params,
    )(*inputs)


def shape(dims, dtype):
    return jax.ShapeDtypeStruct(dims, dtype)


def per_device(volumes, first_kernel, first_bias, second_kernel, second_bias, deep_grad):
    count = lax.axis_size("depth")
    own = lax.all_to_all(volumes, "height", split_axis=0, concat_axis=0, tiled=True)
    chip = lax.ppermute(own, "depth", [(i, i ^ 1) for i in range(count)])
    pairs = [(i, i + 1) for i in range(1, count - 1, 2)]
    link = lax.ppermute(own, "depth", pairs + [(j, i) for i, j in pairs])

    sel = jnp.asarray(select_taps(), BF16)
    k1 = jnp.pad(first_kernel.reshape(108, 32), ((0, 20), (0, 0)))
    w1, w2, wb = call(
        prep_kernel,
        (shape((256, 256), BF16), shape((3, 64, 288), BF16), shape((96, 576), BF16)),
        (k1, second_kernel.reshape(864, 64), sel),
    )
    deep, packed = call(
        main_kernel,
        (shape((64, 256), BF16), shape((ROWS, 128), F32)),
        (
            own, chip, link, deep_grad.reshape(64, 256), w1, w2, wb,
            first_bias.reshape(32, 1), second_bias.reshape(64, 1), sel,
            jnp.asarray(split_width(), BF16), jnp.asarray(pool_lanes(), BF16),
        ),
        (
            ((1280, 128), F32), ((640, 256), F32), ((640, 256), F32), ((640, 1024), BF16),
            ((4, 256, 1024), F32), ((4, 32, 1024), F32), ((4, 288, 1024), BF16), ((2, 64, 1024), F32),
            ((2, 576, 1024), BF16), ((4, 32, 1024), F32), ((64, 1024), F32), ((256, 1024), BF16), ((864, 64), F32),
        ),
        40 * 1024 * 1024,
    )
    pieces = lax.all_to_all(packed.reshape(256, 2, 128), AXES, split_axis=0, concat_axis=0, tiled=True)
    (copies,) = call(sum_kernel, (shape((ROWS, 128), F32),), (pieces.reshape(ROWS, 128),))
    whole = lax.all_to_all(copies.reshape(256, 2, 128), AXES, split_axis=0, concat_axis=0, tiled=True)
    second, first, bias1, bias2 = call(
        unpack_kernel,
        (shape((864, 64), F32), shape((27, 4, 32), F32), shape((1, 32), F32), shape((1, 64), F32)),
        (whole.reshape(ROWS, 128),),
    )
    return (
        deep.reshape(1, 64, 1, 8, 32),
        first.reshape(3, 3, 3, 4, 32),
        bias1.reshape(32),
        second.reshape(3, 3, 3, 32, 64),
        bias2.reshape(64),
    )


def solution(mesh):
    in_specs = (
        P("batch", None, "depth", "height", None),
        P(),
        P(),
        P(),
        P(),
        P(("batch", "height"), None, "depth", None, None),
    )
    out_specs = (P(("batch", "height"), None, "depth", None, None), P(), P(), P(), P())
    return jax.shard_map(
        per_device, mesh=mesh, in_specs=in_specs, out_specs=out_specs, check_vma=False
    )
```

```python
import jax
import jax.numpy as jnp
import numpy as np
from jax import lax
from jax.experimental import pallas as pl
from jax.experimental.pallas import tpu as pltpu
from jax.sharding import Mesh, PartitionSpec as P

F32 = jnp.float32
BF16 = jnp.bfloat16
DEPTH = ("z", "x_lo", "core")
PLANE = ("x_lo", "core", "y", "x_hi")
ROWS = 512
MIB = 1024 * 1024
NT = (((1,), (1,)), ((), ()))


def window_index(a4, b4, k4, ch):
    half, low = divmod(a4, 2)
    hb, hs = ((1, 1), (0, 0), (1, 0), (0, 1))[b4]
    wb, ws = ((1, 1), (0, 0), (1, 0), (0, 1))[k4]
    return half * 128 + (hs * 2 + ws) * 32 + hb * 16 + wb * 8 + low * 4 + ch


def select_taps():
    sel = np.zeros((128, 2048), np.float32)
    for pos in range(8):
        dz, dy, dx = pos // 4, pos // 2 % 2, pos % 2
        for a in range(3):
            for b in range(3):
                for c in range(3):
                    for ch in range(4):
                        tap = ((a * 3 + b) * 3 + c) * 4 + ch
                        sel[tap, pos * 256 + window_index(a + dz, b + dy, c + dx, ch)] = 1.0
    return sel


def split_width():
    out = np.zeros((256, 256), np.float32)
    for row in range(2):
        for cell in range(128):
            out[row * 128 + cell, (cell % 2) * 128 + row * 64 + cell // 2] = 1.0
    return out


def pool_lanes():
    out = np.zeros((512, 128), np.float32)
    for lane in range(512):
        out[lane, lane // 128 * 32 + lane % 64 // 2] = 0.125
    return out


def dot(a, b):
    return jnp.dot(a, b, preferred_element_type=F32)


def dot_nt(a, b):
    return lax.dot_general(a, b, NT, preferred_element_type=F32)


def prep_kernel(k1_ref, k2_ref, sel_ref, w1_ref, w2_ref, wb_ref):
    flat = lax.dot_general(k1_ref[...], sel_ref[0:108, :], (((0,), (0,)), ((), ())), preferred_element_type=F32)
    for pos in range(8):
        w1_ref[pos * 32 : pos * 32 + 32, :] = (0.5 * flat[:, pos * 256 : pos * 256 + 256]).astype(BF16)
    rows = lax.broadcasted_iota(jnp.int32, (64, 64), 0)
    cols = lax.broadcasted_iota(jnp.int32, (64, 64), 1)
    half_eye = jnp.where(rows == cols, 0.5, 0.0).astype(BF16)
    for a in range(3):
        w2_ref[a] = dot_nt(half_eye, k2_ref[a * 288 : a * 288 + 288, :]).astype(BF16)
        blocks = []
        for b in range(3):
            for c in range(3):
                at = ((a * 3 + 2 - b) * 3 + 2 - c) * 32
                blocks.append(k2_ref[at : at + 32, :].astype(F32))
        wb_ref[a * 32 : a * 32 + 32, :] = jnp.concatenate(blocks, axis=1).astype(BF16)


def lane_masks(rows):
    lane = lax.broadcasted_iota(jnp.int32, (rows, 128), 1)
    cell = lane % 64
    return lane < 64, cell != 0, cell != 63


def width_shift(tiles, step, masks):
    _, not_first, not_last = masks
    if step < 0:
        return [jnp.where(not_first, pltpu.roll(t, 1, 1), 0.0) for t in tiles]
    return [jnp.where(not_last, pltpu.roll(t, 127, 1), 0.0) for t in tiles]


def height_shift(tiles, steps, masks):
    low = masks[0]
    swapped = [pltpu.roll(t, 64, 1) for t in tiles]
    zero = jnp.zeros_like(tiles[0])
    out = []
    for step in steps:
        if step < 0:
            before = [zero] + swapped[:-1]
            out.append([jnp.where(low, before[i], swapped[i]) for i in range(len(tiles))])
        else:
            after = swapped[1:] + [zero]
            out.append([jnp.where(low, swapped[i], after[i]) for i in range(len(tiles))])
    return out


def store_shifts(tiles, put, masks):
    for c in range(3):
        moved = tiles if c == 1 else width_shift(tiles, c - 1, masks)
        before, after = height_shift(moved, (-1, 1), masks)
        for b, group in enumerate((before, moved, after)):
            for t in range(8):
                put(b * 3 + c, t, group[t])


def main_kernel(
    own_ref, chip_ref, link_ref, dg_ref, w1_ref, w2_ref, wb_ref, b1_ref, b2_ref, sel_ref, split_ref, pool_ref,
    deep_ref, packed_ref,
    f_ref, l_ref, g_ref, x_ref, slope_ref, y_ref, z_ref, g2_ref, gz_ref, back_ref, ds_ref, g1_ref, kg_ref,
):
    place = lax.axis_index(DEPTH)
    parity = place % 2
    keep_low = jnp.where(place > 0, 1.0, 0.0).astype(F32)
    keep_high = jnp.where(place < lax.axis_size(DEPTH) - 1, 1.0, 0.0).astype(F32)

    def fill(ref, plane, at):
        for y in range(4):
            for ch in range(4):
                f_ref[pl.ds((at * 4 + ch) * 32 + y * 8, 8), :] = ref[y, ch, plane].astype(F32)

    for plane in range(4):
        fill(own_ref, plane, 3 + plane)

    @pl.when(parity == 0)
    def _():
        for plane in range(3):
            fill(link_ref, plane + 1, plane)
            fill(chip_ref, plane, 7 + plane)

    @pl.when(parity == 1)
    def _():
        for plane in range(3):
            fill(chip_ref, plane + 1, plane)
            fill(link_ref, plane, 7 + plane)

    for hb in range(2):
        for qq in range(8):
            for low in range(2):
                l_ref[pl.ds((hb * 8 + qq) * 40, 40), low * 128 : low * 128 + 128] = f_ref[
                    pl.ds(4 * qq + 2 * low + hb, 40, stride=32), :
                ]
    g_ref[...] = dot(l_ref[...].astype(BF16), split_ref[...])

    masks8 = lane_masks(8)
    for pair in range(5):
        for hb in range(2):
            still, moved = [], []
            for wb in range(2):
                tiles = [
                    g_ref[(hb * 8 + qq) * 40 + pair * 8 : (hb * 8 + qq) * 40 + pair * 8 + 8, wb * 128 : wb * 128 + 128]
                    for qq in range(8)
                ]
                still.append(tiles)
                moved.append(width_shift(tiles, 1 if wb == 0 else -1, masks8))
            for ws, group in enumerate((still, moved)):
                step = 1 if hb == 0 else -1
                raised = [height_shift(group[wb], (step,), masks8)[0] for wb in range(2)]
                for hs, part in enumerate((group, raised)):
                    at = pair * 128 + (hs * 2 + ws) * 32 + hb * 16
                    for qq in range(8):
                        both = jnp.concatenate([part[0][qq], part[1][qq]], axis=0)
                        x_ref[at : at + 16, qq * 128 : qq * 128 + 128] = both.astype(BF16)

    bias1 = jnp.broadcast_to(0.5 * b1_ref[...], (32, 256))
    for plane in range(4):
        for t in range(4):
            lanes = slice(t * 256, t * 256 + 256)
            pre = dot(w1_ref[...], x_ref[plane * 128 : plane * 128 + 256, lanes])
            total = jnp.zeros((32, 256), F32)
            for pos in range(8):
                u = pre[pos * 32 : pos * 32 + 32] + bias1
                tanh = jnp.tanh(u)
                w = 1.0 + tanh
                silu = u * w
                slope_ref[plane, pos * 32 : pos * 32 + 32, lanes] = w + silu * (1.0 - tanh)
                total = total + silu
            scale = 0.125
            if plane == 0:
                scale = 0.125 * keep_low
            if plane == 3:
                scale = 0.125 * keep_high
            y_ref[plane, :, lanes] = total * scale

    masks32 = lane_masks(32)
    for plane in range(4):

        def put(at, t, value, plane=plane):
            z_ref[plane, at * 32 : at * 32 + 32, t * 128 : t * 128 + 128] = value.astype(BF16)

        store_shifts([y_ref[plane, :, t * 128 : t * 128 + 128] for t in range(8)], put, masks32)

    bias2 = jnp.broadcast_to(0.5 * b2_ref[...], (64, 256))
    sum2 = jnp.zeros((64, 128), F32)
    for plane in range(2):
        for t in range(4):
            lanes = slice(t * 256, t * 256 + 256)
            if plane == 0 and t % 2 == 0:
                wide = dot_nt(dg_ref[:, t * 64 : t * 64 + 128], pool_ref[...])
                g2_ref[0, :, t * 256 : t * 256 + 512] = wide
                g2_ref[1, :, t * 256 : t * 256 + 512] = wide
            u = bias2
            for a in range(3):
                u = u + dot(w2_ref[a], z_ref[plane + a, :, lanes])
            tanh = jnp.tanh(u)
            w = 1.0 + tanh
            silu = u * w
            if plane == 0:
                ds_ref[:, lanes] = silu
            else:
                ds_ref[:, lanes] = ds_ref[:, lanes] + silu
            grad = (0.5 * g2_ref[plane, :, lanes]) * (w + silu * (1.0 - tanh))
            g2_ref[plane, :, lanes] = grad
            sum2 = sum2 + grad[:, :128] + grad[:, 128:]

    for half in range(2):
        part = ds_ref[:, half * 512 : half * 512 + 512]
        high = part.astype(BF16)
        low = (part - high.astype(F32)).astype(BF16)
        deep = dot(high, pool_ref[...]) + dot(low, pool_ref[...])
        deep_ref[:, half * 128 : half * 128 + 128] = deep.astype(BF16)

    masks64 = lane_masks(64)
    for plane in range(2):

        def put(at, t, value, plane=plane):
            gz_ref[plane, at * 64 : at * 64 + 64, t * 128 : t * 128 + 128] = value.astype(BF16)

        store_shifts([g2_ref[plane, :, t * 128 : t * 128 + 128] for t in range(8)], put, masks64)

    for a in range(3):
        total = dot_nt(z_ref[a], gz_ref[0, 256:320, :]) + dot_nt(z_ref[a + 1], gz_ref[1, 256:320, :])
        kg_ref[a * 288 : a * 288 + 288, :] = total

    for t in range(4):
        lanes = slice(t * 256, t * 256 + 256)
        one = dot(wb_ref[...], gz_ref[0, :, lanes])
        two = dot(wb_ref[...], gz_ref[1, :, lanes])
        back_ref[0, :, lanes] = one[0:32] * (0.0625 * keep_low)
        back_ref[1, :, lanes] = (one[32:64] + two[0:32]) * 0.0625
        back_ref[2, :, lanes] = (one[64:96] + two[32:64]) * 0.0625
        back_ref[3, :, lanes] = two[64:96] * (0.0625 * keep_high)

    sum1 = jnp.zeros((32, 128), F32)
    grads = jnp.zeros((256, 256), F32)
    for plane in range(4):
        for t in range(4):
            lanes = slice(t * 256, t * 256 + 256)
            back = back_ref[plane, :, lanes]
            for pos in range(8):
                grad = back * slope_ref[plane, pos * 32 : pos * 32 + 32, lanes]
                g1_ref[pos * 32 : pos * 32 + 32, lanes] = grad.astype(BF16)
                sum1 = sum1 + grad[:, :128] + grad[:, 128:]
        grads = grads + dot_nt(g1_ref[...], x_ref[plane * 128 : plane * 128 + 256, :])

    first = jnp.zeros((128, 32), F32)
    for pos in range(8):
        part = grads[pos * 32 : pos * 32 + 32]
        high = part.astype(BF16)
        low = (part - high.astype(F32)).astype(BF16)
        sel = sel_ref[:, pos * 256 : pos * 256 + 256]
        first = first + dot_nt(sel, high) + dot_nt(sel, low)

    ones = jnp.ones((8, 128), F32)
    bias_rows = [
        lax.dot_general(ones, s, NT, precision=lax.Precision.HIGHEST, preferred_element_type=F32) for s in (sum1, sum2)
    ]
    packed_ref[0:432, :] = jnp.concatenate([kg_ref[0:432, :], kg_ref[432:864, :]], axis=1)
    packed_ref[432:464, :] = jnp.concatenate([first[32 * i : 32 * i + 32] for i in range(4)], axis=1)
    packed_ref[464:472, :] = jnp.concatenate(bias_rows + [jnp.zeros((8, 32), F32)], axis=1)
    packed_ref[472:512, :] = jnp.zeros((40, 128), F32)


def sum_kernel(in_ref, out_ref):
    total = in_ref[0:16, :]
    for i in range(1, in_ref.shape[0] // 16):
        total = total + in_ref[16 * i : 16 * i + 16, :]
    for i in range(out_ref.shape[0] // 16):
        out_ref[16 * i : 16 * i + 16, :] = total


def unpack_kernel(in_ref, second_ref, first_ref, bias1_ref, bias2_ref):
    second_ref[0:432, :] = in_ref[0:432, 0:64]
    second_ref[432:864, :] = in_ref[0:432, 64:128]
    for g in range(4):
        for m in range(8):
            if 8 * g + m < 27:
                first_ref[8 * g + m] = in_ref[432 + 4 * m : 436 + 4 * m, 32 * g : 32 * g + 32]
    bias1_ref[...] = in_ref[464:465, 0:32]
    bias2_ref[...] = in_ref[464:465, 32:96]


def vmem(count):
    return [pl.BlockSpec(memory_space=pltpu.VMEM) for _ in range(count)]


def call(kernel, outs, inputs, scratch=(), limit=None):
    params = pltpu.CompilerParams(vmem_limit_bytes=limit) if limit else None
    return pl.pallas_call(
        kernel,
        out_shape=outs,
        in_specs=vmem(len(inputs)),
        out_specs=vmem(len(outs)),
        scratch_shapes=[pltpu.VMEM(shape, dtype) for shape, dtype in scratch],
        compiler_params=params,
    )(*inputs)


def shape(dims, dtype):
    return jax.ShapeDtypeStruct(dims, dtype)


def exchange(rows, axes):
    blocks = rows.reshape(-1, 16, 128)
    return lax.all_to_all(blocks, axes, split_axis=0, concat_axis=0, tiled=True).reshape(-1, 128)


def per_device(volumes, first_kernel, first_bias, second_kernel, second_bias, deep_grad):
    count = lax.axis_size(DEPTH)
    own = lax.all_to_all(volumes, "y", split_axis=0, concat_axis=0, tiled=True)
    chip = lax.ppermute(own, DEPTH, [(i, i ^ 1) for i in range(count)])
    pairs = [(i, i + 1) for i in range(1, count - 1, 2)]
    link = lax.ppermute(own, DEPTH, pairs + [(j, i) for i, j in pairs])

    sel = jnp.asarray(select_taps(), BF16)
    w1, w2, wb = call(
        prep_kernel,
        (shape((256, 256), BF16), shape((3, 64, 288), BF16), shape((96, 576), BF16)),
        (first_kernel.reshape(108, 32), second_kernel.reshape(864, 64), sel),
        limit=8 * MIB,
    )
    deep, packed = call(
        main_kernel,
        (shape((64, 256), BF16), shape((ROWS, 128), F32)),
        (
            own, chip, link, deep_grad.reshape(64, 256), w1, w2, wb,
            first_bias.reshape(32, 1), second_bias.reshape(64, 1), sel,
            jnp.asarray(split_width(), BF16), jnp.asarray(pool_lanes(), BF16),
        ),
        (
            ((1280, 128), F32), ((640, 256), F32), ((640, 256), F32), ((640, 1024), BF16),
            ((4, 256, 1024), F32), ((4, 32, 1024), F32), ((4, 288, 1024), BF16), ((2, 64, 1024), F32),
            ((2, 576, 1024), BF16), ((4, 32, 1024), F32), ((64, 1024), F32), ((256, 1024), BF16), ((864, 64), F32),
        ),
        24 * MIB,
    )
    pieces = exchange(packed, PLANE)
    (copies,) = call(sum_kernel, (shape((128, 128), F32),), (pieces,), limit=2 * MIB)
    parts = exchange(copies, "z")
    (copies,) = call(sum_kernel, (shape((ROWS, 128), F32),), (parts,), limit=2 * MIB)
    whole = exchange(copies, PLANE)
    second, first, bias1, bias2 = call(
        unpack_kernel,
        (shape((864, 64), F32), shape((27, 4, 32), F32), shape((1, 32), F32), shape((1, 64), F32)),
        (whole,),
        limit=4 * MIB,
    )
    return (
        deep.reshape(1, 64, 1, 8, 32),
        first.reshape(3, 3, 3, 4, 32),
        bias1.reshape(32),
        second.reshape(3, 3, 3, 32, 64),
        bias2.reshape(64),
    )


def solution(mesh):
    split = Mesh(mesh.devices.reshape(-1, 2, 2, *mesh.devices.shape[1:]), DEPTH + ("y", "x_hi"))
    samples = P(("x_hi", "y"), None, DEPTH, None, None)
    in_specs = (P("x_hi", None, DEPTH, "y", None), P(), P(), P(), P(), samples)
    out_specs = (samples, P(), P(), P(), P())
    return jax.shard_map(per_device, mesh=split, in_specs=in_specs, out_specs=out_specs, check_vma=False)
```

```python
import jax
import jax.numpy as jnp
import numpy as np
from jax import lax
from jax.experimental import pallas as pl
from jax.experimental.pallas import tpu as pltpu
from jax.sharding import Mesh, PartitionSpec as P

F32 = jnp.float32
BF16 = jnp.bfloat16
DEPTH = ("z", "x_lo", "core")
PLANE = ("x_lo", "core", "y", "x_hi")
ROWS = 512
MIB = 1024 * 1024
NT = (((1,), (1,)), ((), ()))


def window_index(a4, b4, k4, ch):
    half, low = divmod(a4, 2)
    hb, hs = ((1, 1), (0, 0), (1, 0), (0, 1))[b4]
    wb, ws = ((1, 1), (0, 0), (1, 0), (0, 1))[k4]
    return half * 128 + (hs * 2 + ws) * 32 + hb * 16 + wb * 8 + low * 4 + ch


def select_taps():
    sel = np.zeros((128, 2048), np.float32)
    for pos in range(8):
        dz, dy, dx = pos // 4, pos // 2 % 2, pos % 2
        for a in range(3):
            for b in range(3):
                for c in range(3):
                    for ch in range(4):
                        tap = ((a * 3 + b) * 3 + c) * 4 + ch
                        sel[tap, pos * 256 + window_index(a + dz, b + dy, c + dx, ch)] = 1.0
    return sel


def split_width():
    out = np.zeros((256, 256), np.float32)
    for row in range(2):
        for cell in range(128):
            out[row * 128 + cell, (cell % 2) * 128 + row * 64 + cell // 2] = 1.0
    return out


def pool_lanes():
    out = np.zeros((128, 512), np.float32)
    for lane in range(512):
        out[lane // 128 * 32 + lane % 64 // 2, lane] = 0.125
    return out


def dot(a, b):
    return jnp.dot(a, b, preferred_element_type=F32)


def dot_nt(a, b):
    return lax.dot_general(a, b, NT, preferred_element_type=F32)


def dot_tn(a, b):
    return lax.dot_general(a, b, (((0,), (0,)), ((), ())), preferred_element_type=F32)


def prep_kernel(k1_ref, k2_ref, sel_ref, w1_ref, w2_ref, wb_ref):
    flat = dot_tn(k1_ref[...], sel_ref[0:108, :])
    for pos in range(8):
        w1_ref[pos * 32 : pos * 32 + 32, :] = (0.5 * flat[:, pos * 256 : pos * 256 + 256]).astype(BF16)
    rows = lax.broadcasted_iota(jnp.int32, (64, 64), 0)
    cols = lax.broadcasted_iota(jnp.int32, (64, 64), 1)
    half_eye = jnp.where(rows == cols, 0.5, 0.0).astype(BF16)
    for a in range(3):
        w2_ref[a] = dot_nt(half_eye, k2_ref[a * 288 : a * 288 + 288, :]).astype(BF16)
        blocks = []
        for b in range(3):
            for c in range(3):
                at = ((a * 3 + 2 - b) * 3 + 2 - c) * 32
                blocks.append(k2_ref[at : at + 32, :].astype(F32))
        wb_ref[a * 32 : a * 32 + 32, :] = jnp.concatenate(blocks, axis=1).astype(BF16)


def lane_masks(rows):
    lane = lax.broadcasted_iota(jnp.int32, (rows, 128), 1)
    cell = lane % 64
    return lane < 64, cell != 0, cell != 63


def width_shift(tiles, step, masks):
    _, not_first, not_last = masks
    if step < 0:
        return [jnp.where(not_first, pltpu.roll(t, 1, 1), 0.0) for t in tiles]
    return [jnp.where(not_last, pltpu.roll(t, 127, 1), 0.0) for t in tiles]


def height_shift(tiles, steps, masks):
    low = masks[0]
    swapped = [pltpu.roll(t, 64, 1) for t in tiles]
    zero = jnp.zeros_like(tiles[0])
    out = []
    for step in steps:
        if step < 0:
            before = [zero] + swapped[:-1]
            out.append([jnp.where(low, before[i], swapped[i]) for i in range(len(tiles))])
        else:
            after = swapped[1:] + [zero]
            out.append([jnp.where(low, swapped[i], after[i]) for i in range(len(tiles))])
    return out


def store_shifts(tiles, put, masks):
    for c in range(3):
        moved = tiles if c == 1 else width_shift(tiles, c - 1, masks)
        before, after = height_shift(moved, (-1, 1), masks)
        for b, group in enumerate((before, moved, after)):
            for t in range(8):
                put(b * 3 + c, t, group[t])


def main_kernel(
    pair_ref, chip_ref, dg_ref, w1_ref, w2_ref, wb_ref, b1_ref, b2_ref, sel_ref, split_ref, pool_ref,
    deep_ref, packed_ref,
    f_ref, l_ref, g_ref, x_ref, slope_ref, y_ref, z_ref, g2_ref, gz_ref, back_ref, ds_ref, g1_ref, kg_ref,
):
    place = lax.axis_index(DEPTH)
    parity = place % 2
    keep_low = jnp.where(place > 0, 1.0, 0.0).astype(F32)
    keep_high = jnp.where(place < lax.axis_size(DEPTH) - 1, 1.0, 0.0).astype(F32)

    def fill(ref, cell, at, keep=None):
        for y in range(4):
            for ch in range(4):
                part = ref[cell // 4 * 4 + y, ch, cell % 4].astype(F32)
                f_ref[pl.ds((at * 4 + ch) * 32 + y * 8, 8), :] = part if keep is None else part * keep

    @pl.when(parity == 0)
    def _():
        for cell in range(1, 8):
            fill(pair_ref, cell, cell - 1, keep_low if cell < 4 else None)
        for cell in range(3):
            fill(chip_ref, cell, 7 + cell)

    @pl.when(parity == 1)
    def _():
        for cell in range(7):
            fill(pair_ref, cell, cell + 3, keep_high if cell >= 4 else None)
        for cell in range(5, 8):
            fill(chip_ref, cell, cell - 5)

    for hb in range(2):
        for qq in range(8):
            for low in range(2):
                l_ref[pl.ds((hb * 8 + qq) * 40, 40), low * 128 : low * 128 + 128] = f_ref[
                    pl.ds(4 * qq + 2 * low + hb, 40, stride=32), :
                ]
    g_ref[...] = dot(l_ref[...].astype(BF16), split_ref[...])

    masks8 = lane_masks(8)
    for pair in range(5):
        for hb in range(2):
            still, moved = [], []
            for wb in range(2):
                tiles = [
                    g_ref[(hb * 8 + qq) * 40 + pair * 8 : (hb * 8 + qq) * 40 + pair * 8 + 8, wb * 128 : wb * 128 + 128]
                    for qq in range(8)
                ]
                still.append(tiles)
                moved.append(width_shift(tiles, 1 if wb == 0 else -1, masks8))
            for ws, group in enumerate((still, moved)):
                step = 1 if hb == 0 else -1
                raised = [height_shift(group[wb], (step,), masks8)[0] for wb in range(2)]
                for hs, part in enumerate((group, raised)):
                    at = pair * 128 + (hs * 2 + ws) * 32 + hb * 16
                    for qq in range(8):
                        both = jnp.concatenate([part[0][qq], part[1][qq]], axis=0)
                        x_ref[at : at + 16, qq * 128 : qq * 128 + 128] = both.astype(BF16)

    bias1 = jnp.broadcast_to(0.5 * b1_ref[...], (32, 256))
    for plane in range(4):
        for t in range(4):
            lanes = slice(t * 256, t * 256 + 256)
            pre = dot(w1_ref[...], x_ref[plane * 128 : plane * 128 + 256, lanes])
            total = jnp.zeros((32, 256), F32)
            for pos in range(8):
                u = pre[pos * 32 : pos * 32 + 32] + bias1
                tanh = jnp.tanh(u)
                w = 1.0 + tanh
                silu = u * w
                slope_ref[plane, pos * 32 : pos * 32 + 32, lanes] = w + silu * (1.0 - tanh)
                total = total + silu
            scale = 0.125
            if plane == 0:
                scale = 0.125 * keep_low
            if plane == 3:
                scale = 0.125 * keep_high
            y_ref[plane, :, lanes] = total * scale

    masks32 = lane_masks(32)
    for plane in range(4):

        def put(at, t, value, plane=plane):
            z_ref[plane, at * 32 : at * 32 + 32, t * 128 : t * 128 + 128] = value.astype(BF16)

        store_shifts([y_ref[plane, :, t * 128 : t * 128 + 128] for t in range(8)], put, masks32)

    bias2 = jnp.broadcast_to(0.5 * b2_ref[...], (64, 256))
    sum2 = jnp.zeros((64, 128), F32)
    for plane in range(2):
        for t in range(4):
            lanes = slice(t * 256, t * 256 + 256)
            if plane == 0 and t % 2 == 0:
                wide = dot_tn(dg_ref[t * 64 : t * 64 + 128, :], pool_ref[...])
                g2_ref[0, :, t * 256 : t * 256 + 512] = wide
                g2_ref[1, :, t * 256 : t * 256 + 512] = wide
            u = bias2
            for a in range(3):
                u = u + dot(w2_ref[a], z_ref[plane + a, :, lanes])
            tanh = jnp.tanh(u)
            w = 1.0 + tanh
            silu = u * w
            if plane == 0:
                ds_ref[:, lanes] = silu
            else:
                ds_ref[:, lanes] = ds_ref[:, lanes] + silu
            grad = (0.5 * g2_ref[plane, :, lanes]) * (w + silu * (1.0 - tanh))
            g2_ref[plane, :, lanes] = grad
            sum2 = sum2 + grad[:, :128] + grad[:, 128:]

    for half in range(2):
        part = ds_ref[:, half * 512 : half * 512 + 512]
        high = part.astype(BF16)
        low = (part - high.astype(F32)).astype(BF16)
        deep = dot_nt(pool_ref[...], high) + dot_nt(pool_ref[...], low)
        deep_ref[half * 128 : half * 128 + 128, :] = deep.astype(BF16)

    masks64 = lane_masks(64)
    for plane in range(2):

        def put(at, t, value, plane=plane):
            gz_ref[plane, at * 64 : at * 64 + 64, t * 128 : t * 128 + 128] = value.astype(BF16)

        store_shifts([g2_ref[plane, :, t * 128 : t * 128 + 128] for t in range(8)], put, masks64)

    for a in range(3):
        total = dot_nt(z_ref[a], gz_ref[0, 256:320, :]) + dot_nt(z_ref[a + 1], gz_ref[1, 256:320, :])
        kg_ref[a * 288 : a * 288 + 288, :] = total

    for t in range(4):
        lanes = slice(t * 256, t * 256 + 256)
        one = dot(wb_ref[...], gz_ref[0, :, lanes])
        two = dot(wb_ref[...], gz_ref[1, :, lanes])
        back_ref[0, :, lanes] = one[0:32] * (0.0625 * keep_low)
        back_ref[1, :, lanes] = (one[32:64] + two[0:32]) * 0.0625
        back_ref[2, :, lanes] = (one[64:96] + two[32:64]) * 0.0625
        back_ref[3, :, lanes] = two[64:96] * (0.0625 * keep_high)

    sum1 = jnp.zeros((32, 128), F32)
    grads = jnp.zeros((256, 256), F32)
    for plane in range(4):
        for t in range(4):
            lanes = slice(t * 256, t * 256 + 256)
            back = back_ref[plane, :, lanes]
            for pos in range(8):
                grad = back * slope_ref[plane, pos * 32 : pos * 32 + 32, lanes]
                g1_ref[pos * 32 : pos * 32 + 32, lanes] = grad.astype(BF16)
                sum1 = sum1 + grad[:, :128] + grad[:, 128:]
        grads = grads + dot_nt(g1_ref[...], x_ref[plane * 128 : plane * 128 + 256, :])

    first = jnp.zeros((128, 32), F32)
    for pos in range(8):
        part = grads[pos * 32 : pos * 32 + 32]
        high = part.astype(BF16)
        low = (part - high.astype(F32)).astype(BF16)
        sel = sel_ref[:, pos * 256 : pos * 256 + 256]
        first = first + dot_nt(sel, high) + dot_nt(sel, low)

    ones = jnp.ones((8, 128), F32)
    bias_rows = [
        lax.dot_general(ones, s, NT, precision=lax.Precision.HIGHEST, preferred_element_type=F32) for s in (sum1, sum2)
    ]
    packed_ref[0:432, :] = jnp.concatenate([kg_ref[0:432, :], kg_ref[432:864, :]], axis=1)
    packed_ref[432:464, :] = jnp.concatenate([first[32 * i : 32 * i + 32] for i in range(4)], axis=1)
    packed_ref[464:472, :] = jnp.concatenate(bias_rows + [jnp.zeros((8, 32), F32)], axis=1)
    packed_ref[472:512, :] = jnp.zeros((40, 128), F32)


def sum_kernel(in_ref, out_ref):
    total = in_ref[0:16, :]
    for i in range(1, in_ref.shape[0] // 16):
        total = total + in_ref[16 * i : 16 * i + 16, :]
    for i in range(out_ref.shape[0] // 16):
        out_ref[16 * i : 16 * i + 16, :] = total


def unpack_kernel(in_ref, second_ref, first_ref, bias1_ref, bias2_ref):
    second_ref[0:432, :] = in_ref[0:432, 0:64]
    second_ref[432:864, :] = in_ref[0:432, 64:128]
    for g in range(4):
        for m in range(8):
            if 8 * g + m < 27:
                first_ref[8 * g + m] = in_ref[432 + 4 * m : 436 + 4 * m, 32 * g : 32 * g + 32]
    bias1_ref[...] = in_ref[464:465, 0:32]
    bias2_ref[...] = in_ref[464:465, 32:96]


def vmem(count):
    return [pl.BlockSpec(memory_space=pltpu.VMEM) for _ in range(count)]


def call(kernel, outs, inputs, scratch=(), limit=None, cost=None):
    params = pltpu.CompilerParams(vmem_limit_bytes=limit)
    return pl.pallas_call(
        kernel,
        out_shape=outs,
        in_specs=vmem(len(inputs)),
        out_specs=vmem(len(outs)),
        scratch_shapes=[pltpu.VMEM(shape, dtype) for shape, dtype in scratch],
        compiler_params=params,
        cost_estimate=cost,
    )(*inputs)


def shape(dims, dtype):
    return jax.ShapeDtypeStruct(dims, dtype)


def exchange(rows, axes):
    blocks = rows.reshape(-1, 16, 128)
    return lax.all_to_all(blocks, axes, split_axis=0, concat_axis=0, tiled=True).reshape(-1, 128)


def per_device(volumes, first_kernel, first_bias, second_kernel, second_bias, deep_grad):
    count = lax.axis_size(DEPTH)
    groups = [
        [slab % count * 4 + y for slab in (odd, odd + 1) for y in range(4)] for odd in range(1, count, 2)
    ]
    pair = lax.all_to_all(
        jnp.concatenate([volumes, volumes]), DEPTH + ("y",), 0, 0, axis_index_groups=groups, tiled=True
    )
    chip = lax.ppermute(pair, "core", [(0, 1), (1, 0)])

    sel = jnp.asarray(select_taps(), BF16)
    w1, w2, wb = call(
        prep_kernel,
        (shape((256, 256), BF16), shape((3, 64, 288), BF16), shape((96, 576), BF16)),
        (first_kernel.reshape(108, 32), second_kernel.reshape(864, 64), sel),
        limit=8 * MIB,
        cost=pl.CostEstimate(flops=10**8, bytes_accessed=10**6, transcendentals=0),
    )
    deep, packed = call(
        main_kernel,
        (shape((256, 64), BF16), shape((ROWS, 128), F32)),
        (
            pair, chip, deep_grad.reshape(64, 256).T, w1, w2, wb,
            first_bias.reshape(32, 1), second_bias.reshape(64, 1), sel,
            jnp.asarray(split_width(), BF16), jnp.asarray(pool_lanes(), BF16),
        ),
        (
            ((1280, 128), F32), ((640, 256), F32), ((640, 256), F32), ((640, 1024), BF16),
            ((4, 256, 1024), F32), ((4, 32, 1024), F32), ((4, 288, 1024), BF16), ((2, 64, 1024), F32),
            ((2, 576, 1024), BF16), ((4, 32, 1024), F32), ((64, 1024), F32), ((256, 1024), BF16), ((864, 64), F32),
        ),
        24 * MIB,
    )
    pieces = exchange(packed, PLANE)
    (copies,) = call(sum_kernel, (shape((128, 128), F32),), (pieces,), limit=2 * MIB)
    parts = exchange(copies, "z")
    (copies,) = call(sum_kernel, (shape((ROWS, 128), F32),), (parts,), limit=2 * MIB)
    whole = exchange(copies, PLANE)
    second, first, bias1, bias2 = call(
        unpack_kernel,
        (shape((864, 64), F32), shape((27, 4, 32), F32), shape((1, 32), F32), shape((1, 64), F32)),
        (whole,),
        limit=4 * MIB,
    )
    return (
        deep.T.reshape(1, 64, 1, 8, 32),
        first.reshape(3, 3, 3, 4, 32),
        bias1.reshape(32),
        second.reshape(3, 3, 3, 32, 64),
        bias2.reshape(64),
    )


def solution(mesh):
    split = Mesh(mesh.devices.reshape(-1, 2, 2, *mesh.devices.shape[1:]), DEPTH + ("y", "x_hi"))
    samples = P(("x_hi", "y"), None, DEPTH, None, None)
    in_specs = (P("x_hi", None, DEPTH, "y", None), P(), P(), P(), P(), samples)
    out_specs = (samples, P(), P(), P(), P())
    return jax.shard_map(per_device, mesh=split, in_specs=in_specs, out_specs=out_specs, check_vma=False)
```

```python
import jax
import jax.numpy as jnp
from jax import lax
from jax.experimental import pallas as pl
from jax.experimental.pallas import tpu as pltpu
from jax.sharding import Mesh, PartitionSpec as P

F32 = jnp.float32
BF16 = jnp.bfloat16
DEPTH = ("z", "x_lo", "core")
PLANE = ("x_lo", "core", "y", "x_hi")
ROWS = 512
PLAIN = 27
MIB = 1024 * 1024
NT = (((1,), (1,)), ((), ()))


def iota(dims, dim):
    return lax.broadcasted_iota(jnp.int32, dims, dim)


def window_cell(shifted, odd):
    return jnp.where(shifted == 1, 3 - 3 * odd, 1 + odd)


def select_taps(pos):
    row = iota((1, 256), 1)
    a = (row >> 7) * 2 + ((row >> 2) & 1) - pos // 4
    b = window_cell((row >> 6) & 1, (row >> 4) & 1) - pos // 2 % 2
    c = window_cell((row >> 5) & 1, (row >> 3) & 1) - pos % 2
    low = jnp.minimum(jnp.minimum(a, b), c)
    high = jnp.maximum(jnp.maximum(a, b), c)
    tap = jnp.where((low >= 0) & (high <= 2), ((a * 3 + b) * 3 + c) * 4 + (row & 3), -1)
    return jnp.where(iota((128, 256), 0) == tap, 1.0, 0.0).astype(BF16)


def split_width():
    col = iota((1, 256), 1)
    at = ((col >> 6) & 1) * 128 + 2 * (col & 63) + (col >> 7)
    return jnp.where(iota((256, 256), 0) == at, 1.0, 0.0).astype(BF16)


def pool_lanes():
    lane = iota((1, 512), 1)
    at = (lane >> 7) * 32 + ((lane & 63) >> 1)
    return jnp.where(iota((128, 512), 0) == at, 0.125, 0.0).astype(BF16)


def half_column(row, size):
    spread = jnp.broadcast_to(0.5 * row, (size, size))
    eye = iota((size, size), 0) == iota((size, size), 1)
    return jnp.broadcast_to(jnp.sum(jnp.where(eye, spread, 0.0), axis=1, keepdims=True), (size, 128))


def dot(a, b):
    return jnp.dot(a, b, preferred_element_type=F32)


def dot_nt(a, b):
    return lax.dot_general(a, b, NT, preferred_element_type=F32)


def dot_tn(a, b):
    return lax.dot_general(a, b, (((0,), (0,)), ((), ())), preferred_element_type=F32)


def prep_kernel(
    k1_ref, k2_ref, b1_ref, b2_ref, dg_in_ref,
    w1_ref, w2_ref, wb_ref, bias1_ref, bias2_ref, dg_ref, sel_ref, split_ref, pool_ref,
):
    split_ref[...] = split_width()
    pool_ref[...] = pool_lanes()
    dg_ref[...] = dg_in_ref[...]
    bias1_ref[...] = half_column(b1_ref[...], 32)
    bias2_ref[...] = half_column(b2_ref[...], 64)
    for pos in range(8):
        sel = select_taps(pos)
        sel_ref[:, pos * 256 : pos * 256 + 256] = sel
        w1_ref[pos * 32 : pos * 32 + 32, :] = (0.5 * dot_tn(k1_ref[...], sel[0:108, :])).astype(BF16)
    half_eye = jnp.where(iota((64, 64), 0) == iota((64, 64), 1), 0.5, 0.0).astype(BF16)
    none = jnp.zeros((288, 64), BF16)
    for plane in range(2):
        stack = [none, k2_ref[...]] if plane else [k2_ref[...], none]
        w2_ref[plane * 64 : plane * 64 + 64, :] = dot_nt(half_eye, jnp.concatenate(stack, axis=0)).astype(BF16)
    blank = jnp.zeros((32, 64), F32)
    for target in range(4):
        blocks = []
        for plane in range(2):
            for b in range(3):
                for c in range(3):
                    a = target - plane
                    at = ((a * 3 + 2 - b) * 3 + 2 - c) * 32
                    blocks.append(k2_ref[at : at + 32, :].astype(F32) if 0 <= a <= 2 else blank)
        wb_ref[target * 32 : target * 32 + 32, :] = jnp.concatenate(blocks, axis=1).astype(BF16)


def lane_masks(rows):
    lane = iota((rows, 128), 1)
    cell = lane % 64
    return lane < 64, cell != 0, cell != 63


def width_shift(tiles, step, masks):
    _, not_first, not_last = masks
    if step < 0:
        return [jnp.where(not_first, pltpu.roll(t, 1, 1), 0.0) for t in tiles]
    return [jnp.where(not_last, pltpu.roll(t, 127, 1), 0.0) for t in tiles]


def height_shift(tiles, steps, masks):
    low = masks[0]
    swapped = [pltpu.roll(t, 64, 1) for t in tiles]
    zero = jnp.zeros_like(tiles[0])
    out = []
    for step in steps:
        if step < 0:
            before = [zero] + swapped[:-1]
            out.append([jnp.where(low, before[i], swapped[i]) for i in range(len(tiles))])
        else:
            after = swapped[1:] + [zero]
            out.append([jnp.where(low, swapped[i], after[i]) for i in range(len(tiles))])
    return out


def store_shifts(tiles, put, masks):
    for c in range(3):
        moved = tiles if c == 1 else width_shift(tiles, c - 1, masks)
        before, after = height_shift(moved, (-1, 1), masks)
        for b, group in enumerate((before, moved, after)):
            for t in range(8):
                put(b * 3 + c, t, group[t])


def main_kernel(
    pair_ref, chip_ref, w1_ref, w2_ref, wb_ref, b1_ref, b2_ref, dg_ref, sel_ref, split_ref, pool_ref,
    deep_ref, packed_ref,
    f_ref, l_ref, g_ref, x_ref, slope_ref, y_ref, z_ref, g2_ref, gg_ref, gz_ref, back_ref, ds_ref, g1_ref, kg_ref,
):
    place = lax.axis_index(DEPTH)
    parity = place % 2
    keep_low = jnp.where(place > 0, 1.0, 0.0).astype(F32)
    keep_high = jnp.where(place < lax.axis_size(DEPTH) - 1, 1.0, 0.0).astype(F32)

    def fill(ref, cell, at, keep=None):
        for y in range(4):
            for ch in range(4):
                part = ref[cell // 4 * 4 + y, ch, cell % 4].astype(F32)
                f_ref[pl.ds((at * 4 + ch) * 32 + y * 8, 8), :] = part if keep is None else part * keep

    @pl.when(parity == 0)
    def _():
        for cell in range(1, 8):
            fill(pair_ref, cell, cell - 1, keep_low if cell < 4 else None)
        for cell in range(3):
            fill(chip_ref, cell, 7 + cell)

    @pl.when(parity == 1)
    def _():
        for cell in range(7):
            fill(pair_ref, cell, cell + 3, keep_high if cell >= 4 else None)
        for cell in range(5, 8):
            fill(chip_ref, cell, cell - 5)

    for hb in range(2):
        for qq in range(8):
            for low in range(2):
                l_ref[pl.ds((hb * 8 + qq) * 40, 40), low * 128 : low * 128 + 128] = f_ref[
                    pl.ds(4 * qq + 2 * low + hb, 40, stride=32), :
                ]
    g_ref[...] = dot(l_ref[...].astype(BF16), split_ref[...])

    masks8 = lane_masks(8)
    for pair in range(5):
        for hb in range(2):
            still, moved = [], []
            for wb in range(2):
                tiles = [
                    g_ref[(hb * 8 + qq) * 40 + pair * 8 : (hb * 8 + qq) * 40 + pair * 8 + 8, wb * 128 : wb * 128 + 128]
                    for qq in range(8)
                ]
                still.append(tiles)
                moved.append(width_shift(tiles, 1 if wb == 0 else -1, masks8))
            for ws, group in enumerate((still, moved)):
                step = 1 if hb == 0 else -1
                raised = [height_shift(group[wb], (step,), masks8)[0] for wb in range(2)]
                for hs, part in enumerate((group, raised)):
                    at = pair * 128 + (hs * 2 + ws) * 32 + hb * 16
                    for qq in range(8):
                        both = jnp.concatenate([part[0][qq], part[1][qq]], axis=0)
                        x_ref[at : at + 16, qq * 128 : qq * 128 + 128] = both.astype(BF16)

    bias1 = jnp.concatenate([b1_ref[...], b1_ref[...]], axis=1)
    for plane in range(4):
        for t in range(4):
            lanes = slice(t * 256, t * 256 + 256)
            pre = dot(w1_ref[...], x_ref[plane * 128 : plane * 128 + 256, lanes])
            total = jnp.zeros((32, 256), F32)
            for pos in range(8):
                u = pre[pos * 32 : pos * 32 + 32] + bias1
                tanh = jnp.tanh(u)
                w = 1.0 + tanh
                silu = u * w
                slope_ref[plane, pos * 32 : pos * 32 + 32, lanes] = w + silu * (1.0 - tanh)
                total = total + silu
            scale = 0.125
            if plane == 0:
                scale = 0.125 * keep_low
            if plane == 3:
                scale = 0.125 * keep_high
            y_ref[plane, :, lanes] = total * scale

    masks32 = lane_masks(32)
    for plane in range(4):

        def put(at, t, value, plane=plane):
            row = plane * 288 + at * 32
            z_ref[row : row + 32, t * 128 : t * 128 + 128] = value.astype(BF16)

        store_shifts([y_ref[plane, :, t * 128 : t * 128 + 128] for t in range(8)], put, masks32)

    bias2 = jnp.concatenate([b2_ref[...], b2_ref[...]], axis=1)
    sum2 = jnp.zeros((64, 128), F32)
    for half in range(2):
        wide = dot_tn(dg_ref[half * 128 : half * 128 + 128, :], pool_ref[...])
        g2_ref[0, :, half * 512 : half * 512 + 512] = wide
    for t in range(4):
        lanes = slice(t * 256, t * 256 + 256)
        pre = dot(w2_ref[...], z_ref[:, lanes])
        given = 0.5 * g2_ref[0, :, lanes]
        total = jnp.zeros((64, 256), F32)
        for plane in range(2):
            u = pre[plane * 64 : plane * 64 + 64] + bias2
            tanh = jnp.tanh(u)
            w = 1.0 + tanh
            silu = u * w
            total = total + silu
            grad = given * (w + silu * (1.0 - tanh))
            g2_ref[plane, :, lanes] = grad
            gg_ref[plane * 64 : plane * 64 + 64, lanes] = grad.astype(BF16)
            sum2 = sum2 + grad[:, :128] + grad[:, 128:]
        ds_ref[:, lanes] = total

    for half in range(2):
        part = ds_ref[:, half * 512 : half * 512 + 512]
        high, low = halves(part)
        deep = dot_nt(pool_ref[...], jnp.concatenate([high, low], axis=0))
        deep_ref[half * 128 : half * 128 + 128, :] = (deep[:, :64] + deep[:, 64:]).astype(BF16)

    masks64 = lane_masks(64)
    for plane in range(2):

        def put(at, t, value, plane=plane):
            row = plane * 576 + at * 64
            gz_ref[row : row + 64, t * 128 : t * 128 + 128] = value.astype(BF16)

        store_shifts([g2_ref[plane, :, t * 128 : t * 128 + 128] for t in range(8)], put, masks64)

    kg_ref[...] = dot_nt(z_ref[...], gg_ref[...])

    for t in range(4):
        lanes = slice(t * 256, t * 256 + 256)
        back = dot(wb_ref[...], gz_ref[:, lanes])
        back_ref[0:32, lanes] = back[0:32] * (0.0625 * keep_low)
        back_ref[32:96, lanes] = back[32:96] * 0.0625
        back_ref[96:128, lanes] = back[96:128] * (0.0625 * keep_high)

    sum1 = jnp.zeros((32, 128), F32)
    grads = jnp.zeros((256, 256), F32)
    for plane in range(4):
        for t in range(4):
            lanes = slice(t * 256, t * 256 + 256)
            back = back_ref[plane * 32 : plane * 32 + 32, lanes]
            for pos in range(8):
                grad = back * slope_ref[plane, pos * 32 : pos * 32 + 32, lanes]
                g1_ref[pos * 32 : pos * 32 + 32, lanes] = grad.astype(BF16)
                sum1 = sum1 + grad[:, :128] + grad[:, 128:]
        grads = grads + dot_nt(g1_ref[...], x_ref[plane * 128 : plane * 128 + 256, :])

    spread = jnp.concatenate([grads[pos * 32 : pos * 32 + 32] for pos in range(8)], axis=1)
    high, low = halves(spread)
    first = dot_nt(jnp.concatenate([high, low], axis=0), sel_ref[...])
    biases = lax.dot_general(
        jnp.ones((8, 128), F32),
        jnp.concatenate([sum1, sum2, jnp.zeros((32, 128), F32)], axis=0),
        NT,
        precision=lax.Precision.HIGHEST,
        preferred_element_type=F32,
    )

    low_lanes = iota((432, 128), 1) < 64
    left = kg_ref[0:432, :] + pltpu.roll(kg_ref[288:720, :], 64, 1)
    right = pltpu.roll(kg_ref[432:864, :], 64, 1) + kg_ref[720:1152, :]
    packed_ref[0:432, :] = jnp.where(low_lanes, left, right).astype(BF16)
    first = first[:32] + first[32:]
    for block in range(5):
        rows = first[block * 8 : block * 8 + 8] if block < 4 else biases
        at = PLAIN * 16 + block * 16
        packed_ref[at : at + 16, :] = jnp.concatenate(halves(rows), axis=0)


def halves(rows):
    high = rows.astype(BF16)
    return high, (rows - high.astype(F32)).astype(BF16)


def block_sum(ref):
    total = ref[0:16, :].astype(F32)
    for i in range(1, ref.shape[0] // 16):
        total = total + ref[16 * i : 16 * i + 16, :].astype(F32)
    return total


def plane_sum_kernel(in_ref, out_ref):
    total = block_sum(in_ref)
    split = lax.axis_index(PLANE) >= PLAIN
    rows = total[0:8] + total[8:16]
    total = jnp.where(split, jnp.concatenate([rows, rows], axis=0), total)
    for i in range(out_ref.shape[0] // 16):
        out_ref[16 * i : 16 * i + 16, :] = total


def whole_sum_kernel(in_ref, out_ref):
    total = block_sum(in_ref)
    split = lax.axis_index(PLANE) >= PLAIN
    rows = total[0:8]
    rest = jnp.where(split, rows - rows.astype(BF16).astype(F32), total[8:16])
    total = jnp.concatenate([rows, rest], axis=0).astype(BF16)
    for i in range(out_ref.shape[0] // 16):
        out_ref[16 * i : 16 * i + 16, :] = total


def unpack_kernel(in_ref, second_ref, first_ref, bias1_ref, bias2_ref):
    second_ref[0:432, :] = in_ref[0:432, 0:64].astype(F32)
    second_ref[432:864, :] = in_ref[0:432, 64:128].astype(F32)
    blocks = [in_ref[at : at + 16, :].astype(F32) for at in range(PLAIN * 16, ROWS, 16)]
    rows = [block[0:8] + block[8:16] for block in blocks]
    first = jnp.concatenate(rows[:4], axis=0).T
    for tap in range(27):
        first_ref[tap] = first[4 * tap : 4 * tap + 4, :]
    bias1_ref[...] = rows[4][0:1, 0:32]
    bias2_ref[...] = rows[4][0:1, 32:96]


def vmem(count):
    return [pl.BlockSpec(memory_space=pltpu.VMEM) for _ in range(count)]


def call(kernel, outs, inputs, scratch=(), limit=None, cost=None):
    params = pltpu.CompilerParams(vmem_limit_bytes=limit)
    return pl.pallas_call(
        kernel,
        out_shape=outs,
        in_specs=vmem(len(inputs)),
        out_specs=vmem(len(outs)),
        scratch_shapes=[pltpu.VMEM(shape, dtype) for shape, dtype in scratch],
        compiler_params=params,
        cost_estimate=cost,
    )(*inputs)


def shape(dims, dtype):
    return jax.ShapeDtypeStruct(dims, dtype)


def exchange(rows, axes):
    blocks = rows.reshape(-1, 16, 128)
    return lax.all_to_all(blocks, axes, split_axis=0, concat_axis=0, tiled=True).reshape(-1, 128)


def per_device(volumes, first_kernel, first_bias, second_kernel, second_bias, deep_grad):
    count = lax.axis_size(DEPTH)
    groups = [
        [slab % count * 4 + y for slab in (odd, odd + 1) for y in range(4)] for odd in range(1, count, 2)
    ]
    twice = jnp.concatenate([volumes, volumes])
    pair = lax.all_to_all(twice, DEPTH + ("y",), 0, 0, axis_index_groups=groups, tiled=True)
    prepared = call(
        prep_kernel,
        (
            shape((256, 256), BF16), shape((128, 1152), BF16), shape((128, 1152), BF16), shape((32, 128), F32),
            shape((64, 128), F32), shape((256, 64), BF16), shape((128, 2048), BF16), shape((256, 256), BF16),
            shape((128, 512), BF16),
        ),
        (
            first_kernel.reshape(108, 32), second_kernel.reshape(864, 64), first_bias.reshape(1, 32),
            second_bias.reshape(1, 64), deep_grad.reshape(64, 256).T,
        ),
        limit=8 * MIB,
        cost=pl.CostEstimate(flops=10**8, bytes_accessed=10**6, transcendentals=0),
    )
    chip = lax.ppermute(pair, "core", [(0, 1), (1, 0)])
    deep, packed = call(
        main_kernel,
        (shape((256, 64), BF16), shape((ROWS, 128), BF16)),
        (pair, chip, *prepared),
        (
            ((1280, 128), F32), ((640, 256), F32), ((640, 256), F32), ((640, 1024), BF16),
            ((4, 256, 1024), F32), ((4, 32, 1024), F32), ((1152, 1024), BF16), ((2, 64, 1024), F32),
            ((128, 1024), BF16), ((1152, 1024), BF16), ((128, 1024), F32), ((64, 1024), F32), ((256, 1024), BF16),
            ((1152, 128), F32),
        ),
        24 * MIB,
    )
    pieces = exchange(packed, PLANE)
    (copies,) = call(plane_sum_kernel, (shape((128, 128), F32),), (pieces,), limit=2 * MIB)
    parts = exchange(copies, "z")
    (copies,) = call(whole_sum_kernel, (shape((ROWS, 128), BF16),), (parts,), limit=2 * MIB)
    whole = exchange(copies, PLANE)
    second, first, bias1, bias2 = call(
        unpack_kernel,
        (shape((864, 64), F32), shape((27, 4, 32), F32), shape((1, 32), F32), shape((1, 64), F32)),
        (whole,),
        limit=4 * MIB,
    )
    return (
        deep.T.reshape(1, 64, 1, 8, 32),
        first.reshape(3, 3, 3, 4, 32),
        bias1.reshape(32),
        second.reshape(3, 3, 3, 32, 64),
        bias2.reshape(64),
    )


def solution(mesh):
    split = Mesh(mesh.devices.reshape(-1, 2, 2, *mesh.devices.shape[1:]), DEPTH + ("y", "x_hi"))
    samples = P(("x_hi", "y"), None, DEPTH, None, None)
    in_specs = (P("x_hi", None, DEPTH, "y", None), P(), P(), P(), P(), samples)
    out_specs = (samples, P(), P(), P(), P())
    return jax.shard_map(per_device, mesh=split, in_specs=in_specs, out_specs=out_specs, check_vma=False)
```

```python
import jax
import jax.numpy as jnp
from jax import lax
from jax.experimental import pallas as pl
from jax.experimental.pallas import tpu as pltpu
from jax.sharding import Mesh, PartitionSpec as P

F32 = jnp.float32
BF16 = jnp.bfloat16
DEPTH = ("z", "x_lo", "core")
PLANE = ("x_lo", "core", "y", "x_hi")
LINE = ("z",)
ROWS = 512
CHUNK = 16
PLAIN = 27
MIB = 1024 * 1024
NT = (((1,), (1,)), ((), ()))


def iota(dims, dim):
    return lax.broadcasted_iota(jnp.int32, dims, dim)


def window_cell(shifted, odd):
    return jnp.where(shifted == 1, 3 - 3 * odd, 1 + odd)


def select_taps(pos):
    row = iota((1, 256), 1)
    a = (row >> 7) * 2 + ((row >> 2) & 1) - pos // 4
    b = window_cell((row >> 6) & 1, (row >> 4) & 1) - pos // 2 % 2
    c = window_cell((row >> 5) & 1, (row >> 3) & 1) - pos % 2
    low = jnp.minimum(jnp.minimum(a, b), c)
    high = jnp.maximum(jnp.maximum(a, b), c)
    tap = jnp.where((low >= 0) & (high <= 2), ((a * 3 + b) * 3 + c) * 4 + (row & 3), -1)
    return jnp.where(iota((128, 256), 0) == tap, 1.0, 0.0).astype(BF16)


def split_width():
    col = iota((1, 256), 1)
    at = ((col >> 6) & 1) * 128 + 2 * (col & 63) + (col >> 7)
    return jnp.where(iota((256, 256), 0) == at, 1.0, 0.0).astype(BF16)


def pool_lanes():
    lane = iota((1, 512), 1)
    at = (lane >> 7) * 32 + ((lane & 63) >> 1)
    return jnp.where(iota((128, 512), 0) == at, 0.125, 0.0).astype(BF16)


def half_column(row, size):
    spread = jnp.broadcast_to(0.5 * row, (size, size))
    eye = iota((size, size), 0) == iota((size, size), 1)
    return jnp.broadcast_to(jnp.sum(jnp.where(eye, spread, 0.0), axis=1, keepdims=True), (size, 128))


def dot(a, b):
    return jnp.dot(a, b, preferred_element_type=F32)


def dot_nt(a, b):
    return lax.dot_general(a, b, NT, preferred_element_type=F32)


def dot_tn(a, b):
    return lax.dot_general(a, b, (((0,), (0,)), ((), ())), preferred_element_type=F32)


def front_kernel(
    volumes_hbm, k1_hbm, k2_hbm, b1_hbm, b2_hbm, dg_hbm,
    twice_ref, w1_ref, w2_ref, wb_ref, bias1_ref, bias2_ref, dg_ref, sel_ref, split_ref, pool_ref,
    k1_in, k1_ref, k2_ref, b1_ref, b2_ref, sems,
):
    pairs = (
        (k1_hbm, k1_in), (k2_hbm, k2_ref), (b1_hbm, b1_ref), (b2_hbm, b2_ref), (dg_hbm, dg_ref),
        (volumes_hbm, twice_ref.at[pl.ds(0, 4)]), (volumes_hbm, twice_ref.at[pl.ds(4, 4)]),
    )
    copies = [pltpu.make_async_copy(src, dst, sems.at[n]) for n, (src, dst) in enumerate(pairs)]
    for copy in copies:
        copy.start()
    split_ref[...] = split_width()
    pool_ref[...] = pool_lanes()
    sels = [select_taps(pos) for pos in range(8)]
    for pos in range(8):
        sel_ref[:, pos * 256 : pos * 256 + 256] = sels[pos]
    for copy in copies[:5]:
        copy.wait()
    bias1_ref[...] = half_column(b1_ref[...], 32)
    bias2_ref[...] = half_column(b2_ref[...], 64)
    for tap in range(27):
        k1_ref[4 * tap : 4 * tap + 4, :] = 0.5 * k1_in[tap].astype(F32)
    k1_ref[108:128, :] = jnp.zeros((20, 32), F32)
    k1 = k1_ref[...].astype(BF16)
    for pos in range(8):
        w1_ref[pos * 32 : pos * 32 + 32, :] = dot_tn(k1, sels[pos]).astype(BF16)
    half_eye = jnp.where(iota((64, 64), 0) == iota((64, 64), 1), 0.5, 0.0).astype(BF16)
    none = jnp.zeros((32, 64), BF16)

    def tap(a, b, c):
        at = ((a * 3 + b) * 3 + c) * 32
        return k2_ref[at : at + 32, :] if 0 <= a <= 2 else none

    for c in range(3):
        for plane in range(2):
            stack = [tap(rim - plane, b, c) for rim in range(4) for b in range(3)]
            at = (c * 2 + plane) * 64
            w2_ref[at : at + 64, :] = dot_nt(half_eye, jnp.concatenate(stack, axis=0)).astype(BF16)
        for rim in range(4):
            row = [tap(rim - plane, 2 - b, 2 - c).astype(F32) for plane in range(2) for b in range(3)]
            at = (c * 4 + rim) * 32
            wb_ref[at : at + 32, :] = jnp.concatenate(row, axis=1).astype(BF16)
    for copy in copies[5:]:
        copy.wait()


def lane_masks(rows):
    lane = iota((rows, 128), 1)
    cell = lane % 64
    return lane < 64, cell != 0, cell != 63


def width_shift(tiles, step, masks):
    _, not_first, not_last = masks
    if step < 0:
        return [jnp.where(not_first, pltpu.roll(t, 1, 1), 0.0) for t in tiles]
    return [jnp.where(not_last, pltpu.roll(t, 127, 1), 0.0) for t in tiles]


def height_shift(tiles, steps, masks):
    low = masks[0]
    swapped = [pltpu.roll(t, 64, 1) for t in tiles]
    zero = jnp.zeros_like(tiles[0])
    out = []
    for step in steps:
        if step < 0:
            before = [zero] + swapped[:-1]
            out.append([jnp.where(low, before[i], swapped[i]) for i in range(len(tiles))])
        else:
            after = swapped[1:] + [zero]
            out.append([jnp.where(low, swapped[i], after[i]) for i in range(len(tiles))])
    return out


def store_height_shifts(ref, put, masks):
    tiles = [ref[:, t * 128 : t * 128 + 128] for t in range(8)]
    before, after = height_shift(tiles, (-1, 1), masks)
    for b, group in enumerate((before, tiles, after)):
        for t in range(8):
            put(b, t, group[t].astype(BF16))


def add_width_shifts(parts, masks):
    sides = []
    for half in range(2):
        one, two, three = (part[:, half * 128 : half * 128 + 128] for part in parts)
        sides.append(two + width_shift([one], -1, masks)[0] + width_shift([three], 1, masks)[0])
    return jnp.concatenate(sides, axis=1)


def grid_ends():
    place = lax.axis_index(DEPTH)
    keep_low = jnp.where(place > 0, 1.0, 0.0).astype(F32)
    keep_high = jnp.where(place < lax.axis_size(DEPTH) - 1, 1.0, 0.0).astype(F32)
    return place % 2, keep_low, keep_high


def fill(f_ref, ref, cell, at, keep=None):
    for y in range(4):
        for ch in range(4):
            part = ref[cell // 4 * 4 + y, ch, cell % 4].astype(F32)
            f_ref[pl.ds((at * 4 + ch) * 32 + y * 8, 8), :] = part if keep is None else part * keep


def split_rows(f_ref, l_ref, g_ref, split_ref, rows):
    for hb in range(2):
        for qq in range(8):
            for low in range(2):
                l_ref[pl.ds((hb * 8 + qq) * rows, rows), low * 128 : low * 128 + 128] = f_ref[
                    pl.ds(4 * qq + 2 * low + hb, rows, stride=32), :
                ]
    g_ref[...] = dot(l_ref[...].astype(BF16), split_ref[...])


def store_windows(g_ref, rows, pair, put):
    masks = lane_masks(8)
    for hb in range(2):
        still, moved = [], []
        for wb in range(2):
            starts = [(hb * 8 + qq) * rows + pair * 8 for qq in range(8)]
            tiles = [g_ref[at : at + 8, wb * 128 : wb * 128 + 128] for at in starts]
            still.append(tiles)
            moved.append(width_shift(tiles, 1 if wb == 0 else -1, masks))
        for ws, group in enumerate((still, moved)):
            step = 1 if hb == 0 else -1
            raised = [height_shift(group[wb], (step,), masks)[0] for wb in range(2)]
            for hs, part in enumerate((group, raised)):
                for qq in range(8):
                    both = jnp.concatenate([part[0][qq], part[1][qq]], axis=0)
                    put((hs * 2 + ws) * 32 + hb * 16, qq, both.astype(BF16))


def first_conv(x_ref, w1_ref, b1_ref, slope_ref, y_ref, scales):
    bias = jnp.concatenate([b1_ref[...], b1_ref[...]], axis=1)
    for plane in range(2):
        for t in range(4):
            lanes = slice(t * 256, t * 256 + 256)
            pre = dot(w1_ref[...], x_ref[plane * 128 : plane * 128 + 256, lanes])
            total = jnp.zeros((32, 256), F32)
            for pos in range(8):
                u = pre[pos * 32 : pos * 32 + 32] + bias
                tanh = jnp.tanh(u)
                w = 1.0 + tanh
                silu = u * w
                slope_ref[plane, pos * 32 : pos * 32 + 32, lanes] = w + silu * (1.0 - tanh)
                total = total + silu
            y_ref[plane, :, lanes] = total * scales[plane]


def store_second_windows(y_ref, put):
    masks = lane_masks(32)
    for plane in range(2):
        store_height_shifts(y_ref.at[plane], lambda b, t, value, plane=plane: put(plane * 96 + b * 32, t, value), masks)


def early_kernel(
    pair_ref, w1_ref, b1_ref, split_ref, x_ref, slope_ref, z_ref, f_ref, l_ref, g_ref, y_ref
):
    _, keep_low, keep_high = grid_ends()
    for cell in range(1, 7):
        fill(f_ref, pair_ref, cell, cell - 1, keep_low if cell < 4 else keep_high)
    split_rows(f_ref, l_ref, g_ref, split_ref, 24)
    for pair in range(3):

        def put(row, t, value, pair=pair):
            x_ref[pair * 128 + row : pair * 128 + row + 16, t * 128 : t * 128 + 128] = value

        store_windows(g_ref, 24, pair, put)
    first_conv(x_ref, w1_ref, b1_ref, slope_ref, y_ref, (0.125 * keep_low, 0.125 * keep_high))

    def put_second(row, t, value):
        z_ref[row : row + 32, t * 128 : t * 128 + 128] = value

    store_second_windows(y_ref, put_second)


def main_kernel(
    pair_ref, chip_ref, early_x_ref, early_slope_ref, early_z_ref,
    w1_ref, w2_ref, wb_ref, b1_ref, b2_ref, dg_ref, sel_ref, split_ref, pool_ref,
    deep_ref, packed_ref,
    f_ref, l_ref, g_ref, x_ref, slope_ref, y_ref, z_ref, g2_ref, gg_ref, gz_ref, back_ref, ds_ref, g1_ref, kg_ref,
):
    parity, keep_low, keep_high = grid_ends()

    @pl.when(parity == 0)
    def _():
        fill(f_ref, pair_ref, 7, 0)
        for cell in range(3):
            fill(f_ref, chip_ref, cell, 1 + cell)

    @pl.when(parity == 1)
    def _():
        for cell in range(3):
            fill(f_ref, chip_ref, 5 + cell, cell)
        fill(f_ref, pair_ref, 0, 3)

    split_rows(f_ref, l_ref, g_ref, split_ref, 16)
    fresh = pl.multiple_of(128 * (1 - parity), 128)
    shared = pl.multiple_of(256 * parity, 128)
    x_ref[pl.ds(shared, 128), :] = early_x_ref[pl.ds(pl.multiple_of(256 * (1 - parity), 128), 128), :]
    for pair in range(2):

        def put(row, t, value, pair=pair):
            x_ref[pl.ds(pl.multiple_of(fresh + (pair * 128 + row), 16), 16), t * 128 : t * 128 + 128] = value

        store_windows(g_ref, 16, pair, put)
    first_conv(x_ref, w1_ref, b1_ref, slope_ref, y_ref, (0.125, 0.125))

    early_at = pl.multiple_of(192 * parity, 16)
    late_at = pl.multiple_of(192 * (1 - parity), 16)
    z_ref[pl.ds(early_at, 192), :] = early_z_ref[...]

    def put_second(row, t, value):
        z_ref[pl.ds(pl.multiple_of(late_at + row, 16), 32), t * 128 : t * 128 + 128] = value

    store_second_windows(y_ref, put_second)

    bias2 = jnp.concatenate([b2_ref[...], b2_ref[...]], axis=1)
    sum2 = jnp.zeros((64, 128), F32)
    masks64, masks128 = lane_masks(64), lane_masks(128)
    for half in range(2):
        wide = dot_tn(dg_ref[half * 128 : half * 128 + 128, :], pool_ref[...])
        g2_ref[0, :, half * 512 : half * 512 + 512] = wide
    for t in range(4):
        lanes = slice(t * 256, t * 256 + 256)
        taps = dot(w2_ref[...], z_ref[:, lanes])
        pre = add_width_shifts([taps[c * 128 : c * 128 + 128] for c in range(3)], masks128)
        given = 0.5 * g2_ref[0, :, lanes]
        total = jnp.zeros((64, 256), F32)
        for plane in range(2):
            u = pre[plane * 64 : plane * 64 + 64] + bias2
            tanh = jnp.tanh(u)
            w = 1.0 + tanh
            silu = u * w
            total = total + silu
            grad = given * (w + silu * (1.0 - tanh))
            g2_ref[plane, :, lanes] = grad
            for half in range(2):
                tile = grad[:, half * 128 : half * 128 + 128]
                at = t * 256 + half * 128
                for c, part in enumerate((width_shift([tile], 1, masks64), [tile], width_shift([tile], -1, masks64))):
                    row = c * 128 + plane * 64
                    gg_ref[row : row + 64, at : at + 128] = part[0].astype(BF16)
            sum2 = sum2 + grad[:, :128] + grad[:, 128:]
        ds_ref[:, lanes] = total

    for half in range(2):
        part = ds_ref[:, half * 512 : half * 512 + 512]
        high, low = halves(part)
        deep = dot_nt(pool_ref[...], jnp.concatenate([high, low], axis=0))
        deep_ref[half * 128 : half * 128 + 128, :] = (deep[:, :64] + deep[:, 64:]).astype(BF16)

    for plane in range(2):

        def put(b, t, value, plane=plane):
            row = plane * 192 + b * 64
            gz_ref[row : row + 64, t * 128 : t * 128 + 128] = value

        store_height_shifts(g2_ref.at[plane], put, masks64)
    for t in range(4):
        lanes = slice(t * 256, t * 256 + 256)
        taps = dot(wb_ref[...], gz_ref[:, lanes])
        back = add_width_shifts([taps[c * 128 : c * 128 + 128] for c in range(3)], masks128)
        back_ref[0:32, lanes] = back[0:32] * (0.0625 * keep_low)
        back_ref[32:96, lanes] = back[32:96] * 0.0625
        back_ref[96:128, lanes] = back[96:128] * (0.0625 * keep_high)

    kg_ref[...] = dot_nt(z_ref[...], gg_ref[...])

    sum1 = jnp.zeros((32, 128), F32)
    grads = jnp.zeros((256, 256), F32)
    for early in range(2):
        windows_ref, slopes_ref = ((x_ref, slope_ref), (early_x_ref, early_slope_ref))[early]
        start = 64 * (parity if early else 1 - parity)
        for plane in range(2):
            at = pl.multiple_of(start + plane * 32, 32)
            for t in range(4):
                lanes = slice(t * 256, t * 256 + 256)
                back = back_ref[pl.ds(at, 32), lanes]
                for pos in range(8):
                    grad = back * slopes_ref[plane, pos * 32 : pos * 32 + 32, lanes]
                    g1_ref[pos * 32 : pos * 32 + 32, lanes] = grad.astype(BF16)
                    sum1 = sum1 + grad[:, :128] + grad[:, 128:]
            grads = grads + dot_nt(g1_ref[...], windows_ref[plane * 128 : plane * 128 + 256, :])

    spread = jnp.concatenate([grads[pos * 32 : pos * 32 + 32] for pos in range(8)], axis=1)
    high, low = halves(spread)
    first = dot_nt(jnp.concatenate([high, low], axis=0), sel_ref[...])
    sums = jnp.concatenate([sum1, sum2, jnp.zeros((32, 128), F32)], axis=0)
    biases = dot_nt(jnp.ones((16, 128), BF16), jnp.concatenate(halves(sums), axis=0))[0:8]
    biases = biases[:, :128] + biases[:, 128:]

    low_lanes = iota((288, 128), 1) < 64
    left, right = [], []
    for c in range(3):
        one, two = kg_ref[0:288, c * 128 : c * 128 + 128], kg_ref[96:384, c * 128 : c * 128 + 128]
        left.append(one + pltpu.roll(two, 64, 1))
        right.append(pltpu.roll(one, 64, 1) + two)
    packed_ref[0:288, :] = jnp.where(low_lanes, left[0], right[1]).astype(BF16)
    packed_ref[288:432, :] = jnp.where(low_lanes[0:144], left[2][0:144], right[2][144:288]).astype(BF16)
    first = first[:32] + first[32:]
    for block in range(5):
        rows = first[block * 8 : block * 8 + 8] if block < 4 else biases
        at = PLAIN * 16 + block * 16
        packed_ref[at : at + 16, :] = jnp.concatenate(halves(rows), axis=0)


def halves(rows):
    high = rows.astype(BF16)
    return high, (rows - high.astype(F32)).astype(BF16)


def sum_kernel(in_ref, out_ref):
    total = in_ref[0:CHUNK, :].astype(F32)
    for i in range(1, in_ref.shape[0] // CHUNK):
        total = total + in_ref[CHUNK * i : CHUNK * i + CHUNK, :].astype(F32)
    blocks = []
    for i in range(CHUNK // 16):
        split = lax.axis_index(PLANE) * (CHUNK // 16) + i >= PLAIN
        upper, lower = total[16 * i : 16 * i + 8], total[16 * i + 8 : 16 * i + 16]
        upper = jnp.where(split, upper + lower, upper)
        lower = jnp.where(split, upper - upper.astype(BF16).astype(F32), lower)
        blocks += [upper, lower]
    chunk = jnp.concatenate(blocks, axis=0).astype(BF16)
    for i in range(out_ref.shape[0] // CHUNK):
        out_ref[CHUNK * i : CHUNK * i + CHUNK, :] = chunk


def unpack_kernel(in_ref, deep_in_ref, deep_ref, second_ref, first_ref, bias1_ref, bias2_ref):
    deep_ref[...] = deep_in_ref[...]
    for tap in range(9):
        for c in range(2):
            at = (tap * 3 + c) * 32
            second_ref[at : at + 32, :] = in_ref[tap * 32 : tap * 32 + 32, c * 64 : c * 64 + 64].astype(F32)
        for half in range(2):
            at = (tap * 3 + 2) * 32 + half * 16
            column, row = divmod(tap * 32 + half * 16, 144)
            rows = in_ref[288 + row : 304 + row, column * 64 : column * 64 + 64]
            second_ref[at : at + 16, :] = rows.astype(F32)
    blocks = [in_ref[at : at + 16, :].astype(F32) for at in range(PLAIN * 16, ROWS, 16)]
    rows = [block[0:8] + block[8:16] for block in blocks]
    first = jnp.concatenate(rows[:4], axis=0).T
    for tap in range(27):
        first_ref[tap] = first[4 * tap : 4 * tap + 4, :]
    bias1_ref[...] = rows[4][0:1, 0:32]
    bias2_ref[...] = rows[4][0:1, 32:96]


def call(kernel, outs, inputs, scratch, limit, flops=0, in_hbm=False):
    place = pl.ANY if in_hbm else pltpu.VMEM
    if in_hbm:
        inputs = [pltpu.with_memory_space_constraint(x, pltpu.HBM) for x in inputs]
    return pl.pallas_call(
        kernel,
        out_shape=outs,
        in_specs=[pl.BlockSpec(memory_space=place) for _ in inputs],
        out_specs=[pl.BlockSpec(memory_space=pltpu.VMEM) for _ in outs],
        scratch_shapes=[pltpu.VMEM(*s) if isinstance(s, tuple) else s for s in scratch],
        compiler_params=pltpu.CompilerParams(vmem_limit_bytes=limit * MIB),
        cost_estimate=pl.CostEstimate(flops=flops, bytes_accessed=10**6, transcendentals=0) if flops else None,
    )(*inputs)


def shape(dims, dtype):
    return jax.ShapeDtypeStruct(dims, dtype)


def exchange(rows, axes):
    blocks = rows.reshape(-1, CHUNK, 128)
    return lax.all_to_all(blocks, axes, split_axis=0, concat_axis=0, tiled=True).reshape(-1, 128)


def per_device(volumes, first_kernel, first_bias, second_kernel, second_bias, deep_grad):
    count = lax.axis_size(DEPTH)
    groups = [
        [slab % count * 4 + y for slab in (odd, odd + 1) for y in range(4)] for odd in range(1, count, 2)
    ]
    twice, *prepared = call(
        front_kernel,
        (
            shape((8,) + volumes.shape[1:], BF16),
            shape((256, 256), BF16), shape((384, 384), BF16), shape((384, 384), BF16), shape((32, 128), F32),
            shape((64, 128), F32), shape((256, 64), BF16), shape((128, 2048), BF16), shape((256, 256), BF16),
            shape((128, 512), BF16),
        ),
        (
            volumes, first_kernel.reshape(27, 4, 32), second_kernel.reshape(864, 64), first_bias.reshape(1, 32),
            second_bias.reshape(1, 64), deep_grad.reshape(64, 256).T,
        ),
        (
            ((27, 4, 32), BF16), ((128, 32), F32), ((864, 64), BF16), ((1, 32), F32), ((1, 64), F32),
            pltpu.SemaphoreType.DMA((7,)),
        ),
        8,
        in_hbm=True,
    )
    w1, _, _, bias1, _, _, _, split, _ = prepared
    pair = lax.all_to_all(twice, DEPTH + ("y",), 0, 0, axis_index_groups=groups, tiled=True)
    chip = lax.ppermute(pair, "core", [(0, 1), (1, 0)])
    early = call(
        early_kernel,
        (shape((384, 1024), BF16), shape((2, 256, 1024), F32), shape((192, 1024), BF16)),
        (pair, w1, bias1, split),
        (((768, 128), F32), ((384, 256), F32), ((384, 256), F32), ((2, 32, 1024), F32)),
        8,
        10**9,
    )
    deep, packed = call(
        main_kernel,
        (shape((256, 64), BF16), shape((ROWS, 128), BF16)),
        (pair, chip, *early, *prepared),
        (
            ((512, 128), F32), ((256, 256), F32), ((256, 256), F32), ((384, 1024), BF16),
            ((2, 256, 1024), F32), ((2, 32, 1024), F32), ((384, 1024), BF16), ((2, 64, 1024), F32),
            ((384, 1024), BF16), ((384, 1024), BF16), ((128, 1024), F32), ((64, 1024), F32), ((256, 1024), BF16),
            ((384, 384), F32),
        ),
        20,
        10**9,
    )
    pieces = exchange(packed, PLANE)
    (copies,) = call(sum_kernel, (shape((128, 128), BF16),), (pieces,), (), 2)
    parts = exchange(copies, LINE)
    (copies,) = call(sum_kernel, (shape((ROWS, 128), BF16),), (parts,), (), 2)
    whole = exchange(copies, PLANE)
    deep, second, first, bias1, bias2 = call(
        unpack_kernel,
        (shape((256, 64), BF16), shape((864, 64), F32), shape((27, 4, 32), F32), shape((1, 32), F32), shape((1, 64), F32)),
        (whole, deep),
        (),
        4,
    )
    return (
        deep.T.reshape(1, 64, 1, 8, 32),
        first.reshape(3, 3, 3, 4, 32),
        bias1.reshape(32),
        second.reshape(3, 3, 3, 32, 64),
        bias2.reshape(64),
    )


def solution(mesh):
    split = Mesh(mesh.devices.reshape(-1, 2, 2, *mesh.devices.shape[1:]), DEPTH + ("y", "x_hi"))
    samples = P(("x_hi", "y"), None, DEPTH, None, None)
    in_specs = (P("x_hi", None, DEPTH, "y", None), P(), P(), P(), P(), samples)
    out_specs = (samples, P(), P(), P(), P())
    return jax.shard_map(per_device, mesh=split, in_specs=in_specs, out_specs=out_specs, check_vma=False)
```

```python
import jax
import jax.numpy as jnp
from jax import lax
from jax.experimental import pallas as pl
from jax.experimental.pallas import tpu as pltpu
from jax.sharding import Mesh, PartitionSpec as P

F32 = jnp.float32
BF16 = jnp.bfloat16
DEPTH = ("z", "x_lo", "core")
PLANE = ("x_lo", "core", "y", "x_hi")
LINE = ("z",)
ROWS = 512
CHUNK = 16
PLAIN = 27
MIB = 1024 * 1024
NT = (((1,), (1,)), ((), ()))


def iota(dims, dim):
    return lax.broadcasted_iota(jnp.int32, dims, dim)


def window_cell(shifted, odd):
    return jnp.where(shifted == 1, 3 - 3 * odd, 1 + odd)


def select_taps(pos):
    row = iota((1, 256), 1)
    a = (row >> 7) * 2 + ((row >> 2) & 1) - pos // 4
    b = window_cell((row >> 6) & 1, (row >> 4) & 1) - pos // 2 % 2
    c = window_cell((row >> 5) & 1, (row >> 3) & 1) - pos % 2
    low = jnp.minimum(jnp.minimum(a, b), c)
    high = jnp.maximum(jnp.maximum(a, b), c)
    tap = jnp.where((low >= 0) & (high <= 2), ((a * 3 + b) * 3 + c) * 4 + (row & 3), -1)
    return jnp.where(iota((128, 256), 0) == tap, 1.0, 0.0).astype(BF16)


def split_width():
    col = iota((1, 256), 1)
    at = ((col >> 6) & 1) * 128 + 2 * (col & 63) + (col >> 7)
    return jnp.where(iota((256, 256), 0) == at, 1.0, 0.0).astype(BF16)


def pool_lanes():
    lane = iota((1, 512), 1)
    at = (lane >> 7) * 32 + ((lane & 63) >> 1)
    return jnp.where(iota((128, 512), 0) == at, 0.125, 0.0).astype(BF16)


def half_column(row, size):
    spread = jnp.broadcast_to(0.5 * row, (size, size))
    eye = iota((size, size), 0) == iota((size, size), 1)
    return jnp.broadcast_to(jnp.sum(jnp.where(eye, spread, 0.0), axis=1, keepdims=True), (size, 128))


def dot(a, b):
    return jnp.dot(a, b, preferred_element_type=F32)


def dot_nt(a, b):
    return lax.dot_general(a, b, NT, preferred_element_type=F32)


def dot_tn(a, b):
    return lax.dot_general(a, b, (((0,), (0,)), ((), ())), preferred_element_type=F32)


def front_kernel(
    volumes_hbm, k1_hbm, k2_hbm, b1_hbm, b2_hbm, dg_hbm,
    twice_ref, w1_ref, k2_ref, bias1_ref, bias2_ref, dg_ref, sel_ref, split_ref, pool_ref,
    k1_in, k1_ref, b1_ref, b2_ref, sems,
):
    pairs = (
        (k1_hbm, k1_in), (k2_hbm, k2_ref), (b1_hbm, b1_ref), (b2_hbm, b2_ref), (dg_hbm, dg_ref),
        (volumes_hbm, twice_ref.at[pl.ds(0, 4)]), (volumes_hbm, twice_ref.at[pl.ds(4, 4)]),
    )
    copies = [pltpu.make_async_copy(src, dst, sems.at[n]) for n, (src, dst) in enumerate(pairs)]
    for copy in copies:
        copy.start()
    split_ref[...] = split_width()
    pool_ref[...] = pool_lanes()
    sels = [select_taps(pos) for pos in range(8)]
    for pos in range(8):
        sel_ref[:, pos * 256 : pos * 256 + 256] = sels[pos]
    for copy in copies[:5]:
        copy.wait()
    bias1_ref[...] = half_column(b1_ref[...], 32)
    bias2_ref[...] = half_column(b2_ref[...], 64)
    for tap in range(27):
        k1_ref[4 * tap : 4 * tap + 4, :] = 0.5 * k1_in[tap].astype(F32)
    k1_ref[108:128, :] = jnp.zeros((20, 32), F32)
    k1 = k1_ref[...].astype(BF16)
    for pos in range(8):
        w1_ref[pos * 32 : pos * 32 + 32, :] = dot_tn(k1, sels[pos]).astype(BF16)
    for copy in copies[5:]:
        copy.wait()


def store_second_weights(k2_ref, w2_ref, wb_ref):
    half_eye = jnp.where(iota((64, 64), 0) == iota((64, 64), 1), 0.5, 0.0).astype(BF16)
    none = jnp.zeros((32, 64), BF16)

    def tap(a, b, c):
        at = ((a * 3 + b) * 3 + c) * 32
        return k2_ref[at : at + 32, :] if 0 <= a <= 2 else none

    for c in range(3):
        for plane in range(2):
            stack = [tap(rim - plane, b, c) for rim in range(4) for b in range(3)]
            at = (c * 2 + plane) * 64
            w2_ref[at : at + 64, :] = dot_nt(half_eye, jnp.concatenate(stack, axis=0)).astype(BF16)
        for rim in range(4):
            row = [tap(rim - plane, 2 - b, 2 - c).astype(F32) for plane in range(2) for b in range(3)]
            at = (c * 4 + rim) * 32
            wb_ref[at : at + 32, :] = jnp.concatenate(row, axis=1).astype(BF16)


def lane_masks(rows):
    lane = iota((rows, 128), 1)
    cell = lane % 64
    return lane < 64, cell != 0, cell != 63


def width_shift(tiles, step, masks):
    _, not_first, not_last = masks
    if step < 0:
        return [jnp.where(not_first, pltpu.roll(t, 1, 1), 0.0) for t in tiles]
    return [jnp.where(not_last, pltpu.roll(t, 127, 1), 0.0) for t in tiles]


def height_shift(tiles, steps, masks):
    low = masks[0]
    swapped = [pltpu.roll(t, 64, 1) for t in tiles]
    zero = jnp.zeros_like(tiles[0])
    out = []
    for step in steps:
        if step < 0:
            before = [zero] + swapped[:-1]
            out.append([jnp.where(low, before[i], swapped[i]) for i in range(len(tiles))])
        else:
            after = swapped[1:] + [zero]
            out.append([jnp.where(low, swapped[i], after[i]) for i in range(len(tiles))])
    return out


def store_height_shifts(ref, put, masks):
    tiles = [ref[:, t * 128 : t * 128 + 128] for t in range(8)]
    before, after = height_shift(tiles, (-1, 1), masks)
    for b, group in enumerate((before, tiles, after)):
        for t in range(8):
            put(b, t, group[t].astype(BF16))


def add_width_shifts(parts, masks):
    sides = []
    for half in range(2):
        one, two, three = (part[:, half * 128 : half * 128 + 128] for part in parts)
        sides.append(two + width_shift([one], -1, masks)[0] + width_shift([three], 1, masks)[0])
    return jnp.concatenate(sides, axis=1)


def grid_ends():
    place = lax.axis_index(DEPTH)
    keep_low = jnp.where(place > 0, 1.0, 0.0).astype(F32)
    keep_high = jnp.where(place < lax.axis_size(DEPTH) - 1, 1.0, 0.0).astype(F32)
    return place % 2, keep_low, keep_high


def fill(f_ref, ref, cell, at, keep=None):
    for y in range(4):
        for ch in range(4):
            part = ref[cell // 4 * 4 + y, ch, cell % 4].astype(F32)
            f_ref[pl.ds((at * 4 + ch) * 32 + y * 8, 8), :] = part if keep is None else part * keep


def split_rows(f_ref, l_ref, g_ref, split_ref, rows):
    for hb in range(2):
        for qq in range(8):
            for low in range(2):
                l_ref[pl.ds((hb * 8 + qq) * rows, rows), low * 128 : low * 128 + 128] = f_ref[
                    pl.ds(4 * qq + 2 * low + hb, rows, stride=32), :
                ]
    g_ref[...] = dot(l_ref[...].astype(BF16), split_ref[...])


def store_windows(g_ref, rows, pair, put):
    masks = lane_masks(8)
    for hb in range(2):
        still, moved = [], []
        for wb in range(2):
            starts = [(hb * 8 + qq) * rows + pair * 8 for qq in range(8)]
            tiles = [g_ref[at : at + 8, wb * 128 : wb * 128 + 128] for at in starts]
            still.append(tiles)
            moved.append(width_shift(tiles, 1 if wb == 0 else -1, masks))
        for ws, group in enumerate((still, moved)):
            step = 1 if hb == 0 else -1
            raised = [height_shift(group[wb], (step,), masks)[0] for wb in range(2)]
            for hs, part in enumerate((group, raised)):
                for qq in range(8):
                    both = jnp.concatenate([part[0][qq], part[1][qq]], axis=0)
                    put((hs * 2 + ws) * 32 + hb * 16, qq, both.astype(BF16))


def first_conv(x_ref, w1_ref, b1_ref, slope_ref, y_ref, scales):
    bias = jnp.concatenate([b1_ref[...], b1_ref[...]], axis=1)
    for plane in range(2):
        for t in range(4):
            lanes = slice(t * 256, t * 256 + 256)
            pre = dot(w1_ref[...], x_ref[plane * 128 : plane * 128 + 256, lanes])
            total = jnp.zeros((32, 256), F32)
            for pos in range(8):
                u = pre[pos * 32 : pos * 32 + 32] + bias
                tanh = jnp.tanh(u)
                w = 1.0 + tanh
                silu = u * w
                slope_ref[plane, pos * 32 : pos * 32 + 32, lanes] = w + silu * (1.0 - tanh)
                total = total + silu
            y_ref[plane, :, lanes] = total * scales[plane]


def store_second_windows(y_ref, put):
    masks = lane_masks(32)
    for plane in range(2):
        store_height_shifts(y_ref.at[plane], lambda b, t, value, plane=plane: put(plane * 96 + b * 32, t, value), masks)


def early_kernel(
    pair_ref, w1_ref, k2_ref, b1_ref, split_ref,
    x_ref, slope_ref, z_ref, w2_ref, wb_ref, f_ref, l_ref, g_ref, y_ref,
):
    _, keep_low, keep_high = grid_ends()
    store_second_weights(k2_ref, w2_ref, wb_ref)
    for cell in range(1, 7):
        fill(f_ref, pair_ref, cell, cell - 1, keep_low if cell < 4 else keep_high)
    split_rows(f_ref, l_ref, g_ref, split_ref, 24)
    for pair in range(3):

        def put(row, t, value, pair=pair):
            x_ref[pair * 128 + row : pair * 128 + row + 16, t * 128 : t * 128 + 128] = value

        store_windows(g_ref, 24, pair, put)
    first_conv(x_ref, w1_ref, b1_ref, slope_ref, y_ref, (0.125 * keep_low, 0.125 * keep_high))

    def put_second(row, t, value):
        z_ref[row : row + 32, t * 128 : t * 128 + 128] = value

    store_second_windows(y_ref, put_second)


def main_kernel(
    pair_ref, chip_ref, early_x_ref, early_slope_ref, early_z_ref, w2_ref, wb_ref,
    w1_ref, b1_ref, b2_ref, dg_ref, sel_ref, split_ref, pool_ref,
    deep_ref, packed_ref,
    f_ref, l_ref, g_ref, x_ref, slope_ref, y_ref, z_ref, g2_ref, gg_ref, gz_ref, back_ref, ds_ref, g1_ref, kg_ref,
):
    parity, keep_low, keep_high = grid_ends()

    @pl.when(parity == 0)
    def _():
        fill(f_ref, pair_ref, 7, 0)
        for cell in range(3):
            fill(f_ref, chip_ref, cell, 1 + cell)

    @pl.when(parity == 1)
    def _():
        for cell in range(3):
            fill(f_ref, chip_ref, 5 + cell, cell)
        fill(f_ref, pair_ref, 0, 3)

    split_rows(f_ref, l_ref, g_ref, split_ref, 16)
    fresh = pl.multiple_of(128 * (1 - parity), 128)
    shared = pl.multiple_of(256 * parity, 128)
    x_ref[pl.ds(shared, 128), :] = early_x_ref[pl.ds(pl.multiple_of(256 * (1 - parity), 128), 128), :]
    for pair in range(2):

        def put(row, t, value, pair=pair):
            x_ref[pl.ds(pl.multiple_of(fresh + (pair * 128 + row), 16), 16), t * 128 : t * 128 + 128] = value

        store_windows(g_ref, 16, pair, put)
    first_conv(x_ref, w1_ref, b1_ref, slope_ref, y_ref, (0.125, 0.125))

    early_at = pl.multiple_of(192 * parity, 16)
    late_at = pl.multiple_of(192 * (1 - parity), 16)
    z_ref[pl.ds(early_at, 192), :] = early_z_ref[...]

    def put_second(row, t, value):
        z_ref[pl.ds(pl.multiple_of(late_at + row, 16), 32), t * 128 : t * 128 + 128] = value

    store_second_windows(y_ref, put_second)

    bias2 = jnp.concatenate([b2_ref[...], b2_ref[...]], axis=1)
    sum2 = jnp.zeros((64, 128), F32)
    masks64, masks128 = lane_masks(64), lane_masks(128)
    for half in range(2):
        wide = dot_tn(dg_ref[half * 128 : half * 128 + 128, :], pool_ref[...])
        g2_ref[0, :, half * 512 : half * 512 + 512] = wide
    for t in range(4):
        lanes = slice(t * 256, t * 256 + 256)
        taps = dot(w2_ref[...], z_ref[:, lanes])
        pre = add_width_shifts([taps[c * 128 : c * 128 + 128] for c in range(3)], masks128)
        given = 0.5 * g2_ref[0, :, lanes]
        total = jnp.zeros((64, 256), F32)
        for plane in range(2):
            u = pre[plane * 64 : plane * 64 + 64] + bias2
            tanh = jnp.tanh(u)
            w = 1.0 + tanh
            silu = u * w
            total = total + silu
            grad = given * (w + silu * (1.0 - tanh))
            g2_ref[plane, :, lanes] = grad
            for half in range(2):
                tile = grad[:, half * 128 : half * 128 + 128]
                at = t * 256 + half * 128
                for c, part in enumerate((width_shift([tile], 1, masks64), [tile], width_shift([tile], -1, masks64))):
                    row = c * 128 + plane * 64
                    gg_ref[row : row + 64, at : at + 128] = part[0].astype(BF16)
            sum2 = sum2 + grad[:, :128] + grad[:, 128:]
        ds_ref[:, lanes] = total

    for half in range(2):
        part = ds_ref[:, half * 512 : half * 512 + 512]
        high, low = halves(part)
        deep = dot_nt(pool_ref[...], jnp.concatenate([high, low], axis=0))
        deep_ref[half * 128 : half * 128 + 128, :] = (deep[:, :64] + deep[:, 64:]).astype(BF16)

    for plane in range(2):

        def put(b, t, value, plane=plane):
            row = plane * 192 + b * 64
            gz_ref[row : row + 64, t * 128 : t * 128 + 128] = value

        store_height_shifts(g2_ref.at[plane], put, masks64)
    for t in range(4):
        lanes = slice(t * 256, t * 256 + 256)
        taps = dot(wb_ref[...], gz_ref[:, lanes])
        back = add_width_shifts([taps[c * 128 : c * 128 + 128] for c in range(3)], masks128)
        back_ref[0:32, lanes] = back[0:32] * (0.0625 * keep_low)
        back_ref[32:96, lanes] = back[32:96] * 0.0625
        back_ref[96:128, lanes] = back[96:128] * (0.0625 * keep_high)

    kg_ref[...] = dot_nt(z_ref[...], gg_ref[...])

    sum1 = jnp.zeros((32, 128), F32)
    grads = jnp.zeros((256, 256), F32)
    for early in range(2):
        windows_ref, slopes_ref = ((x_ref, slope_ref), (early_x_ref, early_slope_ref))[early]
        start = 64 * (parity if early else 1 - parity)
        for plane in range(2):
            at = pl.multiple_of(start + plane * 32, 32)
            for t in range(4):
                lanes = slice(t * 256, t * 256 + 256)
                back = back_ref[pl.ds(at, 32), lanes]
                for pos in range(8):
                    grad = back * slopes_ref[plane, pos * 32 : pos * 32 + 32, lanes]
                    g1_ref[pos * 32 : pos * 32 + 32, lanes] = grad.astype(BF16)
                    sum1 = sum1 + grad[:, :128] + grad[:, 128:]
            grads = grads + dot_nt(g1_ref[...], windows_ref[plane * 128 : plane * 128 + 256, :])

    spread = jnp.concatenate([grads[pos * 32 : pos * 32 + 32] for pos in range(8)], axis=1)
    high, low = halves(spread)
    first = dot_nt(jnp.concatenate([high, low], axis=0), sel_ref[...])
    sums = jnp.concatenate([sum1, sum2, jnp.zeros((32, 128), F32)], axis=0)
    biases = dot_nt(jnp.ones((16, 128), BF16), jnp.concatenate(halves(sums), axis=0))[0:8]
    biases = biases[:, :128] + biases[:, 128:]

    low_lanes = iota((288, 128), 1) < 64
    left, right = [], []
    for c in range(3):
        one, two = kg_ref[0:288, c * 128 : c * 128 + 128], kg_ref[96:384, c * 128 : c * 128 + 128]
        left.append(one + pltpu.roll(two, 64, 1))
        right.append(pltpu.roll(one, 64, 1) + two)
    packed_ref[0:288, :] = jnp.where(low_lanes, left[0], right[1]).astype(BF16)
    packed_ref[288:432, :] = jnp.where(low_lanes[0:144], left[2][0:144], right[2][144:288]).astype(BF16)
    first = first[:32] + first[32:]
    for block in range(5):
        rows = first[block * 8 : block * 8 + 8] if block < 4 else biases
        at = PLAIN * 16 + block * 16
        packed_ref[at : at + 16, :] = jnp.concatenate(halves(rows), axis=0)


def halves(rows):
    high = rows.astype(BF16)
    return high, (rows - high.astype(F32)).astype(BF16)


def sum_kernel(in_ref, out_ref):
    total = in_ref[0:CHUNK, :].astype(F32)
    for i in range(1, in_ref.shape[0] // CHUNK):
        total = total + in_ref[CHUNK * i : CHUNK * i + CHUNK, :].astype(F32)
    blocks = []
    for i in range(CHUNK // 16):
        split = lax.axis_index(PLANE) * (CHUNK // 16) + i >= PLAIN
        upper, lower = total[16 * i : 16 * i + 8], total[16 * i + 8 : 16 * i + 16]
        upper = jnp.where(split, upper + lower, upper)
        lower = jnp.where(split, upper - upper.astype(BF16).astype(F32), lower)
        blocks += [upper, lower]
    chunk = jnp.concatenate(blocks, axis=0).astype(BF16)
    for i in range(out_ref.shape[0] // CHUNK):
        out_ref[CHUNK * i : CHUNK * i + CHUNK, :] = chunk


def unpack_kernel(in_ref, deep_in_ref, deep_ref, second_ref, first_ref, bias1_ref, bias2_ref):
    deep_ref[...] = deep_in_ref[...]
    for tap in range(9):
        for c in range(2):
            at = (tap * 3 + c) * 32
            second_ref[at : at + 32, :] = in_ref[tap * 32 : tap * 32 + 32, c * 64 : c * 64 + 64].astype(F32)
        for half in range(2):
            at = (tap * 3 + 2) * 32 + half * 16
            column, row = divmod(tap * 32 + half * 16, 144)
            rows = in_ref[288 + row : 304 + row, column * 64 : column * 64 + 64]
            second_ref[at : at + 16, :] = rows.astype(F32)
    blocks = [in_ref[at : at + 16, :].astype(F32) for at in range(PLAIN * 16, ROWS, 16)]
    rows = [block[0:8] + block[8:16] for block in blocks]
    first = jnp.concatenate(rows[:4], axis=0).T
    for tap in range(27):
        first_ref[tap] = first[4 * tap : 4 * tap + 4, :]
    bias1_ref[...] = rows[4][0:1, 0:32]
    bias2_ref[...] = rows[4][0:1, 32:96]


def call(kernel, outs, inputs, scratch, limit, flops=0, in_hbm=False):
    place = pl.ANY if in_hbm else pltpu.VMEM
    if in_hbm:
        inputs = [pltpu.with_memory_space_constraint(x, pltpu.HBM) for x in inputs]
    return pl.pallas_call(
        kernel,
        out_shape=outs,
        in_specs=[pl.BlockSpec(memory_space=place) for _ in inputs],
        out_specs=[pl.BlockSpec(memory_space=pltpu.VMEM) for _ in outs],
        scratch_shapes=[pltpu.VMEM(*s) if isinstance(s, tuple) else s for s in scratch],
        compiler_params=pltpu.CompilerParams(vmem_limit_bytes=limit * MIB),
        cost_estimate=pl.CostEstimate(flops=flops, bytes_accessed=10**6, transcendentals=0) if flops else None,
    )(*inputs)


def shape(dims, dtype):
    return jax.ShapeDtypeStruct(dims, dtype)


def exchange(rows, axes):
    blocks = rows.reshape(-1, CHUNK, 128)
    return lax.all_to_all(blocks, axes, split_axis=0, concat_axis=0, tiled=True).reshape(-1, 128)


def per_device(volumes, first_kernel, first_bias, second_kernel, second_bias, deep_grad):
    count = lax.axis_size(DEPTH)
    groups = [
        [slab % count * 4 + y for slab in (odd, odd + 1) for y in range(4)] for odd in range(1, count, 2)
    ]
    twice, *prepared = call(
        front_kernel,
        (
            shape((8,) + volumes.shape[1:], BF16),
            shape((256, 256), BF16), shape((864, 64), BF16), shape((32, 128), F32), shape((64, 128), F32), shape((256, 64), BF16), shape((128, 2048), BF16), shape((256, 256), BF16),
            shape((128, 512), BF16),
        ),
        (
            volumes, first_kernel.reshape(27, 4, 32), second_kernel.reshape(864, 64), first_bias.reshape(1, 32),
            second_bias.reshape(1, 64), deep_grad.reshape(64, 256).T,
        ),
        (
            ((27, 4, 32), BF16), ((128, 32), F32), ((1, 32), F32), ((1, 64), F32),
            pltpu.SemaphoreType.DMA((7,)),
        ),
        8,
        in_hbm=True,
    )
    w1, k2, bias1, bias2, dg, sel, split, pool = prepared
    pair = lax.all_to_all(twice, DEPTH + ("y",), 0, 0, axis_index_groups=groups, tiled=True)
    chip = lax.ppermute(pair, "core", [(0, 1), (1, 0)])
    early = call(
        early_kernel,
        (shape((384, 1024), BF16), shape((2, 256, 1024), F32), shape((192, 1024), BF16), shape((384, 384), BF16), shape((384, 384), BF16)),
        (pair, w1, k2, bias1, split),
        (((768, 128), F32), ((384, 256), F32), ((384, 256), F32), ((2, 32, 1024), F32)),
        8,
        10**9,
    )
    deep, packed = call(
        main_kernel,
        (shape((256, 64), BF16), shape((ROWS, 128), BF16)),
        (pair, chip, *early, w1, bias1, bias2, dg, sel, split, pool),
        (
            ((512, 128), F32), ((256, 256), F32), ((256, 256), F32), ((384, 1024), BF16),
            ((2, 256, 1024), F32), ((2, 32, 1024), F32), ((384, 1024), BF16), ((2, 64, 1024), F32),
            ((384, 1024), BF16), ((384, 1024), BF16), ((128, 1024), F32), ((64, 1024), F32), ((256, 1024), BF16),
            ((384, 384), F32),
        ),
        20,
        10**9,
    )
    pieces = exchange(packed, PLANE)
    (copies,) = call(sum_kernel, (shape((128, 128), BF16),), (pieces,), (), 2)
    parts = exchange(copies, LINE)
    (copies,) = call(sum_kernel, (shape((ROWS, 128), BF16),), (parts,), (), 2)
    whole = exchange(copies, PLANE)
    deep, second, first, bias1, bias2 = call(
        unpack_kernel,
        (shape((256, 64), BF16), shape((864, 64), F32), shape((27, 4, 32), F32), shape((1, 32), F32), shape((1, 64), F32)),
        (whole, deep),
        (),
        4,
    )
    return (
        deep.T.reshape(1, 64, 1, 8, 32),
        first.reshape(3, 3, 3, 4, 32),
        bias1.reshape(32),
        second.reshape(3, 3, 3, 32, 64),
        bias2.reshape(64),
    )


def solution(mesh):
    split = Mesh(mesh.devices.reshape(-1, 2, 2, *mesh.devices.shape[1:]), DEPTH + ("y", "x_hi"))
    samples = P(("x_hi", "y"), None, DEPTH, None, None)
    in_specs = (P("x_hi", None, DEPTH, "y", None), P(), P(), P(), P(), samples)
    out_specs = (samples, P(), P(), P(), P())
    return jax.shard_map(per_device, mesh=split, in_specs=in_specs, out_specs=out_specs, check_vma=False)
```

```python
import jax
import jax.numpy as jnp
from jax import lax
from jax.experimental import pallas as pl
from jax.experimental.pallas import tpu as pltpu
from jax.sharding import Mesh, PartitionSpec as P

F32 = jnp.float32
BF16 = jnp.bfloat16
DEPTH = ("z", "x_lo", "core")
PLANE = ("x_lo", "core", "y", "x_hi")
LINE = ("z",)
ROWS = 512
CHUNK = 16
PLAIN = 27
MIB = 1024 * 1024
NT = (((1,), (1,)), ((), ()))


def iota(dims, dim):
    return lax.broadcasted_iota(jnp.int32, dims, dim)


def window_cell(shifted, odd):
    return jnp.where(shifted == 1, 3 - 3 * odd, 1 + odd)


def select_taps(pos):
    row = iota((1, 256), 1)
    a = (row >> 7) * 2 + ((row >> 2) & 1) - pos // 4
    b = window_cell((row >> 6) & 1, (row >> 4) & 1) - pos // 2 % 2
    c = window_cell((row >> 5) & 1, (row >> 3) & 1) - pos % 2
    low = jnp.minimum(jnp.minimum(a, b), c)
    high = jnp.maximum(jnp.maximum(a, b), c)
    tap = jnp.where((low >= 0) & (high <= 2), ((a * 3 + b) * 3 + c) * 4 + (row & 3), -1)
    return jnp.where(iota((128, 256), 0) == tap, 1.0, 0.0).astype(BF16)


def split_width():
    col = iota((1, 256), 1)
    at = ((col >> 6) & 1) * 128 + 2 * (col & 63) + (col >> 7)
    return jnp.where(iota((256, 256), 0) == at, 1.0, 0.0).astype(BF16)


def pool_lanes():
    lane = iota((1, 512), 1)
    at = (lane >> 7) * 32 + ((lane & 63) >> 1)
    return jnp.where(iota((128, 512), 0) == at, 0.125, 0.0).astype(BF16)


def half_column(row, size):
    spread = jnp.broadcast_to(0.5 * row, (size, size))
    eye = iota((size, size), 0) == iota((size, size), 1)
    return jnp.broadcast_to(jnp.sum(jnp.where(eye, spread, 0.0), axis=1, keepdims=True), (size, 128))


def dot(a, b):
    return jnp.dot(a, b, preferred_element_type=F32)


def dot_nt(a, b):
    return lax.dot_general(a, b, NT, preferred_element_type=F32)


def dot_tn(a, b):
    return lax.dot_general(a, b, (((0,), (0,)), ((), ())), preferred_element_type=F32)


def front_kernel(
    volumes_hbm, k1_hbm, k2_hbm, b1_hbm, b2_hbm, dg_hbm,
    twice_ref, w1_ref, k2_ref, bias1_ref, bias2_ref, dg_ref, sel_ref, split_ref, pool_ref,
    k1_in, k1_ref, b1_ref, b2_ref, sems,
):
    pairs = (
        (k1_hbm, k1_in), (k2_hbm, k2_ref), (b1_hbm, b1_ref), (b2_hbm, b2_ref), (dg_hbm, dg_ref),
        (volumes_hbm, twice_ref.at[pl.ds(0, 4)]), (volumes_hbm, twice_ref.at[pl.ds(4, 4)]),
    )
    copies = [pltpu.make_async_copy(src, dst, sems.at[n]) for n, (src, dst) in enumerate(pairs)]
    for copy in copies:
        copy.start()
    split_ref[...] = split_width()
    pool_ref[...] = pool_lanes()
    sels = [select_taps(pos) for pos in range(8)]
    for pos in range(8):
        sel_ref[:, pos * 256 : pos * 256 + 256] = sels[pos]
    for copy in copies[:5]:
        copy.wait()
    bias1_ref[...] = half_column(b1_ref[...], 32)
    bias2_ref[...] = half_column(b2_ref[...], 64)
    for tap in range(27):
        k1_ref[4 * tap : 4 * tap + 4, :] = 0.5 * k1_in[tap].astype(F32)
    k1_ref[108:128, :] = jnp.zeros((20, 32), F32)
    k1 = k1_ref[...].astype(BF16)
    for pos in range(8):
        w1_ref[pos * 32 : pos * 32 + 32, :] = dot_tn(k1, sels[pos]).astype(BF16)
    for copy in copies[5:]:
        copy.wait()


def store_second_weights(k2_ref, w2_ref, wb_ref):
    half_eye = jnp.where(iota((64, 64), 0) == iota((64, 64), 1), 0.5, 0.0).astype(BF16)
    none = jnp.zeros((32, 64), BF16)

    def tap(a, b, c):
        at = ((a * 3 + b) * 3 + c) * 32
        return k2_ref[at : at + 32, :] if 0 <= a <= 2 else none

    for c in range(3):
        for plane in range(2):
            at = (c * 2 + plane) * 64
            for half in range(2):
                stack = [tap(rim - plane, b, c) for rim in (2 * half, 2 * half + 1) for b in range(3)]
                w2_ref[half, at : at + 64, :] = dot_nt(half_eye, jnp.concatenate(stack, axis=0)).astype(BF16)
        for rim in range(4):
            row = [tap(rim - plane, 2 - b, 2 - c).astype(F32) for plane in range(2) for b in range(3)]
            at = (c * 4 + rim) * 32
            wb_ref[at : at + 32, :] = jnp.concatenate(row, axis=1).astype(BF16)


def lane_masks(rows):
    lane = iota((rows, 128), 1)
    cell = lane % 64
    return lane < 64, cell != 0, cell != 63


def width_shift(tiles, step, masks):
    _, not_first, not_last = masks
    if step < 0:
        return [jnp.where(not_first, pltpu.roll(t, 1, 1), 0.0) for t in tiles]
    return [jnp.where(not_last, pltpu.roll(t, 127, 1), 0.0) for t in tiles]


def height_shift(tiles, steps, masks):
    low = masks[0]
    swapped = [pltpu.roll(t, 64, 1) for t in tiles]
    zero = jnp.zeros_like(tiles[0])
    out = []
    for step in steps:
        if step < 0:
            before = [zero] + swapped[:-1]
            out.append([jnp.where(low, before[i], swapped[i]) for i in range(len(tiles))])
        else:
            after = swapped[1:] + [zero]
            out.append([jnp.where(low, swapped[i], after[i]) for i in range(len(tiles))])
    return out


def store_height_shifts(ref, put, masks):
    tiles = [ref[:, t * 128 : t * 128 + 128] for t in range(8)]
    before, after = height_shift(tiles, (-1, 1), masks)
    for b, group in enumerate((before, tiles, after)):
        for t in range(8):
            put(b, t, group[t].astype(BF16))


def add_width_shifts(parts, masks):
    sides = []
    for half in range(2):
        one, two, three = (part[:, half * 128 : half * 128 + 128] for part in parts)
        sides.append(two + width_shift([one], -1, masks)[0] + width_shift([three], 1, masks)[0])
    return jnp.concatenate(sides, axis=1)


def grid_ends():
    place = lax.axis_index(DEPTH)
    keep_low = jnp.where(place > 0, 1.0, 0.0).astype(F32)
    keep_high = jnp.where(place < lax.axis_size(DEPTH) - 1, 1.0, 0.0).astype(F32)
    return place % 2, keep_low, keep_high


def fill(f_ref, ref, cell, at, keep=None):
    for y in range(4):
        for ch in range(4):
            part = ref[cell // 4 * 4 + y, ch, cell % 4].astype(F32)
            f_ref[pl.ds((at * 4 + ch) * 32 + y * 8, 8), :] = part if keep is None else part * keep


def split_rows(f_ref, l_ref, g_ref, split_ref, rows):
    for hb in range(2):
        for qq in range(8):
            for low in range(2):
                l_ref[pl.ds((hb * 8 + qq) * rows, rows), low * 128 : low * 128 + 128] = f_ref[
                    pl.ds(4 * qq + 2 * low + hb, rows, stride=32), :
                ]
    g_ref[...] = dot(l_ref[...].astype(BF16), split_ref[...])


def store_windows(g_ref, rows, pair, put):
    masks = lane_masks(8)
    for hb in range(2):
        still, moved = [], []
        for wb in range(2):
            starts = [(hb * 8 + qq) * rows + pair * 8 for qq in range(8)]
            tiles = [g_ref[at : at + 8, wb * 128 : wb * 128 + 128] for at in starts]
            still.append(tiles)
            moved.append(width_shift(tiles, 1 if wb == 0 else -1, masks))
        for ws, group in enumerate((still, moved)):
            step = 1 if hb == 0 else -1
            raised = [height_shift(group[wb], (step,), masks)[0] for wb in range(2)]
            for hs, part in enumerate((group, raised)):
                for qq in range(8):
                    both = jnp.concatenate([part[0][qq], part[1][qq]], axis=0)
                    put((hs * 2 + ws) * 32 + hb * 16, qq, both.astype(BF16))


def first_conv(x_ref, w1_ref, b1_ref, slope_ref, y_ref, scales):
    bias = jnp.concatenate([b1_ref[...], b1_ref[...]], axis=1)
    for plane in range(2):
        for t in range(4):
            lanes = slice(t * 256, t * 256 + 256)
            pre = dot(w1_ref[...], x_ref[plane * 128 : plane * 128 + 256, lanes])
            total = jnp.zeros((32, 256), F32)
            for pos in range(8):
                u = pre[pos * 32 : pos * 32 + 32] + bias
                tanh = jnp.tanh(u)
                w = 1.0 + tanh
                silu = u * w
                slope_ref[plane, pos * 32 : pos * 32 + 32, lanes] = w + silu * (1.0 - tanh)
                total = total + silu
            y_ref[plane, :, lanes] = total * scales[plane]


def store_second_windows(y_ref, put):
    masks = lane_masks(32)
    for plane in range(2):
        store_height_shifts(y_ref.at[plane], lambda b, t, value, plane=plane: put(plane * 96 + b * 32, t, value), masks)


def early_kernel(
    pair_ref, w1_ref, k2_ref, b1_ref, split_ref,
    x_ref, slope_ref, z_ref, w2_ref, wb_ref, f_ref, l_ref, g_ref, y_ref,
):
    _, keep_low, keep_high = grid_ends()
    store_second_weights(k2_ref, w2_ref, wb_ref)
    for cell in range(1, 7):
        fill(f_ref, pair_ref, cell, cell - 1, keep_low if cell < 4 else keep_high)
    split_rows(f_ref, l_ref, g_ref, split_ref, 24)
    for pair in range(3):

        def put(row, t, value, pair=pair):
            x_ref[pair * 128 + row : pair * 128 + row + 16, t * 128 : t * 128 + 128] = value

        store_windows(g_ref, 24, pair, put)
    first_conv(x_ref, w1_ref, b1_ref, slope_ref, y_ref, (0.125 * keep_low, 0.125 * keep_high))

    def put_second(row, t, value):
        z_ref[row : row + 32, t * 128 : t * 128 + 128] = value

    store_second_windows(y_ref, put_second)


def main_kernel(
    pair_ref, chip_ref, early_x_ref, early_slope_ref, early_z_ref, w2_ref, wb_ref,
    w1_ref, b1_ref, b2_ref, dg_ref, sel_ref, split_ref, pool_ref,
    deep_ref, packed_ref,
    f_ref, l_ref, g_ref, x_ref, slope_ref, y_ref, z_ref, g2_ref, gg_ref, gz_ref, back_ref, ds_ref, g1_ref, kg_ref, taps_ref,
):
    parity, keep_low, keep_high = grid_ends()

    for t in range(4):
        lanes = slice(t * 256, t * 256 + 256)
        taps_ref[:, lanes] = dot(w2_ref[parity], early_z_ref[:, lanes])

    for plane in range(4):
        for y in range(4):
            for ch in range(4):
                if plane in (1, 2):
                    part = chip_ref[4 * parity + y, ch, plane - 1 + 2 * parity].astype(F32)
                else:
                    own = pair_ref[4 * (1 - parity) + y, ch, 3 * (1 - parity)].astype(F32)
                    rim = chip_ref[4 * parity + y, ch, 1 if plane == 0 else 2].astype(F32)
                    part = jnp.where(parity == (0 if plane == 0 else 1), own, rim)
                f_ref[pl.ds((plane * 4 + ch) * 32 + y * 8, 8), :] = part

    split_rows(f_ref, l_ref, g_ref, split_ref, 16)
    fresh = pl.multiple_of(128 * (1 - parity), 128)
    shared = pl.multiple_of(256 * parity, 128)
    x_ref[pl.ds(shared, 128), :] = early_x_ref[pl.ds(pl.multiple_of(256 * (1 - parity), 128), 128), :]
    for pair in range(2):

        def put(row, t, value, pair=pair):
            x_ref[pl.ds(pl.multiple_of(fresh + (pair * 128 + row), 16), 16), t * 128 : t * 128 + 128] = value

        store_windows(g_ref, 16, pair, put)
    first_conv(x_ref, w1_ref, b1_ref, slope_ref, y_ref, (0.125, 0.125))

    early_at = pl.multiple_of(192 * parity, 16)
    late_at = pl.multiple_of(192 * (1 - parity), 16)
    z_ref[pl.ds(early_at, 192), :] = early_z_ref[...]

    def put_second(row, t, value):
        z_ref[pl.ds(pl.multiple_of(late_at + row, 16), 32), t * 128 : t * 128 + 128] = value

    store_second_windows(y_ref, put_second)

    bias2 = jnp.concatenate([b2_ref[...], b2_ref[...]], axis=1)
    sum2 = jnp.zeros((64, 128), F32)
    masks64, masks128 = lane_masks(64), lane_masks(128)
    for half in range(2):
        wide = dot_tn(dg_ref[half * 128 : half * 128 + 128, :], pool_ref[...])
        g2_ref[0, :, half * 512 : half * 512 + 512] = wide
    for t in range(4):
        lanes = slice(t * 256, t * 256 + 256)
        taps = taps_ref[:, lanes] + dot(w2_ref[1 - parity], z_ref[pl.ds(late_at, 192), lanes])
        pre = add_width_shifts([taps[c * 128 : c * 128 + 128] for c in range(3)], masks128)
        given = 0.5 * g2_ref[0, :, lanes]
        total = jnp.zeros((64, 256), F32)
        for plane in range(2):
            u = pre[plane * 64 : plane * 64 + 64] + bias2
            tanh = jnp.tanh(u)
            w = 1.0 + tanh
            silu = u * w
            total = total + silu
            grad = given * (w + silu * (1.0 - tanh))
            g2_ref[plane, :, lanes] = grad
            for half in range(2):
                tile = grad[:, half * 128 : half * 128 + 128]
                at = t * 256 + half * 128
                for c, part in enumerate((width_shift([tile], 1, masks64), [tile], width_shift([tile], -1, masks64))):
                    row = c * 128 + plane * 64
                    gg_ref[row : row + 64, at : at + 128] = part[0].astype(BF16)
            sum2 = sum2 + grad[:, :128] + grad[:, 128:]
        ds_ref[:, lanes] = total

    for half in range(2):
        part = ds_ref[:, half * 512 : half * 512 + 512]
        high, low = halves(part)
        deep = dot_nt(pool_ref[...], jnp.concatenate([high, low], axis=0))
        deep_ref[half * 128 : half * 128 + 128, :] = (deep[:, :64] + deep[:, 64:]).astype(BF16)

    for plane in range(2):

        def put(b, t, value, plane=plane):
            row = plane * 192 + b * 64
            gz_ref[row : row + 64, t * 128 : t * 128 + 128] = value

        store_height_shifts(g2_ref.at[plane], put, masks64)
    for t in range(4):
        lanes = slice(t * 256, t * 256 + 256)
        taps = dot(wb_ref[...], gz_ref[:, lanes])
        back = add_width_shifts([taps[c * 128 : c * 128 + 128] for c in range(3)], masks128)
        back_ref[0:32, lanes] = back[0:32] * (0.0625 * keep_low)
        back_ref[32:96, lanes] = back[32:96] * 0.0625
        back_ref[96:128, lanes] = back[96:128] * (0.0625 * keep_high)

    kg_ref[...] = dot_nt(z_ref[...], gg_ref[...])

    sum1 = jnp.zeros((32, 128), F32)
    grads = jnp.zeros((256, 256), F32)
    for early in range(2):
        windows_ref, slopes_ref = ((x_ref, slope_ref), (early_x_ref, early_slope_ref))[early]
        start = 64 * (parity if early else 1 - parity)
        for plane in range(2):
            at = pl.multiple_of(start + plane * 32, 32)
            for t in range(4):
                lanes = slice(t * 256, t * 256 + 256)
                back = back_ref[pl.ds(at, 32), lanes]
                for pos in range(8):
                    grad = back * slopes_ref[plane, pos * 32 : pos * 32 + 32, lanes]
                    g1_ref[pos * 32 : pos * 32 + 32, lanes] = grad.astype(BF16)
                    sum1 = sum1 + grad[:, :128] + grad[:, 128:]
            grads = grads + dot_nt(g1_ref[...], windows_ref[plane * 128 : plane * 128 + 256, :])

    spread = jnp.concatenate([grads[pos * 32 : pos * 32 + 32] for pos in range(8)], axis=1)
    high, low = halves(spread)
    first = dot_nt(jnp.concatenate([high, low], axis=0), sel_ref[...])
    sums = jnp.concatenate([sum1, sum2, jnp.zeros((32, 128), F32)], axis=0)
    biases = dot_nt(jnp.ones((16, 128), BF16), jnp.concatenate(halves(sums), axis=0))[0:8]
    biases = biases[:, :128] + biases[:, 128:]

    low_lanes = iota((288, 128), 1) < 64
    left, right = [], []
    for c in range(3):
        one, two = kg_ref[0:288, c * 128 : c * 128 + 128], kg_ref[96:384, c * 128 : c * 128 + 128]
        left.append(one + pltpu.roll(two, 64, 1))
        right.append(pltpu.roll(one, 64, 1) + two)
    packed_ref[0:288, :] = jnp.where(low_lanes, left[0], right[1]).astype(BF16)
    packed_ref[288:432, :] = jnp.where(low_lanes[0:144], left[2][0:144], right[2][144:288]).astype(BF16)
    first = first[:32] + first[32:]
    for block in range(5):
        rows = first[block * 8 : block * 8 + 8] if block < 4 else biases
        at = PLAIN * 16 + block * 16
        packed_ref[at : at + 16, :] = jnp.concatenate(halves(rows), axis=0)


def halves(rows):
    high = rows.astype(BF16)
    return high, (rows - high.astype(F32)).astype(BF16)


def sum_kernel(in_ref, out_ref):
    total = in_ref[0:CHUNK, :].astype(F32)
    for i in range(1, in_ref.shape[0] // CHUNK):
        total = total + in_ref[CHUNK * i : CHUNK * i + CHUNK, :].astype(F32)
    blocks = []
    for i in range(CHUNK // 16):
        split = lax.axis_index(PLANE) * (CHUNK // 16) + i >= PLAIN
        upper, lower = total[16 * i : 16 * i + 8], total[16 * i + 8 : 16 * i + 16]
        upper = jnp.where(split, upper + lower, upper)
        lower = jnp.where(split, upper - upper.astype(BF16).astype(F32), lower)
        blocks += [upper, lower]
    chunk = jnp.concatenate(blocks, axis=0).astype(BF16)
    for i in range(out_ref.shape[0] // CHUNK):
        out_ref[CHUNK * i : CHUNK * i + CHUNK, :] = chunk


def unpack_kernel(in_ref, deep_in_ref, deep_ref, second_ref, first_ref, bias1_ref, bias2_ref):
    deep_ref[...] = deep_in_ref[...]
    for tap in range(9):
        for c in range(2):
            at = (tap * 3 + c) * 32
            second_ref[at : at + 32, :] = in_ref[tap * 32 : tap * 32 + 32, c * 64 : c * 64 + 64].astype(F32)
        for half in range(2):
            at = (tap * 3 + 2) * 32 + half * 16
            column, row = divmod(tap * 32 + half * 16, 144)
            rows = in_ref[288 + row : 304 + row, column * 64 : column * 64 + 64]
            second_ref[at : at + 16, :] = rows.astype(F32)
    blocks = [in_ref[at : at + 16, :].astype(F32) for at in range(PLAIN * 16, ROWS, 16)]
    rows = [block[0:8] + block[8:16] for block in blocks]
    first = jnp.concatenate(rows[:4], axis=0).T
    for tap in range(27):
        first_ref[tap] = first[4 * tap : 4 * tap + 4, :]
    bias1_ref[...] = rows[4][0:1, 0:32]
    bias2_ref[...] = rows[4][0:1, 32:96]


def call(kernel, outs, inputs, scratch, limit, flops=0, in_hbm=False):
    place = pl.ANY if in_hbm else pltpu.VMEM
    if in_hbm:
        inputs = [pltpu.with_memory_space_constraint(x, pltpu.HBM) for x in inputs]
    return pl.pallas_call(
        kernel,
        out_shape=outs,
        in_specs=[pl.BlockSpec(memory_space=place) for _ in inputs],
        out_specs=[pl.BlockSpec(memory_space=pltpu.VMEM) for _ in outs],
        scratch_shapes=[pltpu.VMEM(*s) if isinstance(s, tuple) else s for s in scratch],
        compiler_params=pltpu.CompilerParams(vmem_limit_bytes=limit * MIB),
        cost_estimate=pl.CostEstimate(flops=flops, bytes_accessed=10**6, transcendentals=0) if flops else None,
    )(*inputs)


def shape(dims, dtype):
    return jax.ShapeDtypeStruct(dims, dtype)


def exchange(rows, axes):
    blocks = rows.reshape(-1, CHUNK, 128)
    return lax.all_to_all(blocks, axes, split_axis=0, concat_axis=0, tiled=True).reshape(-1, 128)


def per_device(volumes, first_kernel, first_bias, second_kernel, second_bias, deep_grad):
    count = lax.axis_size(DEPTH)
    groups = [
        [slab % count * 4 + y for slab in (odd, odd + 1) for y in range(4)] for odd in range(1, count, 2)
    ]
    twice, *prepared = call(
        front_kernel,
        (
            shape((8,) + volumes.shape[1:], BF16),
            shape((256, 256), BF16), shape((864, 64), BF16), shape((32, 128), F32), shape((64, 128), F32), shape((256, 64), BF16), shape((128, 2048), BF16), shape((256, 256), BF16),
            shape((128, 512), BF16),
        ),
        (
            volumes, first_kernel.reshape(27, 4, 32), second_kernel.reshape(864, 64), first_bias.reshape(1, 32),
            second_bias.reshape(1, 64), deep_grad.reshape(64, 256).T,
        ),
        (
            ((27, 4, 32), BF16), ((128, 32), F32), ((1, 32), F32), ((1, 64), F32),
            pltpu.SemaphoreType.DMA((7,)),
        ),
        8,
        in_hbm=True,
    )
    w1, k2, bias1, bias2, dg, sel, split, pool = prepared
    pair = lax.all_to_all(twice, DEPTH + ("y",), 0, 0, axis_index_groups=groups, tiled=True)
    chip = lax.ppermute(pair, "core", [(0, 1), (1, 0)])
    early = call(
        early_kernel,
        (shape((384, 1024), BF16), shape((2, 256, 1024), F32), shape((192, 1024), BF16), shape((2, 384, 192), BF16), shape((384, 384), BF16)),
        (pair, w1, k2, bias1, split),
        (((768, 128), F32), ((384, 256), F32), ((384, 256), F32), ((2, 32, 1024), F32)),
        8,
        10**9,
    )
    deep, packed = call(
        main_kernel,
        (shape((256, 64), BF16), shape((ROWS, 128), BF16)),
        (pair, chip, *early, w1, bias1, bias2, dg, sel, split, pool),
        (
            ((512, 128), F32), ((256, 256), F32), ((256, 256), F32), ((384, 1024), BF16),
            ((2, 256, 1024), F32), ((2, 32, 1024), F32), ((384, 1024), BF16), ((2, 64, 1024), F32),
            ((384, 1024), BF16), ((384, 1024), BF16), ((128, 1024), F32), ((64, 1024), F32), ((256, 1024), BF16),
            ((384, 384), F32), ((384, 1024), F32),
        ),
        20,
        10**9,
    )
    pieces = exchange(packed, PLANE)
    (copies,) = call(sum_kernel, (shape((128, 128), BF16),), (pieces,), (), 2)
    parts = exchange(copies, LINE)
    (copies,) = call(sum_kernel, (shape((ROWS, 128), BF16),), (parts,), (), 2)
    whole = exchange(copies, PLANE)
    deep, second, first, bias1, bias2 = call(
        unpack_kernel,
        (shape((256, 64), BF16), shape((864, 64), F32), shape((27, 4, 32), F32), shape((1, 32), F32), shape((1, 64), F32)),
        (whole, deep),
        (),
        4,
    )
    return (
        deep.T.reshape(1, 64, 1, 8, 32),
        first.reshape(3, 3, 3, 4, 32),
        bias1.reshape(32),
        second.reshape(3, 3, 3, 32, 64),
        bias2.reshape(64),
    )


def solution(mesh):
    split = Mesh(mesh.devices.reshape(-1, 2, 2, *mesh.devices.shape[1:]), DEPTH + ("y", "x_hi"))
    samples = P(("x_hi", "y"), None, DEPTH, None, None)
    in_specs = (P("x_hi", None, DEPTH, "y", None), P(), P(), P(), P(), samples)
    out_specs = (samples, P(), P(), P(), P())
    return jax.shard_map(per_device, mesh=split, in_specs=in_specs, out_specs=out_specs, check_vma=False)
```

```python
import jax
import jax.numpy as jnp
from jax import lax
from jax.experimental import pallas as pl
from jax.experimental.pallas import tpu as pltpu
from jax.sharding import Mesh, PartitionSpec as P

F32 = jnp.float32
BF16 = jnp.bfloat16
DEPTH = ("z", "x_lo", "core")
PLANE = ("x_lo", "core", "y", "x_hi")
LINE = ("z",)
ROWS = 512
CHUNK = 16
PLAIN = 27
MIB = 1024 * 1024
NT = (((1,), (1,)), ((), ()))


def iota(dims, dim):
    return lax.broadcasted_iota(jnp.int32, dims, dim)


def window_cell(shifted, odd):
    return jnp.where(shifted == 1, 3 - 3 * odd, 1 + odd)


def select_taps(pos):
    row = iota((1, 256), 1)
    a = (row >> 7) * 2 + ((row >> 2) & 1) - pos // 4
    b = window_cell((row >> 6) & 1, (row >> 4) & 1) - pos // 2 % 2
    c = window_cell((row >> 5) & 1, (row >> 3) & 1) - pos % 2
    low = jnp.minimum(jnp.minimum(a, b), c)
    high = jnp.maximum(jnp.maximum(a, b), c)
    tap = jnp.where((low >= 0) & (high <= 2), ((a * 3 + b) * 3 + c) * 4 + (row & 3), -1)
    return jnp.where(iota((128, 256), 0) == tap, 1.0, 0.0).astype(BF16)


def split_width():
    col = iota((1, 256), 1)
    at = ((col >> 6) & 1) * 128 + 2 * (col & 63) + (col >> 7)
    return jnp.where(iota((256, 256), 0) == at, 1.0, 0.0).astype(BF16)


def pool_lanes():
    lane = iota((1, 512), 1)
    at = (lane >> 7) * 32 + ((lane & 63) >> 1)
    return jnp.where(iota((128, 512), 0) == at, 0.125, 0.0).astype(BF16)


def half_column(row, size):
    spread = jnp.broadcast_to(0.5 * row, (size, size))
    eye = iota((size, size), 0) == iota((size, size), 1)
    return jnp.broadcast_to(jnp.sum(jnp.where(eye, spread, 0.0), axis=1, keepdims=True), (size, 128))


def dot(a, b):
    return jnp.dot(a, b, preferred_element_type=F32)


def dot_nt(a, b):
    return lax.dot_general(a, b, NT, preferred_element_type=F32)


def dot_tn(a, b):
    return lax.dot_general(a, b, (((0,), (0,)), ((), ())), preferred_element_type=F32)


def front_kernel(
    volumes_hbm, k1_hbm, k2_hbm, b1_hbm, b2_hbm, dg_hbm,
    twice_ref, k1_ref, k2_ref, bias1_ref, bias2_ref, dg_ref, sel_ref, split_ref, pool_ref,
    b1_ref, b2_ref, sems,
):
    pairs = (
        (k1_hbm, k1_ref), (k2_hbm, k2_ref), (b1_hbm, b1_ref), (b2_hbm, b2_ref), (dg_hbm, dg_ref),
        (volumes_hbm, twice_ref.at[pl.ds(0, 4)]), (volumes_hbm, twice_ref.at[pl.ds(4, 4)]),
    )
    copies = [pltpu.make_async_copy(src, dst, sems.at[n]) for n, (src, dst) in enumerate(pairs)]
    for copy in copies:
        copy.start()
    split_ref[...] = split_width()
    pool_ref[...] = pool_lanes()
    for pos in range(8):
        sel_ref[:, pos * 256 : pos * 256 + 256] = select_taps(pos)
    for copy in copies[2:4]:
        copy.wait()
    bias1_ref[...] = half_column(b1_ref[...], 32)
    bias2_ref[...] = half_column(b2_ref[...], 64)
    for copy in copies[:2] + copies[4:]:
        copy.wait()


def store_first_weights(k1_ref, sel_ref, rows_ref, w1_ref):
    for tap in range(27):
        rows_ref[4 * tap : 4 * tap + 4, :] = 0.5 * k1_ref[tap].astype(F32)
    rows_ref[108:128, :] = jnp.zeros((20, 32), F32)
    k1 = rows_ref[...].T.astype(BF16)
    for pos in range(8):
        w1_ref[pos * 32 : pos * 32 + 32, :] = dot(k1, sel_ref[:, pos * 256 : pos * 256 + 256]).astype(BF16)


def store_second_weights(k2_ref, w2_ref, wb_ref):
    none = jnp.zeros((32, 64), BF16)

    def tap(a, b, c):
        at = ((a * 3 + b) * 3 + c) * 32
        return k2_ref[at : at + 32, :] if 0 <= a <= 2 else none

    for c in range(3):
        for half in range(2):
            stacks = [
                jnp.concatenate([tap(rim - plane, b, c) for rim in (2 * half, 2 * half + 1) for b in range(3)], axis=0)
                for plane in range(2)
            ]
            both = 0.5 * jnp.concatenate([stack.astype(F32) for stack in stacks], axis=1)
            w2_ref[half, c * 128 : c * 128 + 128, :] = both.T.astype(BF16)
        for a in range(3):
            row = [tap(a, 2 - b, 2 - c).astype(F32) for b in range(3)]
            at = (c * 3 + a) * 32
            wb_ref[at : at + 32, :] = jnp.concatenate(row, axis=1).astype(BF16)


def lane_masks(rows):
    lane = iota((rows, 128), 1)
    cell = lane % 64
    return lane < 64, cell != 0, cell != 63


def width_shift(tiles, step, masks):
    _, not_first, not_last = masks
    if step < 0:
        return [jnp.where(not_first, pltpu.roll(t, 1, 1), 0.0) for t in tiles]
    return [jnp.where(not_last, pltpu.roll(t, 127, 1), 0.0) for t in tiles]


def height_shift(tiles, steps, masks):
    low = masks[0]
    swapped = [pltpu.roll(t, 64, 1) for t in tiles]
    zero = jnp.zeros_like(tiles[0])
    out = []
    for step in steps:
        if step < 0:
            before = [zero] + swapped[:-1]
            out.append([jnp.where(low, before[i], swapped[i]) for i in range(len(tiles))])
        else:
            after = swapped[1:] + [zero]
            out.append([jnp.where(low, swapped[i], after[i]) for i in range(len(tiles))])
    return out


def store_height_shifts(ref, put, masks):
    tiles = [ref[:, t * 128 : t * 128 + 128] for t in range(8)]
    before, after = height_shift(tiles, (-1, 1), masks)
    for b, group in enumerate((before, tiles, after)):
        for t in range(8):
            put(b, t, group[t].astype(BF16))


def add_width_shifts(parts, masks):
    sides = []
    for half in range(2):
        one, two, three = (part[:, half * 128 : half * 128 + 128] for part in parts)
        sides.append(two + width_shift([one], -1, masks)[0] + width_shift([three], 1, masks)[0])
    return jnp.concatenate(sides, axis=1)


def grid_ends():
    place = lax.axis_index(DEPTH)
    keep_low = jnp.where(place > 0, 1.0, 0.0).astype(F32)
    keep_high = jnp.where(place < lax.axis_size(DEPTH) - 1, 1.0, 0.0).astype(F32)
    return place % 2, keep_low, keep_high


def fill(f_ref, ref, cell, at, keep=None):
    for y in range(4):
        for ch in range(4):
            part = ref[cell // 4 * 4 + y, ch, cell % 4].astype(F32)
            f_ref[pl.ds((at * 4 + ch) * 32 + y * 8, 8), :] = part if keep is None else part * keep


def split_rows(f_ref, l_ref, g_ref, split_ref, rows):
    for hb in range(2):
        for qq in range(8):
            for low in range(2):
                l_ref[pl.ds((hb * 8 + qq) * rows, rows), low * 128 : low * 128 + 128] = f_ref[
                    pl.ds(4 * qq + 2 * low + hb, rows, stride=32), :
                ]
    g_ref[...] = dot(l_ref[...].astype(BF16), split_ref[...])


def store_windows(g_ref, rows, pair, put):
    masks = lane_masks(8)
    for hb in range(2):
        still, moved = [], []
        for wb in range(2):
            starts = [(hb * 8 + qq) * rows + pair * 8 for qq in range(8)]
            tiles = [g_ref[at : at + 8, wb * 128 : wb * 128 + 128] for at in starts]
            still.append(tiles)
            moved.append(width_shift(tiles, 1 if wb == 0 else -1, masks))
        for ws, group in enumerate((still, moved)):
            step = 1 if hb == 0 else -1
            raised = [height_shift(group[wb], (step,), masks)[0] for wb in range(2)]
            for hs, part in enumerate((group, raised)):
                for qq in range(8):
                    both = jnp.concatenate([part[0][qq], part[1][qq]], axis=0)
                    put((hs * 2 + ws) * 32 + hb * 16, qq, both.astype(BF16))


def first_conv(x_ref, w1_ref, b1_ref, slope_ref, y_ref, scales):
    bias = jnp.concatenate([b1_ref[...], b1_ref[...]], axis=1)
    for plane in range(2):
        for t in range(4):
            lanes = slice(t * 256, t * 256 + 256)
            pre = dot(w1_ref[...], x_ref[plane * 128 : plane * 128 + 256, lanes])
            total = jnp.zeros((32, 256), F32)
            for pos in range(8):
                u = pre[pos * 32 : pos * 32 + 32] + bias
                tanh = jnp.tanh(u)
                w = 1.0 + tanh
                silu = u * w
                slope_ref[plane, pos * 32 : pos * 32 + 32, lanes] = w + silu * (1.0 - tanh)
                total = total + silu
            y_ref[plane, :, lanes] = total * scales[plane]


def store_second_windows(y_ref, put):
    masks = lane_masks(32)
    for plane in range(2):
        store_height_shifts(y_ref.at[plane], lambda b, t, value, plane=plane: put(plane * 96 + b * 32, t, value), masks)


def early_kernel(
    pair_ref, k1_ref, k2_ref, b1_ref, sel_ref, split_ref,
    x_ref, slope_ref, z_ref, w1_ref, w2_ref, wb_ref, f_ref, l_ref, g_ref, y_ref, rows_ref,
):
    _, keep_low, keep_high = grid_ends()
    store_first_weights(k1_ref, sel_ref, rows_ref, w1_ref)
    store_second_weights(k2_ref, w2_ref, wb_ref)
    for cell in range(1, 7):
        fill(f_ref, pair_ref, cell, cell - 1, keep_low if cell < 4 else keep_high)
    split_rows(f_ref, l_ref, g_ref, split_ref, 24)
    for pair in range(3):

        def put(row, t, value, pair=pair):
            x_ref[pair * 128 + row : pair * 128 + row + 16, t * 128 : t * 128 + 128] = value

        store_windows(g_ref, 24, pair, put)
    first_conv(x_ref, w1_ref, b1_ref, slope_ref, y_ref, (0.125 * keep_low, 0.125 * keep_high))

    def put_second(row, t, value):
        z_ref[row : row + 32, t * 128 : t * 128 + 128] = value

    store_second_windows(y_ref, put_second)


def main_kernel(
    pair_ref, chip_ref, early_x_ref, early_slope_ref, early_z_ref, w1_ref, w2_ref, wb_ref,
    b1_ref, b2_ref, dg_ref, sel_ref, split_ref, pool_ref,
    deep_ref, packed_ref,
    f_ref, l_ref, g_ref, x_ref, slope_ref, y_ref, z_ref, g2_ref, gg_ref, gz_ref, back_ref, ds_ref, g1_ref, kg_ref, taps_ref,
):
    parity, keep_low, keep_high = grid_ends()

    for t in range(4):
        lanes = slice(t * 256, t * 256 + 256)
        taps_ref[:, lanes] = dot(w2_ref[parity], early_z_ref[:, lanes])

    for plane in range(4):
        for y in range(4):
            for ch in range(4):
                if plane in (1, 2):
                    part = chip_ref[4 * parity + y, ch, plane - 1 + 2 * parity].astype(F32)
                else:
                    own = pair_ref[4 * (1 - parity) + y, ch, 3 * (1 - parity)].astype(F32)
                    rim = chip_ref[4 * parity + y, ch, 1 if plane == 0 else 2].astype(F32)
                    part = jnp.where(parity == (0 if plane == 0 else 1), own, rim)
                f_ref[pl.ds((plane * 4 + ch) * 32 + y * 8, 8), :] = part

    split_rows(f_ref, l_ref, g_ref, split_ref, 16)
    fresh = pl.multiple_of(128 * (1 - parity), 128)
    shared = pl.multiple_of(256 * parity, 128)
    x_ref[pl.ds(shared, 128), :] = early_x_ref[pl.ds(pl.multiple_of(256 * (1 - parity), 128), 128), :]
    for pair in range(2):

        def put(row, t, value, pair=pair):
            x_ref[pl.ds(pl.multiple_of(fresh + (pair * 128 + row), 16), 16), t * 128 : t * 128 + 128] = value

        store_windows(g_ref, 16, pair, put)
    first_conv(x_ref, w1_ref, b1_ref, slope_ref, y_ref, (0.125, 0.125))

    early_at = pl.multiple_of(192 * parity, 16)
    late_at = pl.multiple_of(192 * (1 - parity), 16)
    z_ref[pl.ds(early_at, 192), :] = early_z_ref[...]

    def put_second(row, t, value):
        z_ref[pl.ds(pl.multiple_of(late_at + row, 16), 32), t * 128 : t * 128 + 128] = value

    store_second_windows(y_ref, put_second)

    bias2 = jnp.concatenate([b2_ref[...], b2_ref[...]], axis=1)
    sum2 = jnp.zeros((64, 128), F32)
    masks64, masks128 = lane_masks(64), lane_masks(128)
    for half in range(2):
        wide = dot_tn(dg_ref[half * 128 : half * 128 + 128, :], pool_ref[...])
        g2_ref[0, :, half * 512 : half * 512 + 512] = wide
    for t in range(4):
        lanes = slice(t * 256, t * 256 + 256)
        taps = taps_ref[:, lanes] + dot(w2_ref[1 - parity], z_ref[pl.ds(late_at, 192), lanes])
        pre = add_width_shifts([taps[c * 128 : c * 128 + 128] for c in range(3)], masks128)
        given = 0.5 * g2_ref[0, :, lanes]
        total = jnp.zeros((64, 256), F32)
        for plane in range(2):
            u = pre[plane * 64 : plane * 64 + 64] + bias2
            tanh = jnp.tanh(u)
            w = 1.0 + tanh
            silu = u * w
            total = total + silu
            grad = given * (w + silu * (1.0 - tanh))
            g2_ref[plane, :, lanes] = grad
            for half in range(2):
                tile = grad[:, half * 128 : half * 128 + 128]
                at = t * 256 + half * 128
                for c, part in enumerate((width_shift([tile], 1, masks64), [tile], width_shift([tile], -1, masks64))):
                    row = plane * 192 + c * 64
                    gg_ref[row : row + 64, at : at + 128] = part[0].astype(BF16)
            sum2 = sum2 + grad[:, :128] + grad[:, 128:]
        ds_ref[:, lanes] = total

    for half in range(2):
        part = ds_ref[:, half * 512 : half * 512 + 512]
        high, low = halves(part)
        deep = dot_nt(pool_ref[...], jnp.concatenate([high, low], axis=0))
        deep_ref[half * 128 : half * 128 + 128, :] = (deep[:, :64] + deep[:, 64:]).astype(BF16)

    for plane in range(2):

        def put(b, t, value, plane=plane):
            row = plane * 192 + b * 64
            gz_ref[row : row + 64, t * 128 : t * 128 + 128] = value

        store_height_shifts(g2_ref.at[plane], put, masks64)
    for t in range(4):
        lanes = slice(t * 256, t * 256 + 256)
        one, two = (dot(wb_ref[...], gz_ref[plane * 192 : plane * 192 + 192, lanes]) for plane in range(2))
        parts = []
        for c in range(3):
            at = c * 96
            both = one[at + 32 : at + 96] + two[at : at + 64]
            parts.append(jnp.concatenate([one[at : at + 32], both, two[at + 64 : at + 96]], axis=0))
        back = add_width_shifts(parts, masks128)
        back_ref[0:32, lanes] = back[0:32] * (0.0625 * keep_low)
        back_ref[32:96, lanes] = back[32:96] * 0.0625
        back_ref[96:128, lanes] = back[96:128] * (0.0625 * keep_high)

    kg_ref[...] = dot_nt(z_ref[0:288, :], gg_ref[0:192, :]) + dot_nt(z_ref[96:384, :], gg_ref[192:384, :])

    sum1 = jnp.zeros((32, 128), F32)
    grads = jnp.zeros((256, 256), F32)
    for early in range(2):
        windows_ref, slopes_ref = ((x_ref, slope_ref), (early_x_ref, early_slope_ref))[early]
        start = 64 * (parity if early else 1 - parity)
        for plane in range(2):
            at = pl.multiple_of(start + plane * 32, 32)
            for t in range(4):
                lanes = slice(t * 256, t * 256 + 256)
                back = back_ref[pl.ds(at, 32), lanes]
                for pos in range(8):
                    grad = back * slopes_ref[plane, pos * 32 : pos * 32 + 32, lanes]
                    g1_ref[pos * 32 : pos * 32 + 32, lanes] = grad.astype(BF16)
                    sum1 = sum1 + grad[:, :128] + grad[:, 128:]
            grads = grads + dot_nt(g1_ref[...], windows_ref[plane * 128 : plane * 128 + 256, :])

    spread = jnp.concatenate([grads[pos * 32 : pos * 32 + 32] for pos in range(8)], axis=1)
    high, low = halves(spread)
    first = dot_nt(jnp.concatenate([high, low], axis=0), sel_ref[...])
    sums = jnp.concatenate([sum1, sum2, jnp.zeros((32, 128), F32)], axis=0)
    biases = dot_nt(jnp.ones((16, 128), BF16), jnp.concatenate(halves(sums), axis=0))[0:8]
    biases = biases[:, :128] + biases[:, 128:]

    packed_ref[0:288, :] = kg_ref[:, 0:128].astype(BF16)
    last = jnp.concatenate([kg_ref[0:144, 128:192], kg_ref[144:288, 128:192]], axis=1)
    packed_ref[288:432, :] = last.astype(BF16)
    first = first[:32] + first[32:]
    for block in range(5):
        rows = first[block * 8 : block * 8 + 8] if block < 4 else biases
        at = PLAIN * 16 + block * 16
        packed_ref[at : at + 16, :] = jnp.concatenate(halves(rows), axis=0)


def halves(rows):
    high = rows.astype(BF16)
    return high, (rows - high.astype(F32)).astype(BF16)


def sum_kernel(in_ref, out_ref):
    total = in_ref[0:CHUNK, :].astype(F32)
    for i in range(1, in_ref.shape[0] // CHUNK):
        total = total + in_ref[CHUNK * i : CHUNK * i + CHUNK, :].astype(F32)
    blocks = []
    for i in range(CHUNK // 16):
        split = lax.axis_index(PLANE) * (CHUNK // 16) + i >= PLAIN
        upper, lower = total[16 * i : 16 * i + 8], total[16 * i + 8 : 16 * i + 16]
        upper = jnp.where(split, upper + lower, upper)
        lower = jnp.where(split, upper - upper.astype(BF16).astype(F32), lower)
        blocks += [upper, lower]
    chunk = jnp.concatenate(blocks, axis=0).astype(BF16)
    for i in range(out_ref.shape[0] // CHUNK):
        out_ref[CHUNK * i : CHUNK * i + CHUNK, :] = chunk


def unpack_kernel(in_ref, deep_in_ref, deep_ref, second_ref, first_ref, bias1_ref, bias2_ref):
    deep_ref[...] = deep_in_ref[...]
    for tap in range(9):
        for c in range(2):
            at = (tap * 3 + c) * 32
            second_ref[at : at + 32, :] = in_ref[tap * 32 : tap * 32 + 32, c * 64 : c * 64 + 64].astype(F32)
        for half in range(2):
            at = (tap * 3 + 2) * 32 + half * 16
            column, row = divmod(tap * 32 + half * 16, 144)
            rows = in_ref[288 + row : 304 + row, column * 64 : column * 64 + 64]
            second_ref[at : at + 16, :] = rows.astype(F32)
    blocks = [in_ref[at : at + 16, :].astype(F32) for at in range(PLAIN * 16, ROWS, 16)]
    rows = [block[0:8] + block[8:16] for block in blocks]
    first = jnp.concatenate(rows[:4], axis=0).T
    for tap in range(27):
        first_ref[tap] = first[4 * tap : 4 * tap + 4, :]
    bias1_ref[...] = rows[4][0:1, 0:32]
    bias2_ref[...] = rows[4][0:1, 32:96]


def call(kernel, outs, inputs, scratch, limit, flops=0, in_hbm=False):
    place = pl.ANY if in_hbm else pltpu.VMEM
    if in_hbm:
        inputs = [pltpu.with_memory_space_constraint(x, pltpu.HBM) for x in inputs]
    return pl.pallas_call(
        kernel,
        out_shape=outs,
        in_specs=[pl.BlockSpec(memory_space=place) for _ in inputs],
        out_specs=[pl.BlockSpec(memory_space=pltpu.VMEM) for _ in outs],
        scratch_shapes=[pltpu.VMEM(*s) if isinstance(s, tuple) else s for s in scratch],
        compiler_params=pltpu.CompilerParams(vmem_limit_bytes=limit * MIB),
        cost_estimate=pl.CostEstimate(flops=flops, bytes_accessed=10**6, transcendentals=0) if flops else None,
    )(*inputs)


def shape(dims, dtype):
    return jax.ShapeDtypeStruct(dims, dtype)


def exchange(rows, axes):
    blocks = rows.reshape(-1, CHUNK, 128)
    return lax.all_to_all(blocks, axes, split_axis=0, concat_axis=0, tiled=True).reshape(-1, 128)


def per_device(volumes, first_kernel, first_bias, second_kernel, second_bias, deep_grad):
    count = lax.axis_size(DEPTH)
    groups = [
        [slab % count * 4 + y for slab in (odd, odd + 1) for y in range(4)] for odd in range(1, count, 2)
    ]
    twice, *prepared = call(
        front_kernel,
        (
            shape((8,) + volumes.shape[1:], BF16),
            shape((27, 4, 32), BF16), shape((864, 64), BF16), shape((32, 128), F32), shape((64, 128), F32), shape((256, 64), BF16), shape((128, 2048), BF16), shape((256, 256), BF16),
            shape((128, 512), BF16),
        ),
        (
            volumes, first_kernel.reshape(27, 4, 32), second_kernel.reshape(864, 64), first_bias.reshape(1, 32),
            second_bias.reshape(1, 64), deep_grad.reshape(64, 256).T,
        ),
        (
            ((1, 32), F32), ((1, 64), F32),
            pltpu.SemaphoreType.DMA((7,)),
        ),
        8,
        in_hbm=True,
    )
    k1, k2, bias1, bias2, dg, sel, split, pool = prepared
    pair = lax.all_to_all(twice, DEPTH + ("y",), 0, 0, axis_index_groups=groups, tiled=True)
    chip = lax.ppermute(pair, "core", [(0, 1), (1, 0)])
    early = call(
        early_kernel,
        (
            shape((384, 1024), BF16), shape((2, 256, 1024), F32), shape((192, 1024), BF16),
            shape((256, 256), BF16), shape((2, 384, 192), BF16), shape((288, 192), BF16),
        ),
        (pair, k1, k2, bias1, sel, split),
        (
            ((768, 128), F32), ((384, 256), F32), ((384, 256), F32), ((2, 32, 1024), F32), ((128, 32), F32),
        ),
        8,
        10**9,
    )
    deep, packed = call(
        main_kernel,
        (shape((256, 64), BF16), shape((ROWS, 128), BF16)),
        (pair, chip, *early, bias1, bias2, dg, sel, split, pool),
        (
            ((512, 128), F32), ((256, 256), F32), ((256, 256), F32), ((384, 1024), BF16),
            ((2, 256, 1024), F32), ((2, 32, 1024), F32), ((384, 1024), BF16), ((2, 64, 1024), F32),
            ((384, 1024), BF16), ((384, 1024), BF16), ((128, 1024), F32), ((64, 1024), F32), ((256, 1024), BF16),
            ((288, 192), F32), ((384, 1024), F32),
        ),
        20,
        10**9,
    )
    pieces = exchange(packed, PLANE)
    (copies,) = call(sum_kernel, (shape((128, 128), BF16),), (pieces,), (), 2)
    parts = exchange(copies, LINE)
    (copies,) = call(sum_kernel, (shape((ROWS, 128), BF16),), (parts,), (), 2)
    whole = exchange(copies, PLANE)
    deep, second, first, bias1, bias2 = call(
        unpack_kernel,
        (shape((256, 64), BF16), shape((864, 64), F32), shape((27, 4, 32), F32), shape((1, 32), F32), shape((1, 64), F32)),
        (whole, deep),
        (),
        4,
    )
    return (
        deep.T.reshape(1, 64, 1, 8, 32),
        first.reshape(3, 3, 3, 4, 32),
        bias1.reshape(32),
        second.reshape(3, 3, 3, 32, 64),
        bias2.reshape(64),
    )


def solution(mesh):
    split = Mesh(mesh.devices.reshape(-1, 2, 2, *mesh.devices.shape[1:]), DEPTH + ("y", "x_hi"))
    samples = P(("x_hi", "y"), None, DEPTH, None, None)
    in_specs = (P("x_hi", None, DEPTH, "y", None), P(), P(), P(), P(), samples)
    out_specs = (samples, P(), P(), P(), P())
    return jax.shard_map(per_device, mesh=split, in_specs=in_specs, out_specs=out_specs, check_vma=False)
```

```python
import jax
import jax.numpy as jnp
from jax import lax
from jax.experimental import pallas as pl
from jax.experimental.pallas import tpu as pltpu
from jax.sharding import Mesh, PartitionSpec as P

F32 = jnp.float32
BF16 = jnp.bfloat16
DEPTH = ("z", "x_lo", "core")
PLANE = ("y", "x_hi", "x_lo", "core")
LINE = ("z",)
ROWS = 512
CHUNK = 16
PLAIN = 27
MIB = 1024 * 1024
NT = (((1,), (1,)), ((), ()))


def iota(dims, dim):
    return lax.broadcasted_iota(jnp.int32, dims, dim)


def window_cell(shifted, odd):
    return jnp.where(shifted == 1, 3 - 3 * odd, 1 + odd)


def select_taps(pos):
    row = iota((1, 256), 1)
    a = (row >> 7) * 2 + ((row >> 2) & 1) - pos // 4
    b = window_cell((row >> 6) & 1, (row >> 4) & 1) - pos // 2 % 2
    c = window_cell((row >> 5) & 1, (row >> 3) & 1) - pos % 2
    low = jnp.minimum(jnp.minimum(a, b), c)
    high = jnp.maximum(jnp.maximum(a, b), c)
    tap = jnp.where((low >= 0) & (high <= 2), ((a * 3 + b) * 3 + c) * 4 + (row & 3), -1)
    return jnp.where(iota((128, 256), 0) == tap, 1.0, 0.0).astype(BF16)


def split_width():
    col = iota((1, 256), 1)
    at = ((col >> 6) & 1) * 128 + 2 * (col & 63) + (col >> 7)
    return jnp.where(iota((256, 256), 0) == at, 1.0, 0.0).astype(BF16)


def pool_lanes():
    lane = iota((1, 512), 1)
    at = (lane >> 7) * 32 + ((lane & 63) >> 1)
    return jnp.where(iota((128, 512), 0) == at, 0.125, 0.0).astype(BF16)


def half_column(row, size):
    spread = jnp.broadcast_to(0.5 * row, (size, size))
    eye = iota((size, size), 0) == iota((size, size), 1)
    return jnp.broadcast_to(jnp.sum(jnp.where(eye, spread, 0.0), axis=1, keepdims=True), (size, 128))


def dot(a, b):
    return jnp.dot(a, b, preferred_element_type=F32)


def dot_nt(a, b):
    return lax.dot_general(a, b, NT, preferred_element_type=F32)


def dot_tn(a, b):
    return lax.dot_general(a, b, (((0,), (0,)), ((), ())), preferred_element_type=F32)


def front_kernel(
    volumes_hbm, k1_hbm, k2_hbm, b1_hbm, b2_hbm, dg_hbm,
    twice_ref, k1_ref, k2_ref, bias1_ref, bias2_ref, dg_ref, sel_ref, split_ref, pool_ref,
    b1_ref, b2_ref, sems,
):
    pairs = (
        (k1_hbm, k1_ref), (k2_hbm, k2_ref), (b1_hbm, b1_ref), (b2_hbm, b2_ref), (dg_hbm, dg_ref),
        (volumes_hbm, twice_ref.at[pl.ds(0, 4)]), (volumes_hbm, twice_ref.at[pl.ds(4, 4)]),
    )
    copies = [pltpu.make_async_copy(src, dst, sems.at[n]) for n, (src, dst) in enumerate(pairs)]
    for copy in copies:
        copy.start()
    split_ref[...] = split_width()
    pool_ref[...] = pool_lanes()
    for pos in range(8):
        sel_ref[:, pos * 256 : pos * 256 + 256] = select_taps(pos)
    for copy in copies[2:4]:
        copy.wait()
    bias1_ref[...] = half_column(b1_ref[...], 32)
    bias2_ref[...] = half_column(b2_ref[...], 64)
    for copy in copies[:2] + copies[4:]:
        copy.wait()


def store_first_weights(k1_ref, sel_ref, rows_ref, w1_ref):
    for tap in range(27):
        rows_ref[4 * tap : 4 * tap + 4, :] = 0.5 * k1_ref[tap].astype(F32)
    rows_ref[108:128, :] = jnp.zeros((20, 32), F32)
    k1 = rows_ref[...].T.astype(BF16)
    for pos in range(8):
        w1_ref[pos * 32 : pos * 32 + 32, :] = dot(k1, sel_ref[:, pos * 256 : pos * 256 + 256]).astype(BF16)


def store_second_weights(k2_ref, w2_ref, wb_ref):
    none = jnp.zeros((32, 64), BF16)

    def tap(a, b, c):
        at = ((a * 3 + b) * 3 + c) * 32
        return k2_ref[at : at + 32, :] if 0 <= a <= 2 else none

    for c in range(3):
        for half in range(2):
            stacks = [
                jnp.concatenate([tap(rim - plane, b, c) for rim in (2 * half, 2 * half + 1) for b in range(3)], axis=0)
                for plane in range(2)
            ]
            both = 0.5 * jnp.concatenate([stack.astype(F32) for stack in stacks], axis=1)
            w2_ref[half, c * 128 : c * 128 + 128, :] = both.T.astype(BF16)
        for a in range(3):
            row = [tap(a, 2 - b, 2 - c).astype(F32) for b in range(3)]
            at = (c * 3 + a) * 32
            wb_ref[at : at + 32, :] = jnp.concatenate(row, axis=1).astype(BF16)


def lane_masks(rows):
    lane = iota((rows, 128), 1)
    cell = lane % 64
    return lane < 64, cell != 0, cell != 63


def width_shift(tiles, step, masks):
    _, not_first, not_last = masks
    if step < 0:
        return [jnp.where(not_first, pltpu.roll(t, 1, 1), 0.0) for t in tiles]
    return [jnp.where(not_last, pltpu.roll(t, 127, 1), 0.0) for t in tiles]


def height_shift(tiles, steps, masks):
    low = masks[0]
    swapped = [pltpu.roll(t, 64, 1) for t in tiles]
    zero = jnp.zeros_like(tiles[0])
    out = []
    for step in steps:
        if step < 0:
            before = [zero] + swapped[:-1]
            out.append([jnp.where(low, before[i], swapped[i]) for i in range(len(tiles))])
        else:
            after = swapped[1:] + [zero]
            out.append([jnp.where(low, swapped[i], after[i]) for i in range(len(tiles))])
    return out


def store_height_shifts(ref, put, masks):
    tiles = [ref[:, t * 128 : t * 128 + 128] for t in range(8)]
    before, after = height_shift(tiles, (-1, 1), masks)
    for b, group in enumerate((before, tiles, after)):
        for t in range(8):
            put(b, t, group[t].astype(BF16))


def add_width_shifts(parts, masks):
    sides = []
    for half in range(2):
        one, two, three = (part[:, half * 128 : half * 128 + 128] for part in parts)
        sides.append(two + width_shift([one], -1, masks)[0] + width_shift([three], 1, masks)[0])
    return jnp.concatenate(sides, axis=1)


def grid_ends():
    place = lax.axis_index(DEPTH)
    keep_low = jnp.where(place > 0, 1.0, 0.0).astype(F32)
    keep_high = jnp.where(place < lax.axis_size(DEPTH) - 1, 1.0, 0.0).astype(F32)
    return place % 2, keep_low, keep_high


def fill(f_ref, ref, cell, at, keep=None):
    for y in range(4):
        for ch in range(4):
            part = ref[cell // 4 * 4 + y, ch, cell % 4].astype(F32)
            f_ref[pl.ds((at * 4 + ch) * 32 + y * 8, 8), :] = part if keep is None else part * keep


def split_rows(f_ref, l_ref, g_ref, split_ref, rows):
    for hb in range(2):
        for qq in range(8):
            for low in range(2):
                l_ref[pl.ds((hb * 8 + qq) * rows, rows), low * 128 : low * 128 + 128] = f_ref[
                    pl.ds(4 * qq + 2 * low + hb, rows, stride=32), :
                ]
    g_ref[...] = dot(l_ref[...].astype(BF16), split_ref[...])


def store_windows(g_ref, rows, pair, put):
    masks = lane_masks(8)
    for hb in range(2):
        still, moved = [], []
        for wb in range(2):
            starts = [(hb * 8 + qq) * rows + pair * 8 for qq in range(8)]
            tiles = [g_ref[at : at + 8, wb * 128 : wb * 128 + 128] for at in starts]
            still.append(tiles)
            moved.append(width_shift(tiles, 1 if wb == 0 else -1, masks))
        for ws, group in enumerate((still, moved)):
            step = 1 if hb == 0 else -1
            raised = [height_shift(group[wb], (step,), masks)[0] for wb in range(2)]
            for hs, part in enumerate((group, raised)):
                for qq in range(8):
                    both = jnp.concatenate([part[0][qq], part[1][qq]], axis=0)
                    put((hs * 2 + ws) * 32 + hb * 16, qq, both.astype(BF16))


def first_conv(x_ref, w1_ref, b1_ref, slope_ref, y_ref, scales):
    bias = jnp.concatenate([b1_ref[...], b1_ref[...]], axis=1)
    for plane in range(2):
        for t in range(4):
            lanes = slice(t * 256, t * 256 + 256)
            pre = dot(w1_ref[...], x_ref[plane * 128 : plane * 128 + 256, lanes])
            total = jnp.zeros((32, 256), F32)
            for pos in range(8):
                u = pre[pos * 32 : pos * 32 + 32] + bias
                tanh = jnp.tanh(u)
                w = 1.0 + tanh
                silu = u * w
                slope_ref[plane, pos * 32 : pos * 32 + 32, lanes] = w + silu * (1.0 - tanh)
                total = total + silu
            y_ref[plane, :, lanes] = total * scales[plane]


def store_second_windows(y_ref, put):
    masks = lane_masks(32)
    for plane in range(2):
        store_height_shifts(y_ref.at[plane], lambda b, t, value, plane=plane: put(plane * 96 + b * 32, t, value), masks)


def early_kernel(
    pair_ref, k1_ref, k2_ref, b1_ref, sel_ref, split_ref,
    x_ref, slope_ref, z_ref, w1_ref, w2_ref, wb_ref, f_ref, l_ref, g_ref, y_ref, rows_ref,
):
    _, keep_low, keep_high = grid_ends()
    store_first_weights(k1_ref, sel_ref, rows_ref, w1_ref)
    store_second_weights(k2_ref, w2_ref, wb_ref)
    for cell in range(1, 7):
        fill(f_ref, pair_ref, cell, cell - 1, keep_low if cell < 4 else keep_high)
    split_rows(f_ref, l_ref, g_ref, split_ref, 24)
    for pair in range(3):

        def put(row, t, value, pair=pair):
            x_ref[pair * 128 + row : pair * 128 + row + 16, t * 128 : t * 128 + 128] = value

        store_windows(g_ref, 24, pair, put)
    first_conv(x_ref, w1_ref, b1_ref, slope_ref, y_ref, (0.125 * keep_low, 0.125 * keep_high))

    def put_second(row, t, value):
        z_ref[row : row + 32, t * 128 : t * 128 + 128] = value

    store_second_windows(y_ref, put_second)


def main_kernel(
    pair_ref, chip_ref, early_x_ref, early_slope_ref, early_z_ref, w1_ref, w2_ref, wb_ref,
    b1_ref, b2_ref, dg_ref, sel_ref, split_ref, pool_ref,
    deep_ref, packed_ref,
    f_ref, l_ref, g_ref, x_ref, slope_ref, y_ref, z_ref, g2_ref, gg_ref, gz_ref, back_ref, ds_ref, g1_ref, kg_ref, taps_ref,
):
    parity, keep_low, keep_high = grid_ends()

    for t in range(4):
        lanes = slice(t * 256, t * 256 + 256)
        taps_ref[:, lanes] = dot(w2_ref[parity], early_z_ref[:, lanes])

    for plane in range(4):
        for y in range(4):
            for ch in range(4):
                if plane in (1, 2):
                    part = chip_ref[4 * parity + y, ch, plane - 1 + 2 * parity].astype(F32)
                else:
                    own = pair_ref[4 * (1 - parity) + y, ch, 3 * (1 - parity)].astype(F32)
                    rim = chip_ref[4 * parity + y, ch, 1 if plane == 0 else 2].astype(F32)
                    part = jnp.where(parity == (0 if plane == 0 else 1), own, rim)
                f_ref[pl.ds((plane * 4 + ch) * 32 + y * 8, 8), :] = part

    split_rows(f_ref, l_ref, g_ref, split_ref, 16)
    fresh = pl.multiple_of(128 * (1 - parity), 128)
    shared = pl.multiple_of(256 * parity, 128)
    x_ref[pl.ds(shared, 128), :] = early_x_ref[pl.ds(pl.multiple_of(256 * (1 - parity), 128), 128), :]
    for pair in range(2):

        def put(row, t, value, pair=pair):
            x_ref[pl.ds(pl.multiple_of(fresh + (pair * 128 + row), 16), 16), t * 128 : t * 128 + 128] = value

        store_windows(g_ref, 16, pair, put)
    first_conv(x_ref, w1_ref, b1_ref, slope_ref, y_ref, (0.125, 0.125))

    early_at = pl.multiple_of(192 * parity, 16)
    late_at = pl.multiple_of(192 * (1 - parity), 16)
    z_ref[pl.ds(early_at, 192), :] = early_z_ref[...]

    def put_second(row, t, value):
        z_ref[pl.ds(pl.multiple_of(late_at + row, 16), 32), t * 128 : t * 128 + 128] = value

    store_second_windows(y_ref, put_second)

    bias2 = jnp.concatenate([b2_ref[...], b2_ref[...]], axis=1)
    sum2 = jnp.zeros((64, 128), F32)
    masks64, masks128 = lane_masks(64), lane_masks(128)
    for half in range(2):
        wide = dot_tn(dg_ref[half * 128 : half * 128 + 128, :], pool_ref[...])
        g2_ref[0, :, half * 512 : half * 512 + 512] = wide
    for t in range(4):
        lanes = slice(t * 256, t * 256 + 256)
        taps = taps_ref[:, lanes] + dot(w2_ref[1 - parity], z_ref[pl.ds(late_at, 192), lanes])
        pre = add_width_shifts([taps[c * 128 : c * 128 + 128] for c in range(3)], masks128)
        given = 0.5 * g2_ref[0, :, lanes]
        total = jnp.zeros((64, 256), F32)
        for plane in range(2):
            u = pre[plane * 64 : plane * 64 + 64] + bias2
            tanh = jnp.tanh(u)
            w = 1.0 + tanh
            silu = u * w
            total = total + silu
            grad = given * (w + silu * (1.0 - tanh))
            g2_ref[plane, :, lanes] = grad
            for half in range(2):
                tile = grad[:, half * 128 : half * 128 + 128]
                at = t * 256 + half * 128
                for c, part in enumerate((width_shift([tile], 1, masks64), [tile], width_shift([tile], -1, masks64))):
                    row = plane * 192 + c * 64
                    gg_ref[row : row + 64, at : at + 128] = part[0].astype(BF16)
            sum2 = sum2 + grad[:, :128] + grad[:, 128:]
        ds_ref[:, lanes] = total

    for half in range(2):
        part = ds_ref[:, half * 512 : half * 512 + 512]
        high, low = halves(part)
        deep = dot_nt(pool_ref[...], jnp.concatenate([high, low], axis=0))
        deep_ref[half * 128 : half * 128 + 128, :] = (deep[:, :64] + deep[:, 64:]).astype(BF16)

    for plane in range(2):

        def put(b, t, value, plane=plane):
            row = plane * 192 + b * 64
            gz_ref[row : row + 64, t * 128 : t * 128 + 128] = value

        store_height_shifts(g2_ref.at[plane], put, masks64)
    for t in range(4):
        lanes = slice(t * 256, t * 256 + 256)
        one, two = (dot(wb_ref[...], gz_ref[plane * 192 : plane * 192 + 192, lanes]) for plane in range(2))
        parts = []
        for c in range(3):
            at = c * 96
            both = one[at + 32 : at + 96] + two[at : at + 64]
            parts.append(jnp.concatenate([one[at : at + 32], both, two[at + 64 : at + 96]], axis=0))
        back = add_width_shifts(parts, masks128)
        back_ref[0:32, lanes] = back[0:32] * (0.0625 * keep_low)
        back_ref[32:96, lanes] = back[32:96] * 0.0625
        back_ref[96:128, lanes] = back[96:128] * (0.0625 * keep_high)

    kg_ref[...] = dot_nt(z_ref[0:288, :], gg_ref[0:192, :]) + dot_nt(z_ref[96:384, :], gg_ref[192:384, :])

    sum1 = jnp.zeros((32, 128), F32)
    grads = jnp.zeros((256, 256), F32)
    for early in range(2):
        windows_ref, slopes_ref = ((x_ref, slope_ref), (early_x_ref, early_slope_ref))[early]
        start = 64 * (parity if early else 1 - parity)
        for plane in range(2):
            at = pl.multiple_of(start + plane * 32, 32)
            for t in range(4):
                lanes = slice(t * 256, t * 256 + 256)
                back = back_ref[pl.ds(at, 32), lanes]
                for pos in range(8):
                    grad = back * slopes_ref[plane, pos * 32 : pos * 32 + 32, lanes]
                    g1_ref[pos * 32 : pos * 32 + 32, lanes] = grad.astype(BF16)
                    sum1 = sum1 + grad[:, :128] + grad[:, 128:]
            grads = grads + dot_nt(g1_ref[...], windows_ref[plane * 128 : plane * 128 + 256, :])

    spread = jnp.concatenate([grads[pos * 32 : pos * 32 + 32] for pos in range(8)], axis=1)
    high, low = halves(spread)
    first = dot_nt(jnp.concatenate([high, low], axis=0), sel_ref[...])
    sums = jnp.concatenate([sum1, sum2, jnp.zeros((32, 128), F32)], axis=0)
    biases = dot_nt(jnp.ones((16, 128), BF16), jnp.concatenate(halves(sums), axis=0))[0:8]
    biases = biases[:, :128] + biases[:, 128:]

    packed_ref[0:288, :] = kg_ref[:, 0:128].astype(BF16)
    last = jnp.concatenate([kg_ref[0:144, 128:192], kg_ref[144:288, 128:192]], axis=1)
    packed_ref[288:432, :] = last.astype(BF16)
    first = first[:32] + first[32:]
    for block in range(5):
        rows = first[block * 8 : block * 8 + 8] if block < 4 else biases
        at = PLAIN * 16 + block * 16
        packed_ref[at : at + 16, :] = jnp.concatenate(halves(rows), axis=0)


def halves(rows):
    high = rows.astype(BF16)
    return high, (rows - high.astype(F32)).astype(BF16)


def sum_kernel(in_ref, out_ref):
    total = in_ref[0:CHUNK, :].astype(F32)
    for i in range(1, in_ref.shape[0] // CHUNK):
        total = total + in_ref[CHUNK * i : CHUNK * i + CHUNK, :].astype(F32)
    blocks = []
    for i in range(CHUNK // 16):
        split = lax.axis_index(PLANE) * (CHUNK // 16) + i >= PLAIN
        upper, lower = total[16 * i : 16 * i + 8], total[16 * i + 8 : 16 * i + 16]
        upper = jnp.where(split, upper + lower, upper)
        lower = jnp.where(split, upper - upper.astype(BF16).astype(F32), lower)
        blocks += [upper, lower]
    chunk = jnp.concatenate(blocks, axis=0).astype(BF16)
    for i in range(out_ref.shape[0] // CHUNK):
        out_ref[CHUNK * i : CHUNK * i + CHUNK, :] = chunk


def unpack_kernel(in_ref, deep_in_ref, deep_ref, second_ref, first_ref, bias1_ref, bias2_ref):
    deep_ref[...] = deep_in_ref[...]
    for tap in range(9):
        for c in range(2):
            at = (tap * 3 + c) * 32
            second_ref[at : at + 32, :] = in_ref[tap * 32 : tap * 32 + 32, c * 64 : c * 64 + 64].astype(F32)
        for half in range(2):
            at = (tap * 3 + 2) * 32 + half * 16
            column, row = divmod(tap * 32 + half * 16, 144)
            rows = in_ref[288 + row : 304 + row, column * 64 : column * 64 + 64]
            second_ref[at : at + 16, :] = rows.astype(F32)
    blocks = [in_ref[at : at + 16, :].astype(F32) for at in range(PLAIN * 16, ROWS, 16)]
    rows = [block[0:8] + block[8:16] for block in blocks]
    first = jnp.concatenate(rows[:4], axis=0).T
    for tap in range(27):
        first_ref[tap] = first[4 * tap : 4 * tap + 4, :]
    bias1_ref[...] = rows[4][0:1, 0:32]
    bias2_ref[...] = rows[4][0:1, 32:96]


def call(kernel, outs, inputs, scratch, limit, flops=0, in_hbm=False):
    place = pl.ANY if in_hbm else pltpu.VMEM
    if in_hbm:
        inputs = [pltpu.with_memory_space_constraint(x, pltpu.HBM) for x in inputs]
    return pl.pallas_call(
        kernel,
        out_shape=outs,
        in_specs=[pl.BlockSpec(memory_space=place) for _ in inputs],
        out_specs=[pl.BlockSpec(memory_space=pltpu.VMEM) for _ in outs],
        scratch_shapes=[pltpu.VMEM(*s) if isinstance(s, tuple) else s for s in scratch],
        compiler_params=pltpu.CompilerParams(vmem_limit_bytes=limit * MIB),
        cost_estimate=pl.CostEstimate(flops=flops, bytes_accessed=10**6, transcendentals=0) if flops else None,
    )(*inputs)


def shape(dims, dtype):
    return jax.ShapeDtypeStruct(dims, dtype)


def exchange(rows, axes):
    blocks = rows.reshape(-1, CHUNK, 128)
    return lax.all_to_all(blocks, axes, split_axis=0, concat_axis=0, tiled=True).reshape(-1, 128)


def per_device(volumes, first_kernel, first_bias, second_kernel, second_bias, deep_grad):
    count = lax.axis_size(DEPTH)
    groups = [
        [slab % count * 4 + y for slab in (odd, odd + 1) for y in range(4)] for odd in range(1, count, 2)
    ]
    twice, *prepared = call(
        front_kernel,
        (
            shape((8,) + volumes.shape[1:], BF16),
            shape((27, 4, 32), BF16), shape((864, 64), BF16), shape((32, 128), F32), shape((64, 128), F32), shape((256, 64), BF16), shape((128, 2048), BF16), shape((256, 256), BF16),
            shape((128, 512), BF16),
        ),
        (
            volumes, first_kernel.reshape(27, 4, 32), second_kernel.reshape(864, 64), first_bias.reshape(1, 32),
            second_bias.reshape(1, 64), deep_grad.reshape(64, 256).T,
        ),
        (
            ((1, 32), F32), ((1, 64), F32),
            pltpu.SemaphoreType.DMA((7,)),
        ),
        8,
        in_hbm=True,
    )
    k1, k2, bias1, bias2, dg, sel, split, pool = prepared
    pair = lax.all_to_all(twice, DEPTH + ("y",), 0, 0, axis_index_groups=groups, tiled=True)
    chip = lax.ppermute(pair, "core", [(0, 1), (1, 0)])
    early = call(
        early_kernel,
        (
            shape((384, 1024), BF16), shape((2, 256, 1024), F32), shape((192, 1024), BF16),
            shape((256, 256), BF16), shape((2, 384, 192), BF16), shape((288, 192), BF16),
        ),
        (pair, k1, k2, bias1, sel, split),
        (
            ((768, 128), F32), ((384, 256), F32), ((384, 256), F32), ((2, 32, 1024), F32), ((128, 32), F32),
        ),
        8,
        10**9,
    )
    deep, packed = call(
        main_kernel,
        (shape((256, 64), BF16), shape((ROWS, 128), BF16)),
        (pair, chip, *early, bias1, bias2, dg, sel, split, pool),
        (
            ((512, 128), F32), ((256, 256), F32), ((256, 256), F32), ((384, 1024), BF16),
            ((2, 256, 1024), F32), ((2, 32, 1024), F32), ((384, 1024), BF16), ((2, 64, 1024), F32),
            ((384, 1024), BF16), ((384, 1024), BF16), ((128, 1024), F32), ((64, 1024), F32), ((256, 1024), BF16),
            ((288, 192), F32), ((384, 1024), F32),
        ),
        20,
        10**9,
    )
    pieces = exchange(packed, PLANE)
    (copies,) = call(sum_kernel, (shape((128, 128), BF16),), (pieces,), (), 2)
    parts = exchange(copies, LINE)
    (copies,) = call(sum_kernel, (shape((ROWS, 128), BF16),), (parts,), (), 2)
    whole = exchange(copies, PLANE)
    deep, second, first, bias1, bias2 = call(
        unpack_kernel,
        (shape((256, 64), BF16), shape((864, 64), F32), shape((27, 4, 32), F32), shape((1, 32), F32), shape((1, 64), F32)),
        (whole, deep),
        (),
        4,
    )
    return (
        deep.T.reshape(1, 64, 1, 8, 32),
        first.reshape(3, 3, 3, 4, 32),
        bias1.reshape(32),
        second.reshape(3, 3, 3, 32, 64),
        bias2.reshape(64),
    )


def solution(mesh):
    split = Mesh(mesh.devices.reshape(-1, 2, 2, *mesh.devices.shape[1:]), DEPTH + ("y", "x_hi"))
    samples = P(("x_hi", "y"), None, DEPTH, None, None)
    in_specs = (P("x_hi", None, DEPTH, "y", None), P(), P(), P(), P(), samples)
    out_specs = (samples, P(), P(), P(), P())
    return jax.shard_map(per_device, mesh=split, in_specs=in_specs, out_specs=out_specs, check_vma=False)
```
